32 devices in a mesh: bank: 2 (over x), tmpl: 16 (over z, y, core).
Axes of the slice: x: 2, y: 2, z: 4, core: 2. Of those that a mesh axis runs over, the one named last changes fastest.
Arguments:
- strain_fast: bfloat16 [9216], replicated, may hold values from -6 to 6
- strain_half: bfloat16 [8704], replicated, may hold values from -6 to 6
- strain_quarter: bfloat16 [8448], replicated, may hold values from -6 to 6
- strain_eighth: bfloat16 [8320], replicated, may hold values from -6 to 6
- basis_taps: bfloat16 [8, 512, 8192], P('bank', 'tmpl'), parts along dimension 0, may hold values from -0.0625 to 0.0625
- recon_coeffs: bfloat16 [8, 4096, 512], P('bank', 'tmpl'), parts along dimension 0, may hold values from -0.25 to 0.25
Outputs:
- snr_series: bfloat16 [8192, 1024], P(('bank', 'tmpl')), parts along dimension 0
- peak_snr: float32 [2048], P('bank'), parts along dimension 0
The draws below stay inside these ranges and needn't reach their ends.
There are 2 independent parts, one for each index of `bank`. The reference program is written for one: setup_inputs(seed, part) draws one part's arguments, and reference() takes and returns one part's arrays. A program takes and returns all parts, laid end to end along the dimension named above; an argument that names none is the same for every part. Nothing has to cross between parts.
All inputs are finite; a program needn't handle non-finite values.
Results may differ from the reference program's by a relative error of at most 0.0049.
Values may be sent and summed in bfloat16 or wider, within the bound.
No kernel may reach another device: no remote copies, remote signals or barrier semaphores. Data moves between devices by JAX's collectives and lax.ppermute only.
A program may use at most 128 MiB of HBM per device.

```python
import jax
import jax.numpy as jnp
from jax import lax

BASES = 512
TAPS = 8192
TEMPLATES = 4096
SAMPLES = 1024


def block_levels(rng, shape, pieces, low, high):
    def one(position, blocks):
        draws = jax.random.uniform(jax.random.fold_in(jax.random.fold_in(rng, 6), position), (blocks,), jnp.float32, low / len(pieces), high / len(pieces))
        return jnp.repeat(jnp.exp(draws), shape[position] // blocks).reshape((-1,) + (1,) * (len(shape) - position - 1))

    factor_of = one(*pieces[0])
    for cut in pieces[1:]:
        factor_of = factor_of * one(*cut)
    return factor_of


def gaussian(key, dims, scale, reach, pieces=(), dtype=jnp.bfloat16):
    gain = block_levels(key, dims, pieces, -0.22, 0.18) if pieces else 1.0
    array = jax.random.normal(key, dims, jnp.float32) * scale * gain
    return jnp.minimum(jnp.maximum(array, -reach), reach).astype(dtype)


def setup_inputs(seed: int = 0, part: int = 0) -> dict:
    seeds = jax.random.split(jax.random.key(seed), 7)
    part_keys = jax.random.split(jax.random.fold_in(seeds[6], part), 7)
    strain_fast = gaussian(seeds[0], (SAMPLES + TAPS,), 1.0, 6.0)
    strain_half = gaussian(seeds[1], (SAMPLES // 2 + TAPS,), 1.0, 6.0)
    strain_quarter = gaussian(seeds[2], (SAMPLES // 4 + TAPS,), 1.0, 6.0)
    strain_eighth = gaussian(seeds[3], (SAMPLES // 8 + TAPS,), 1.0, 6.0)
    basis_taps = gaussian(part_keys[4], (4, BASES, TAPS), TAPS ** -0.5, 0.0625, ((1, 16),))
    recon_coeffs = gaussian(part_keys[5], (4, TEMPLATES, BASES), BASES ** -0.5, 0.25, ((1, 16),))
    return dict(strain_fast=strain_fast, strain_half=strain_half, strain_quarter=strain_quarter, strain_eighth=strain_eighth, basis_taps=basis_taps, recon_coeffs=recon_coeffs)


def correlate(strain, taps):
    signal = strain.astype(jnp.float32)[None, None, :]
    kernel = taps.astype(jnp.float32)[:, None, :]
    filtered = lax.conv_general_dilated(signal, kernel, (1,), "VALID", dimension_numbers=("NCH", "OIH", "NCH"), precision=lax.Precision.HIGHEST)
    sample_count = strain.shape[0] - taps.shape[1]
    return filtered[0, :, :sample_count].astype(jnp.bfloat16)


def reference(strain_fast, strain_half, strain_quarter, strain_eighth, basis_taps, recon_coeffs):
    streams = (strain_fast, strain_half, strain_quarter, strain_eighth)
    running = None
    for section in (3, 2, 1, 0):
        basis_out = correlate(streams[section], basis_taps[section])
        summed = jnp.dot(recon_coeffs[section], basis_out, preferred_element_type=jnp.float32)
        if section == 3:
            running = summed
        else:
            running = summed + jnp.repeat(running, 2, axis=1)
    return running.astype(jnp.bfloat16), jnp.max(jnp.abs(running), axis=0)
```

```python
import functools

import jax
import jax.numpy as jnp
from jax import lax
from jax.experimental import pallas as pl
from jax.experimental.pallas import tpu as pltpu
from jax.sharding import PartitionSpec as P

LANE = 128
CHUNK = 8
SUB = 16


def shifted_rows(x_ref, start, tiles):
    width = (tiles + 1) * LANE
    wide = jnp.broadcast_to(x_ref[:, pl.ds(start, width)], (SUB, width))
    row = lax.broadcasted_iota(jnp.int32, (SUB, width), 0)
    step = 1
    while step < SUB:
        moved = pltpu.roll(wide, width - step, axis=1)
        wide = jnp.where((row & step) != 0, moved, wide)
        step *= 2
    return wide


def build_frames(x_ref, frames_ref, start, tiles):
    wide = shifted_rows(x_ref, start, tiles)
    width = wide.shape[1]
    for q in range(LANE // SUB):
        moved = wide if q == 0 else pltpu.roll(wide, width - SUB * q, axis=1)
        for tile in range(tiles):
            frames_ref[pl.ds(start + tile * LANE + SUB * q, SUB), :] = moved[
                :, tile * LANE : (tile + 1) * LANE
            ]


def correlate_kernel(x0, x1, x2, x3, taps_ref, out_ref, f0, f1, f2, f3):
    streams, frames = (x0, x1, x2, x3), (f0, f1, f2, f3)
    rows, taps = taps_ref.shape[1], taps_ref.shape[2]
    blocks = [(x.shape[1] - taps) // LANE for x in streams]
    offsets = [sum(blocks[:s]) * LANE for s in range(len(blocks))]
    span = CHUNK * LANE
    chunks = taps // span

    def build(section, start, tiles=CHUNK):
        build_frames(streams[section], frames[section], start, tiles)

    def head(section):
        pieces = []
        for u in range(blocks[section]):
            part = taps_ref[section, :, 0 : span - u * LANE]
            if u:
                part = jnp.concatenate([jnp.zeros((rows, u * LANE), part.dtype), part], axis=1)
            pieces.append(part)
        return jnp.concatenate(pieces, axis=0)

    def middle(section, start):
        pieces = []
        for u in range(blocks[section]):
            first = pl.multiple_of(start - u * LANE, LANE)
            pieces.append(taps_ref[section, :, pl.ds(first, span)])
        return jnp.concatenate(pieces, axis=0)

    def tail(section):
        width = (blocks[section] - 1) * LANE
        pieces = []
        for u in range(blocks[section]):
            parts = []
            if u:
                parts.append(taps_ref[section, :, taps - u * LANE : taps])
            if width > u * LANE:
                parts.append(jnp.zeros((rows, width - u * LANE), taps_ref.dtype))
            pieces.append(jnp.concatenate(parts, axis=1))
        return jnp.concatenate(pieces, axis=0)

    def product(section, left, start):
        right = frames[section][pl.ds(start, left.shape[1]), :]
        return jnp.dot(left, right, preferred_element_type=jnp.float32)

    def build_all(section):
        def step(number, carry):
            build(section, pl.multiple_of(number * span, span))
            return carry

        lax.fori_loop(0, chunks, step, 0)
        if blocks[section] > 1:
            build(section, taps, blocks[section] - 1)

    build_all(0)
    for section in range(len(blocks)):
        following = section + 1 if section + 1 < len(blocks) else None
        total = product(section, head(section), 0)
        if following is not None:
            build(following, 0)

        def step(number, total, section=section, following=following):
            start = pl.multiple_of(number * span, span)
            total = total + product(section, middle(section, start), start)
            if following is not None:
                build(following, start)
            return total

        total = lax.fori_loop(1, chunks, step, total)
        if blocks[section] > 1:
            total = total + product(section, tail(section), taps)
        if following is not None and blocks[following] > 1:
            build(following, taps, blocks[following] - 1)
        for u in range(blocks[section]):
            place = offsets[section] + u * LANE
            out_ref[:, place : place + LANE] = total[u * rows : (u + 1) * rows].astype(out_ref.dtype)


def correlate(streams, basis_taps):
    sections, rows, taps = basis_taps.shape
    padded = -(-rows // SUB) * SUB
    if padded != rows:
        basis_taps = jnp.pad(basis_taps, ((0, 0), (0, padded - rows), (0, 0)))
    samples = [x.shape[0] - taps for x in streams]
    out = pl.pallas_call(
        correlate_kernel,
        out_shape=jax.ShapeDtypeStruct((padded, sum(samples)), jnp.bfloat16),
        in_specs=[pl.BlockSpec(memory_space=pltpu.VMEM)] * 5,
        out_specs=pl.BlockSpec(memory_space=pltpu.VMEM),
        scratch_shapes=[
            pltpu.VMEM((taps + count - LANE, LANE), jnp.bfloat16) for count in samples
        ],
        compiler_params=pltpu.CompilerParams(vmem_limit_bytes=24 * 2**20),
        name="correlate",
    )(*[x.reshape(1, -1) for x in streams], basis_taps)
    return out[:rows]


def recon_kernel(coeffs_ref, basis_ref, snr_ref, peak_ref):
    samples = snr_ref.shape[1]
    source = lax.broadcasted_iota(jnp.int32, (2 * LANE, 2 * LANE), 0) % LANE
    target = lax.broadcasted_iota(jnp.int32, (2 * LANE, 2 * LANE), 1) // 2
    repeat = jnp.where(source == target, 1.0, 0.0).astype(jnp.bfloat16)
    running = None
    for section in (3, 2, 1, 0):
        width = samples >> section
        offset = sum(samples >> s for s in range(section))
        summed = []
        for place in range(0, width, 2 * LANE):
            size = min(2 * LANE, width)
            part = jnp.dot(
                coeffs_ref[section],
                basis_ref[:, offset + place : offset + place + size],
                preferred_element_type=jnp.float32,
            )
            if running is not None:
                coarse = running[place // (2 * LANE)]
                high = coarse.astype(jnp.bfloat16)
                low = (coarse - high.astype(jnp.float32)).astype(jnp.bfloat16)
                part = part + jnp.dot(
                    jnp.concatenate([high, low], axis=1),
                    repeat,
                    preferred_element_type=jnp.float32,
                )
            summed.append(part)
        running = []
        for part in summed:
            running += [part[:, at : at + LANE] for at in range(0, part.shape[1], LANE)]
        if section == 0:
            for number, part in enumerate(summed):
                place = number * 2 * LANE
                snr_ref[:, place : place + 2 * LANE] = part.astype(snr_ref.dtype)
                peak_ref[:, place : place + 2 * LANE] = jnp.max(
                    jnp.abs(part), axis=0, keepdims=True
                )


def reconstruct(coeffs, basis, samples):
    return pl.pallas_call(
        recon_kernel,
        out_shape=(
            jax.ShapeDtypeStruct((coeffs.shape[1], samples), jnp.bfloat16),
            jax.ShapeDtypeStruct((1, samples), jnp.float32),
        ),
        in_specs=[pl.BlockSpec(memory_space=pltpu.VMEM)] * 2,
        out_specs=(pl.BlockSpec(memory_space=pltpu.VMEM),) * 2,
        compiler_params=pltpu.CompilerParams(vmem_limit_bytes=24 * 2**20),
        name="reconstruct",
    )(coeffs, basis)


def per_device(strain_fast, strain_half, strain_quarter, strain_eighth, basis_taps, recon_coeffs):
    streams = (strain_fast, strain_half, strain_quarter, strain_eighth)
    samples = strain_fast.shape[0] - basis_taps.shape[2]
    own = correlate(streams, basis_taps)
    basis = lax.all_gather(own, "tmpl", axis=0, tiled=True)
    snr_series, local_peak = reconstruct(recon_coeffs, basis, samples)
    peak_snr = lax.pmax(local_peak.reshape(samples), "tmpl")
    return (snr_series, peak_snr)


def solution(mesh):
    in_specs = (P(), P(), P(), P(), P("bank", "tmpl", None), P("bank", "tmpl", None))
    out_specs = (P(("bank", "tmpl"), None), P("bank"))
    return jax.shard_map(
        per_device, mesh=mesh, in_specs=in_specs, out_specs=out_specs, check_vma=False
    )
```

```python
import functools

import jax
import jax.numpy as jnp
from jax import lax
from jax.experimental import pallas as pl
from jax.experimental.pallas import tpu as pltpu
from jax.sharding import PartitionSpec as P

LANE = 128
CHUNK = 8
SUB = 16


def shifted_rows(x_ref, start, tiles):
    width = (tiles + 1) * LANE
    wide = jnp.broadcast_to(x_ref[pl.ds(start, width)].reshape(1, width), (SUB, width))
    row = lax.broadcasted_iota(jnp.int32, (SUB, width), 0)
    step = 1
    while step < SUB:
        moved = pltpu.roll(wide, width - step, axis=1)
        wide = jnp.where((row & step) != 0, moved, wide)
        step *= 2
    return wide


def build_frames(x_ref, start, tiles):
    wide = shifted_rows(x_ref, start, tiles)
    width = wide.shape[1]
    moved = [wide]
    for q in range(1, LANE // SUB):
        moved.append(pltpu.roll(wide, width - SUB * q, axis=1))
    pieces = []
    for tile in range(tiles):
        pieces += [part[:, tile * LANE : (tile + 1) * LANE] for part in moved]
    return jnp.concatenate(pieces, axis=0)


def shifted_taps(taps_ref, start, width, u):
    rows, taps = taps_ref.shape
    first, last = start - u * LANE, start - u * LANE + width
    parts = []
    if first < 0:
        parts.append(jnp.zeros((rows, -first), taps_ref.dtype))
    if last > 0 and first < taps:
        parts.append(taps_ref[:, max(first, 0) : min(last, taps)])
    if last > taps:
        parts.append(jnp.zeros((rows, last - taps), taps_ref.dtype))
    return parts[0] if len(parts) == 1 else jnp.concatenate(parts, axis=1)


def correlate_kernel(sections, *refs):
    count = len(sections)
    streams, taps_ref, out_ref = refs[:count], refs[count], refs[count + 1]
    held_ref, sems = refs[count + 2], refs[count + 3]
    rows, taps = taps_ref.shape[1], taps_ref.shape[2]
    copies = [
        pltpu.make_async_copy(taps_ref.at[section], held_ref.at[number], sems.at[number])
        for number, section in enumerate(sections)
    ]
    for copy in copies:
        copy.start()
    place = 0
    for number in range(count):
        blocks = (streams[number].shape[0] - taps) // LANE
        tiles = taps // LANE + blocks - 1
        total = None
        for tile in range(0, tiles, CHUNK):
            size = min(CHUNK, tiles - tile)
            frames = build_frames(streams[number], tile * LANE, size)
            if tile == 0:
                copies[number].wait()
            held = held_ref.at[number]
            left = jnp.concatenate(
                [shifted_taps(held, tile * LANE, size * LANE, u) for u in range(blocks)], axis=0
            )
            part = jnp.dot(left, frames, preferred_element_type=jnp.float32)
            total = part if total is None else total + part
        for u in range(blocks):
            out_ref[:, place : place + LANE] = total[u * rows : (u + 1) * rows].astype(out_ref.dtype)
            place += LANE


def correlate(streams, basis_taps, sections):
    _, rows, taps = basis_taps.shape
    padded = -(-rows // SUB) * SUB
    if padded != rows:
        basis_taps = jnp.pad(basis_taps, ((0, 0), (0, padded - rows), (0, 0)))
    used = [streams[section] for section in sections]
    samples = sum(x.shape[0] - taps for x in used)
    out = pl.pallas_call(
        functools.partial(correlate_kernel, sections),
        out_shape=jax.ShapeDtypeStruct((padded, samples), jnp.bfloat16),
        in_specs=[pl.BlockSpec(memory_space=pltpu.VMEM)] * len(used)
        + [pl.BlockSpec(memory_space=pl.ANY)],
        out_specs=pl.BlockSpec(memory_space=pltpu.VMEM),
        scratch_shapes=[
            pltpu.VMEM((len(used), padded, taps), jnp.bfloat16),
            pltpu.SemaphoreType.DMA((len(used),)),
        ],
        compiler_params=pltpu.CompilerParams(vmem_limit_bytes=16 * 2**20),
        cost_estimate=pl.CostEstimate(
            flops=2 * padded * taps * samples,
            bytes_accessed=2 * len(used) * padded * taps,
            transcendentals=0,
        ),
        name="correlate",
    )(*used, basis_taps)
    return out[:rows]


def exchange(block, distance):
    size = lax.axis_size("tmpl")
    return lax.ppermute(block, "tmpl", [(i, i ^ distance) for i in range(size)])


def gather_blocks(block):
    size = lax.axis_size("tmpl")
    merge = block.shape[0] % SUB != 0
    held = {0: block}
    top = size
    while top > 1:
        radix = 4 if top > 4 and top % 4 == 0 else 2
        stride = top // radix
        for place, own in list(held.items()):
            for step in range(1, radix):
                held[place + step * stride] = exchange(own, step * stride)
        top = stride
    blocks = [held[place] for place in range(size)]
    return [jnp.concatenate(blocks, axis=0)] if merge else blocks


def maximum_over_group(values):
    size = lax.axis_size("tmpl")
    stride = 1
    while stride < size:
        radix = 4 if size // stride >= 4 else 2
        others = [exchange(values, step * stride) for step in range(1, radix)]
        values = functools.reduce(jnp.maximum, others, values)
        stride *= radix
    return values


def arrange_kernel(offset_ref, coeffs_ref, out_ref):
    bases = coeffs_ref.shape[2]
    source = lax.broadcasted_iota(jnp.int32, (bases, bases), 0)
    target = lax.broadcasted_iota(jnp.int32, (bases, bases), 1) ^ offset_ref[0]
    select = jnp.where(source == target, 1.0, 0.0).astype(jnp.bfloat16)
    for section in range(coeffs_ref.shape[0]):
        out_ref[section] = jnp.dot(
            coeffs_ref[section], select, preferred_element_type=jnp.float32
        ).astype(out_ref.dtype)


def arrange(coeffs, offset):
    return pl.pallas_call(
        arrange_kernel,
        out_shape=jax.ShapeDtypeStruct(coeffs.shape, coeffs.dtype),
        in_specs=[
            pl.BlockSpec(memory_space=pltpu.SMEM),
            pl.BlockSpec(memory_space=pltpu.VMEM),
        ],
        out_specs=pl.BlockSpec(memory_space=pltpu.VMEM),
        compiler_params=pltpu.CompilerParams(vmem_limit_bytes=16 * 2**20),
        cost_estimate=pl.CostEstimate(
            flops=2 * coeffs.size * coeffs.shape[2],
            bytes_accessed=4 * coeffs.size,
            transcendentals=0,
        ),
        name="arrange",
    )(offset, coeffs)


def recon_kernel(fast_count, *refs):
    coeffs_ref, snr_ref, peak_ref = refs[0], refs[-2], refs[-1]
    fast_refs, slow_refs = refs[1 : 1 + fast_count], refs[1 + fast_count : -2]
    samples = snr_ref.shape[1]
    source = lax.broadcasted_iota(jnp.int32, (2 * LANE, 2 * LANE), 0) % LANE
    target = lax.broadcasted_iota(jnp.int32, (2 * LANE, 2 * LANE), 1) // 2
    repeat = jnp.where(source == target, 1.0, 0.0).astype(jnp.bfloat16)
    running = None
    for section in (3, 2, 1, 0):
        width = samples >> section
        offset = sum(samples >> s for s in range(1, section))
        pieces = slow_refs if section else fast_refs
        summed = []
        for place in range(0, width, 2 * LANE):
            size = min(2 * LANE, width)
            first = offset + place
            basis = jnp.concatenate([ref[:, first : first + size] for ref in pieces], axis=0)
            part = jnp.dot(coeffs_ref[section], basis, preferred_element_type=jnp.float32)
            if running is not None:
                coarse = running[place // (2 * LANE)]
                high = coarse.astype(jnp.bfloat16)
                low = (coarse - high.astype(jnp.float32)).astype(jnp.bfloat16)
                part = part + jnp.dot(
                    jnp.concatenate([high, low], axis=1),
                    repeat,
                    preferred_element_type=jnp.float32,
                )
            summed.append(part)
        running = []
        for part in summed:
            running += [part[:, at : at + LANE] for at in range(0, part.shape[1], LANE)]
        if section == 0:
            for number, part in enumerate(summed):
                place = number * 2 * LANE
                snr_ref[:, place : place + 2 * LANE] = part.astype(snr_ref.dtype)
                peak_ref[:, place : place + 2 * LANE] = jnp.max(
                    jnp.abs(part), axis=0, keepdims=True
                )


def reconstruct(coeffs, fast, slow, samples):
    return pl.pallas_call(
        functools.partial(recon_kernel, len(fast)),
        out_shape=(
            jax.ShapeDtypeStruct((coeffs.shape[1], samples), jnp.bfloat16),
            jax.ShapeDtypeStruct((1, samples), jnp.float32),
        ),
        in_specs=[pl.BlockSpec(memory_space=pltpu.VMEM)] * (1 + len(fast) + len(slow)),
        out_specs=(pl.BlockSpec(memory_space=pltpu.VMEM),) * 2,
        compiler_params=pltpu.CompilerParams(vmem_limit_bytes=16 * 2**20),
        name="reconstruct",
    )(coeffs, *fast, *slow)


def per_device(strain_fast, strain_half, strain_quarter, strain_eighth, basis_taps, recon_coeffs):
    streams = (strain_fast, strain_half, strain_quarter, strain_eighth)
    samples = strain_fast.shape[0] - basis_taps.shape[2]
    offset = (lax.axis_index("tmpl") * basis_taps.shape[1]).astype(jnp.int32).reshape(1)
    fast = gather_blocks(correlate(streams, basis_taps, (0,)))
    slow = gather_blocks(correlate(streams, basis_taps, (1, 2, 3)))
    coeffs = arrange(recon_coeffs, offset)
    snr_series, local_peak = reconstruct(coeffs, fast, slow, samples)
    peak_snr = maximum_over_group(local_peak.reshape(samples))
    return (snr_series, peak_snr)


def solution(mesh):
    in_specs = (P(), P(), P(), P(), P("bank", "tmpl", None), P("bank", "tmpl", None))
    out_specs = (P(("bank", "tmpl"), None), P("bank"))
    return jax.shard_map(
        per_device, mesh=mesh, in_specs=in_specs, out_specs=out_specs, check_vma=False
    )
```

```python
import functools

import jax
import jax.numpy as jnp
from jax import lax
from jax.experimental import pallas as pl
from jax.experimental.pallas import tpu as pltpu
from jax.sharding import PartitionSpec as P

LANE = 128
CHUNK = 8
SUB = 16


def shifted_rows(x_ref, start, tiles):
    width = (tiles + 1) * LANE
    wide = jnp.broadcast_to(x_ref[pl.ds(start, width)].reshape(1, width), (SUB, width))
    row = lax.broadcasted_iota(jnp.int32, (SUB, width), 0)
    step = 1
    while step < SUB:
        moved = pltpu.roll(wide, width - step, axis=1)
        wide = jnp.where((row & step) != 0, moved, wide)
        step *= 2
    return wide


def build_frames(x_ref, start, tiles):
    wide = shifted_rows(x_ref, start, tiles)
    width = wide.shape[1]
    moved = [wide]
    for q in range(1, LANE // SUB):
        moved.append(pltpu.roll(wide, width - SUB * q, axis=1))
    pieces = []
    for tile in range(tiles):
        pieces += [part[:, tile * LANE : (tile + 1) * LANE] for part in moved]
    return jnp.concatenate(pieces, axis=0)


def shifted_taps(taps_ref, start, width, u):
    rows, taps = taps_ref.shape
    first, last = start - u * LANE, start - u * LANE + width
    parts = []
    if first < 0:
        parts.append(jnp.zeros((rows, -first), taps_ref.dtype))
    if last > 0 and first < taps:
        parts.append(taps_ref[:, max(first, 0) : min(last, taps)])
    if last > taps:
        parts.append(jnp.zeros((rows, last - taps), taps_ref.dtype))
    return parts[0] if len(parts) == 1 else jnp.concatenate(parts, axis=1)


def correlate_kernel(*refs):
    strain_refs, taps_ref, out_ref = refs[:4], refs[4], refs[5]
    held_strains, held_taps, strain_sems, taps_sems = refs[6:10], refs[10], refs[11], refs[12]
    rows, taps = taps_ref.shape[1], taps_ref.shape[2]
    strain_copies, taps_copies = [], []
    for section, source in enumerate(strain_refs):
        copy = pltpu.make_async_copy(source, held_strains[section], strain_sems.at[section])
        copy.start()
        strain_copies.append(copy)
    for section in range(len(strain_refs)):
        copy = pltpu.make_async_copy(
            taps_ref.at[section], held_taps.at[section], taps_sems.at[section]
        )
        copy.start()
        taps_copies.append(copy)
    place = 0
    for section, strain in enumerate(held_strains):
        strain_copies[section].wait()
        blocks = (strain.shape[0] - taps) // LANE
        tiles = taps // LANE + blocks - 1
        held = held_taps.at[section]
        total = None
        for tile in range(0, tiles, CHUNK):
            size = min(CHUNK, tiles - tile)
            frames = build_frames(strain, tile * LANE, size)
            if tile == 0:
                taps_copies[section].wait()
            left = jnp.concatenate(
                [shifted_taps(held, tile * LANE, size * LANE, u) for u in range(blocks)], axis=0
            )
            part = jnp.dot(left, frames, preferred_element_type=jnp.float32)
            total = part if total is None else total + part
        for u in range(blocks):
            out_ref[:, place : place + LANE] = total[u * rows : (u + 1) * rows].astype(out_ref.dtype)
            place += LANE


def correlate(streams, basis_taps):
    sections, rows, taps = basis_taps.shape
    padded = -(-rows // SUB) * SUB
    if padded != rows:
        basis_taps = jnp.pad(basis_taps, ((0, 0), (0, padded - rows), (0, 0)))
    samples = sum(x.shape[0] - taps for x in streams)
    out = pl.pallas_call(
        correlate_kernel,
        out_shape=jax.ShapeDtypeStruct((padded, samples), jnp.bfloat16),
        in_specs=[pl.BlockSpec(memory_space=pltpu.HBM)] * (sections + 1),
        out_specs=pl.BlockSpec(memory_space=pltpu.VMEM),
        scratch_shapes=[pltpu.VMEM(x.shape, x.dtype) for x in streams]
        + [
            pltpu.VMEM((sections, padded, taps), jnp.bfloat16),
            pltpu.SemaphoreType.DMA((sections,)),
            pltpu.SemaphoreType.DMA((sections,)),
        ],
        compiler_params=pltpu.CompilerParams(vmem_limit_bytes=60 * 2**20),
        cost_estimate=pl.CostEstimate(
            flops=2 * padded * taps * samples,
            bytes_accessed=2 * sections * padded * taps,
            transcendentals=0,
        ),
        name="correlate",
    )(*streams, basis_taps)
    return out[:rows]


def exchange(block, distance):
    size = lax.axis_size("tmpl")
    return lax.ppermute(block, "tmpl", [(i, i ^ distance) for i in range(size)])


def gather_blocks(block):
    size = lax.axis_size("tmpl")
    if block.shape[0] % SUB:
        stride = 1
        while stride < size:
            radix = 4 if size // stride >= 4 else 2
            others = [exchange(block, step * stride) for step in range(1, radix)]
            block = jnp.concatenate([block] + others, axis=0)
            stride *= radix
        return [block]
    held = {0: block}
    top = size
    while top > 1:
        radix = 4 if top > 4 and top % 4 == 0 else 2
        stride = top // radix
        for place, own in list(held.items()):
            for step in range(1, radix):
                held[place + step * stride] = exchange(own, step * stride)
        top = stride
    return [held[place] for place in range(size)]


def maximum_over_group(values):
    size = lax.axis_size("tmpl")
    stride = 1
    while stride < size:
        values = jnp.maximum(values, exchange(values, stride))
        stride *= 2
    return values


def arrange_kernel(offset_ref, coeffs_ref, out_ref):
    bases = coeffs_ref.shape[2]
    source = lax.broadcasted_iota(jnp.int32, (bases, bases), 0)
    target = lax.broadcasted_iota(jnp.int32, (bases, bases), 1) ^ offset_ref[0]
    select = jnp.where(source == target, 1.0, 0.0).astype(jnp.bfloat16)
    for section in range(coeffs_ref.shape[0]):
        out_ref[section] = jnp.dot(
            coeffs_ref[section], select, preferred_element_type=jnp.float32
        ).astype(out_ref.dtype)


def arrange(coeffs, offset):
    return pl.pallas_call(
        arrange_kernel,
        out_shape=jax.ShapeDtypeStruct(coeffs.shape, coeffs.dtype),
        in_specs=[
            pl.BlockSpec(memory_space=pltpu.SMEM),
            pl.BlockSpec(memory_space=pltpu.VMEM),
        ],
        out_specs=pl.BlockSpec(memory_space=pltpu.VMEM),
        compiler_params=pltpu.CompilerParams(vmem_limit_bytes=16 * 2**20),
        cost_estimate=pl.CostEstimate(
            flops=2 * coeffs.size * coeffs.shape[2],
            bytes_accessed=4 * coeffs.size,
            transcendentals=0,
        ),
        name="arrange",
    )(offset, coeffs)


def recon_kernel(coeffs_ref, *refs):
    pieces, snr_ref, peak_ref = refs[:-2], refs[-2], refs[-1]
    samples = snr_ref.shape[1]
    source = lax.broadcasted_iota(jnp.int32, (2 * LANE, 2 * LANE), 0) % LANE
    target = lax.broadcasted_iota(jnp.int32, (2 * LANE, 2 * LANE), 1) // 2
    repeat = jnp.where(source == target, 1.0, 0.0).astype(jnp.bfloat16)
    running = None
    for section in (3, 2, 1, 0):
        width = samples >> section
        offset = sum(samples >> s for s in range(section))
        summed = []
        for place in range(0, width, 2 * LANE):
            size = min(2 * LANE, width)
            first = offset + place
            basis = jnp.concatenate([ref[:, first : first + size] for ref in pieces], axis=0)
            part = jnp.dot(coeffs_ref[section], basis, preferred_element_type=jnp.float32)
            if running is not None:
                coarse = running[place // (2 * LANE)]
                high = coarse.astype(jnp.bfloat16)
                low = (coarse - high.astype(jnp.float32)).astype(jnp.bfloat16)
                part = part + jnp.dot(
                    jnp.concatenate([high, low], axis=1),
                    repeat,
                    preferred_element_type=jnp.float32,
                )
            summed.append(part)
        running = []
        for part in summed:
            running += [part[:, at : at + LANE] for at in range(0, part.shape[1], LANE)]
        if section == 0:
            for number, part in enumerate(summed):
                place = number * 2 * LANE
                snr_ref[:, place : place + 2 * LANE] = part.astype(snr_ref.dtype)
                peak_ref[:, place : place + 2 * LANE] = jnp.max(
                    jnp.abs(part), axis=0, keepdims=True
                )


def reconstruct(coeffs, blocks, samples):
    return pl.pallas_call(
        recon_kernel,
        out_shape=(
            jax.ShapeDtypeStruct((coeffs.shape[1], samples), jnp.bfloat16),
            jax.ShapeDtypeStruct((1, samples), jnp.float32),
        ),
        in_specs=[pl.BlockSpec(memory_space=pltpu.VMEM)] * (1 + len(blocks)),
        out_specs=(pl.BlockSpec(memory_space=pltpu.VMEM),) * 2,
        compiler_params=pltpu.CompilerParams(vmem_limit_bytes=16 * 2**20),
        name="reconstruct",
    )(coeffs, *blocks)


def per_device(strain_fast, strain_half, strain_quarter, strain_eighth, basis_taps, recon_coeffs):
    streams = (strain_fast, strain_half, strain_quarter, strain_eighth)
    samples = strain_fast.shape[0] - basis_taps.shape[2]
    offset = (lax.axis_index("tmpl") * basis_taps.shape[1]).astype(jnp.int32).reshape(1)
    blocks = gather_blocks(correlate(streams, basis_taps))
    coeffs = arrange(recon_coeffs, offset)
    snr_series, local_peak = reconstruct(coeffs, blocks, samples)
    peak_snr = maximum_over_group(local_peak.reshape(samples))
    return (snr_series, peak_snr)


def solution(mesh):
    in_specs = (P(), P(), P(), P(), P("bank", "tmpl", None), P("bank", "tmpl", None))
    out_specs = (P(("bank", "tmpl"), None), P("bank"))
    return jax.shard_map(
        per_device, mesh=mesh, in_specs=in_specs, out_specs=out_specs, check_vma=False
    )
```

```python
import functools

import jax
import jax.numpy as jnp
from jax import lax
from jax.experimental import pallas as pl
from jax.experimental.pallas import tpu as pltpu
from jax.sharding import PartitionSpec as P

LANE = 128
CHUNK = 8
SUB = 16
ROWS = 8


def shifted_rows(x_ref, start, tiles):
    width = (tiles + 1) * LANE
    line = x_ref[pl.ds(start, width)].reshape(1, width).astype(jnp.float32)
    wide = jnp.broadcast_to(line, (ROWS, width))
    row = lax.broadcasted_iota(jnp.int32, (ROWS, width), 0)
    step = 1
    while step < ROWS:
        moved = pltpu.roll(wide, width - step, axis=1)
        wide = jnp.where((row & step) != 0, moved, wide)
        step *= 2
    return wide


def build_frames(x_ref, start, tiles):
    wide = shifted_rows(x_ref, start, tiles)
    width = wide.shape[1]
    moved = [wide]
    for q in range(1, LANE // ROWS):
        moved.append(pltpu.roll(wide, width - ROWS * q, axis=1))
    pairs = [
        jnp.concatenate(moved[q : q + 2], axis=0).astype(jnp.bfloat16)
        for q in range(0, len(moved), 2)
    ]
    pieces = []
    for tile in range(tiles):
        pieces += [part[:, tile * LANE : (tile + 1) * LANE] for part in pairs]
    return jnp.concatenate(pieces, axis=0)


def shifted_taps(taps_ref, start, width, u):
    rows, taps = taps_ref.shape
    first, last = start - u * LANE, start - u * LANE + width
    parts = []
    if first < 0:
        parts.append(jnp.zeros((rows, -first), taps_ref.dtype))
    if last > 0 and first < taps:
        parts.append(taps_ref[:, max(first, 0) : min(last, taps)])
    if last > taps:
        parts.append(jnp.zeros((rows, last - taps), taps_ref.dtype))
    return parts[0] if len(parts) == 1 else jnp.concatenate(parts, axis=1)


def correlate_kernel(*refs):
    strain_refs, taps_ref, out_ref = refs[:4], refs[4], refs[5]
    held_strains, held_taps, strain_sems, taps_sems = refs[6:10], refs[10], refs[11], refs[12]
    rows, taps = taps_ref.shape[1], taps_ref.shape[2]
    strain_copies, taps_copies = [], []
    for section, source in enumerate(strain_refs):
        copy = pltpu.make_async_copy(source, held_strains[section], strain_sems.at[section])
        copy.start()
        strain_copies.append(copy)
    for section in range(len(strain_refs)):
        copy = pltpu.make_async_copy(
            taps_ref.at[section], held_taps.at[section], taps_sems.at[section]
        )
        copy.start()
        taps_copies.append(copy)
    place = 0
    for section, strain in enumerate(held_strains):
        strain_copies[section].wait()
        blocks = (strain.shape[0] - taps) // LANE
        tiles = taps // LANE + blocks - 1
        held = held_taps.at[section]
        total = None
        for tile in range(0, tiles, CHUNK):
            size = min(CHUNK, tiles - tile)
            frames = build_frames(strain, tile * LANE, size)
            if tile == 0:
                taps_copies[section].wait()
            left = jnp.concatenate(
                [shifted_taps(held, tile * LANE, size * LANE, u) for u in range(blocks)], axis=0
            )
            part = jnp.dot(left, frames, preferred_element_type=jnp.float32)
            total = part if total is None else total + part
        for u in range(blocks):
            out_ref[:, place : place + LANE] = total[u * rows : (u + 1) * rows].astype(out_ref.dtype)
            place += LANE


def correlate(streams, basis_taps):
    sections, rows, taps = basis_taps.shape
    padded = -(-rows // SUB) * SUB
    if padded != rows:
        basis_taps = jnp.pad(basis_taps, ((0, 0), (0, padded - rows), (0, 0)))
    samples = sum(x.shape[0] - taps for x in streams)
    out = pl.pallas_call(
        correlate_kernel,
        out_shape=jax.ShapeDtypeStruct((padded, samples), jnp.bfloat16),
        in_specs=[pl.BlockSpec(memory_space=pltpu.HBM)] * (sections + 1),
        out_specs=pl.BlockSpec(memory_space=pltpu.VMEM),
        scratch_shapes=[pltpu.VMEM(x.shape, x.dtype) for x in streams]
        + [
            pltpu.VMEM((sections, padded, taps), jnp.bfloat16),
            pltpu.SemaphoreType.DMA((sections,)),
            pltpu.SemaphoreType.DMA((sections,)),
        ],
        compiler_params=pltpu.CompilerParams(vmem_limit_bytes=60 * 2**20),
        cost_estimate=pl.CostEstimate(
            flops=2 * padded * taps * samples,
            bytes_accessed=2 * sections * padded * taps,
            transcendentals=0,
        ),
        name="correlate",
    )(*streams, basis_taps)
    return out[:rows]


def exchange(block, distance):
    size = lax.axis_size("tmpl")
    return lax.ppermute(block, "tmpl", [(i, i ^ distance) for i in range(size)])


def gather_blocks(block):
    size = lax.axis_size("tmpl")
    if block.shape[0] % SUB:
        stride = 1
        while stride < size:
            radix = 4 if size // stride >= 4 else 2
            others = [exchange(block, step * stride) for step in range(1, radix)]
            block = jnp.concatenate([block] + others, axis=0)
            stride *= radix
        return [block]
    held = {0: block}
    top = size
    while top > 1:
        radix = 4 if top > 4 and top % 4 == 0 else 2
        stride = top // radix
        for place in reversed(list(held)):
            for step in reversed(range(1, radix)):
                held[place + step * stride] = exchange(held[place], step * stride)
        top = stride
    return [held[place] for place in range(size)]


def maximum_over_group(values):
    size = lax.axis_size("tmpl")
    tiles = values.reshape(1, -1, LANE)
    copies = jnp.broadcast_to(tiles, (size,) + tiles.shape[1:])
    others = lax.all_to_all(copies, "tmpl", split_axis=0, concat_axis=0, tiled=True)
    return jnp.max(others, axis=0).reshape(values.shape)


def arrange_kernel(offset_ref, coeffs_ref, out_ref):
    bases = coeffs_ref.shape[2]
    source = lax.broadcasted_iota(jnp.int32, (bases, bases), 0)
    target = lax.broadcasted_iota(jnp.int32, (bases, bases), 1) ^ offset_ref[0]
    select = jnp.where(source == target, 1.0, 0.0).astype(jnp.bfloat16)
    for section in range(coeffs_ref.shape[0]):
        out_ref[section] = jnp.dot(
            coeffs_ref[section], select, preferred_element_type=jnp.float32
        ).astype(out_ref.dtype)


def arrange(coeffs, offset):
    return pl.pallas_call(
        arrange_kernel,
        out_shape=jax.ShapeDtypeStruct(coeffs.shape, coeffs.dtype),
        in_specs=[
            pl.BlockSpec(memory_space=pltpu.SMEM),
            pl.BlockSpec(memory_space=pltpu.VMEM),
        ],
        out_specs=pl.BlockSpec(memory_space=pltpu.VMEM),
        compiler_params=pltpu.CompilerParams(vmem_limit_bytes=16 * 2**20),
        cost_estimate=pl.CostEstimate(
            flops=2 * coeffs.size * coeffs.shape[2],
            bytes_accessed=4 * coeffs.size,
            transcendentals=0,
        ),
        name="arrange",
    )(offset, coeffs)


def recon_kernel(coeffs_ref, *refs):
    pieces, snr_ref, peak_ref = refs[:-2], refs[-2], refs[-1]
    samples = snr_ref.shape[1]
    source = lax.broadcasted_iota(jnp.int32, (2 * LANE, 2 * LANE), 0) % LANE
    target = lax.broadcasted_iota(jnp.int32, (2 * LANE, 2 * LANE), 1) // 2
    repeat = jnp.where(source == target, 1.0, 0.0).astype(jnp.bfloat16)
    running = None
    for section in (3, 2, 1, 0):
        width = samples >> section
        offset = sum(samples >> s for s in range(section))
        summed = []
        for place in range(0, width, 2 * LANE):
            size = min(2 * LANE, width)
            first = offset + place
            basis = jnp.concatenate([ref[:, first : first + size] for ref in pieces], axis=0)
            part = jnp.dot(coeffs_ref[section], basis, preferred_element_type=jnp.float32)
            if running is not None:
                coarse = running[place // (2 * LANE)]
                high = coarse.astype(jnp.bfloat16)
                low = (coarse - high.astype(jnp.float32)).astype(jnp.bfloat16)
                part = part + jnp.dot(
                    jnp.concatenate([high, low], axis=1),
                    repeat,
                    preferred_element_type=jnp.float32,
                )
            summed.append(part)
        running = []
        for part in summed:
            running += [part[:, at : at + LANE] for at in range(0, part.shape[1], LANE)]
        if section == 0:
            for number, part in enumerate(summed):
                place = number * 2 * LANE
                snr_ref[:, place : place + 2 * LANE] = part.astype(snr_ref.dtype)
                peak_ref[:, place : place + 2 * LANE] = jnp.max(
                    jnp.abs(part), axis=0, keepdims=True
                )


def reconstruct(coeffs, blocks, samples):
    return pl.pallas_call(
        recon_kernel,
        out_shape=(
            jax.ShapeDtypeStruct((coeffs.shape[1], samples), jnp.bfloat16),
            jax.ShapeDtypeStruct((1, samples), jnp.float32),
        ),
        in_specs=[pl.BlockSpec(memory_space=pltpu.VMEM)] * (1 + len(blocks)),
        out_specs=(pl.BlockSpec(memory_space=pltpu.VMEM),) * 2,
        compiler_params=pltpu.CompilerParams(vmem_limit_bytes=16 * 2**20),
        name="reconstruct",
    )(coeffs, *blocks)


def per_device(strain_fast, strain_half, strain_quarter, strain_eighth, basis_taps, recon_coeffs):
    streams = (strain_fast, strain_half, strain_quarter, strain_eighth)
    samples = strain_fast.shape[0] - basis_taps.shape[2]
    offset = (lax.axis_index("tmpl") * basis_taps.shape[1]).astype(jnp.int32).reshape(1)
    blocks = gather_blocks(correlate(streams, basis_taps))
    coeffs = arrange(recon_coeffs, offset)
    snr_series, local_peak = reconstruct(coeffs, blocks, samples)
    peak_snr = maximum_over_group(local_peak.reshape(samples))
    return (snr_series, peak_snr)


def solution(mesh):
    in_specs = (P(), P(), P(), P(), P("bank", "tmpl", None), P("bank", "tmpl", None))
    out_specs = (P(("bank", "tmpl"), None), P("bank"))
    return jax.shard_map(
        per_device, mesh=mesh, in_specs=in_specs, out_specs=out_specs, check_vma=False
    )
```

```python
import functools

import jax
import jax.numpy as jnp
from jax import lax
from jax.experimental import pallas as pl
from jax.experimental.pallas import tpu as pltpu
from jax.sharding import PartitionSpec as P

LANE = 128
CHUNK = 8
SUB = 16


def build_frames(x_ref, start, tiles, cols):
    width = tiles * LANE + cols
    wide = jnp.broadcast_to(x_ref[pl.ds(start, width)].reshape(1, width), (SUB, width))
    row = lax.broadcasted_iota(jnp.int32, (SUB, width), 0)
    step = 1
    while step < SUB:
        moved = pltpu.roll(wide, width - step, axis=1)
        wide = jnp.where((row & step) != 0, moved, wide)
        step *= 2
    moved = [wide]
    for q in range(1, LANE // SUB):
        moved.append(pltpu.roll(wide, width - SUB * q, axis=1))
    pieces = []
    for tile in range(tiles):
        pieces += [part[:, tile * LANE : tile * LANE + cols] for part in moved]
    return jnp.concatenate(pieces, axis=0)


def correlate_kernel(*refs):
    strain_refs, taps_ref, out_ref = refs[:4], refs[4], refs[5]
    held_strains, held_taps, strain_sems, taps_sems = refs[6:10], refs[10], refs[11], refs[12]
    sections = len(strain_refs)
    rows, taps = taps_ref.shape[1], taps_ref.shape[2]
    pad = (held_taps.shape[2] - taps) // 2
    copies = []
    for section, source in enumerate(strain_refs):
        copies.append(
            pltpu.make_async_copy(source, held_strains[section], strain_sems.at[section])
        )
        copies.append(
            pltpu.make_async_copy(
                taps_ref.at[section],
                held_taps.at[section, :, pl.ds(pad, taps)],
                taps_sems.at[section],
            )
        )
    for copy in copies:
        copy.start()
    samples = [ref.shape[0] - taps for ref in held_strains]
    cols = [min(2 * LANE, count) for count in samples]
    blocks = [count // size for count, size in zip(samples, cols)]
    for section in range(sections):
        if blocks[section] > 1:
            zeros = jnp.zeros((rows, pad), held_taps.dtype)
            held_taps[section, :, :pad] = zeros
            held_taps[section, :, pad + taps :] = zeros
    for copy in copies:
        copy.wait()

    def term(section, start, tiles):
        frames = build_frames(held_strains[section], start, tiles, cols[section])
        left = []
        for u in range(blocks[section]):
            first = pad + start - u * cols[section]
            if not isinstance(first, int):
                first = pl.multiple_of(first, LANE)
            left.append(held_taps[section, :, pl.ds(first, tiles * LANE)])
        left = left[0] if len(left) == 1 else jnp.concatenate(left, axis=0)
        return jnp.dot(left, frames, preferred_element_type=jnp.float32)

    def step(number, totals):
        start = pl.multiple_of(number * (CHUNK * LANE), CHUNK * LANE)
        return tuple(
            total + term(section, start, CHUNK) for section, total in enumerate(totals)
        )

    totals = lax.fori_loop(
        0,
        taps // (CHUNK * LANE),
        step,
        tuple(
            jnp.zeros((blocks[section] * rows, cols[section]), jnp.float32)
            for section in range(sections)
        ),
    )
    place = 0
    for section, total in enumerate(totals):
        extra = (blocks[section] - 1) * cols[section] // LANE
        for tile in range(0, extra, CHUNK):
            total = total + term(section, taps + tile * LANE, min(CHUNK, extra - tile))
        for u in range(blocks[section]):
            part = total[u * rows : (u + 1) * rows].astype(out_ref.dtype)
            out_ref[:, place : place + cols[section]] = part
            place += cols[section]


def correlate(streams, basis_taps):
    sections, rows, taps = basis_taps.shape
    padded = -(-rows // SUB) * SUB
    if padded != rows:
        basis_taps = jnp.pad(basis_taps, ((0, 0), (0, padded - rows), (0, 0)))
    samples = sum(x.shape[0] - taps for x in streams)
    pad = max(x.shape[0] - taps for x in streams) - 2 * LANE
    out = pl.pallas_call(
        correlate_kernel,
        out_shape=jax.ShapeDtypeStruct((padded, samples), jnp.bfloat16),
        in_specs=[pl.BlockSpec(memory_space=pltpu.HBM)] * (sections + 1),
        out_specs=pl.BlockSpec(memory_space=pltpu.VMEM),
        scratch_shapes=[pltpu.VMEM(x.shape, x.dtype) for x in streams]
        + [
            pltpu.VMEM((sections, padded, taps + 2 * pad), jnp.bfloat16),
            pltpu.SemaphoreType.DMA((sections,)),
            pltpu.SemaphoreType.DMA((sections,)),
        ],
        compiler_params=pltpu.CompilerParams(vmem_limit_bytes=60 * 2**20),
        cost_estimate=pl.CostEstimate(
            flops=2 * padded * taps * samples,
            bytes_accessed=2 * sections * padded * taps,
            transcendentals=0,
        ),
        name="correlate",
    )(*streams, basis_taps)
    return out[:rows]


def exchange(block, distance):
    size = lax.axis_size("tmpl")
    return lax.ppermute(block, "tmpl", [(i, i ^ distance) for i in range(size)])


def gather_blocks(block):
    size = lax.axis_size("tmpl")
    if block.shape[0] % SUB:
        stride = 1
        while stride < size:
            radix = 4 if size // stride >= 4 else 2
            others = [exchange(block, step * stride) for step in range(1, radix)]
            block = jnp.concatenate([block] + others, axis=0)
            stride *= radix
        return [block]
    held = {0: block}
    top = size
    while top > 1:
        radix = 4 if top > 4 and top % 4 == 0 else 2
        stride = top // radix
        for place in reversed(list(held)):
            for step in reversed(range(1, radix)):
                held[place + step * stride] = exchange(held[place], step * stride)
        top = stride
    return [held[place] for place in range(size)]


def maximum_over_group(values):
    size = lax.axis_size("tmpl")
    values = jnp.maximum(values, exchange(values, 1))
    tiles = values.reshape(1, -1, LANE)
    copies = jnp.broadcast_to(tiles, (size // 2,) + tiles.shape[1:])
    groups = [list(range(core, size, 2)) for core in range(2)]
    others = lax.all_to_all(
        copies, "tmpl", split_axis=0, concat_axis=0, axis_index_groups=groups, tiled=True
    )
    return jnp.max(others, axis=0).reshape(values.shape)


def arrange_kernel(offset_ref, coeffs_ref, out_ref):
    bases = coeffs_ref.shape[2]
    source = lax.broadcasted_iota(jnp.int32, (bases, bases), 0)
    target = lax.broadcasted_iota(jnp.int32, (bases, bases), 1) ^ offset_ref[0]
    select = jnp.where(source == target, 1.0, 0.0).astype(jnp.bfloat16)
    for section in range(coeffs_ref.shape[0]):
        out_ref[section] = jnp.dot(
            coeffs_ref[section], select, preferred_element_type=jnp.float32
        ).astype(out_ref.dtype)


def arrange(coeffs, offset):
    return pl.pallas_call(
        arrange_kernel,
        out_shape=jax.ShapeDtypeStruct(coeffs.shape, coeffs.dtype),
        in_specs=[
            pl.BlockSpec(memory_space=pltpu.SMEM),
            pl.BlockSpec(memory_space=pltpu.VMEM),
        ],
        out_specs=pl.BlockSpec(memory_space=pltpu.VMEM),
        compiler_params=pltpu.CompilerParams(vmem_limit_bytes=16 * 2**20),
        cost_estimate=pl.CostEstimate(
            flops=2 * coeffs.size * coeffs.shape[2],
            bytes_accessed=4 * coeffs.size,
            transcendentals=0,
        ),
        name="arrange",
    )(offset, coeffs)


def recon_kernel(coeffs_ref, *refs):
    pieces, snr_ref, peak_ref = refs[-3::-1], refs[-2], refs[-1]
    samples = snr_ref.shape[1]
    source = lax.broadcasted_iota(jnp.int32, (2 * LANE, 2 * LANE), 0) % LANE
    target = lax.broadcasted_iota(jnp.int32, (2 * LANE, 2 * LANE), 1) // 2
    repeat = jnp.where(source == target, 1.0, 0.0).astype(jnp.bfloat16)
    running = None
    for section in (3, 2, 1, 0):
        width = samples >> section
        offset = sum(samples >> s for s in range(section))
        summed = []
        for place in range(0, width, 2 * LANE):
            size = min(2 * LANE, width)
            first = offset + place
            basis = jnp.concatenate([ref[:, first : first + size] for ref in pieces], axis=0)
            part = jnp.dot(coeffs_ref[section], basis, preferred_element_type=jnp.float32)
            if running is not None:
                coarse = running[place // (2 * LANE)]
                high = coarse.astype(jnp.bfloat16)
                low = (coarse - high.astype(jnp.float32)).astype(jnp.bfloat16)
                part = part + jnp.dot(
                    jnp.concatenate([high, low], axis=1),
                    repeat,
                    preferred_element_type=jnp.float32,
                )
            summed.append(part)
        running = []
        for part in summed:
            running += [part[:, at : at + LANE] for at in range(0, part.shape[1], LANE)]
        if section == 0:
            for number, part in enumerate(summed):
                place = number * 2 * LANE
                snr_ref[:, place : place + 2 * LANE] = part.astype(snr_ref.dtype)
                peak_ref[:, place : place + 2 * LANE] = jnp.max(
                    jnp.abs(part), axis=0, keepdims=True
                )


def reconstruct(coeffs, blocks, samples):
    return pl.pallas_call(
        recon_kernel,
        out_shape=(
            jax.ShapeDtypeStruct((coeffs.shape[1], samples), jnp.bfloat16),
            jax.ShapeDtypeStruct((1, samples), jnp.float32),
        ),
        in_specs=[pl.BlockSpec(memory_space=pltpu.VMEM)] * (1 + len(blocks)),
        out_specs=(pl.BlockSpec(memory_space=pltpu.VMEM),) * 2,
        compiler_params=pltpu.CompilerParams(vmem_limit_bytes=16 * 2**20),
        name="reconstruct",
    )(coeffs, *blocks[::-1])


def per_device(strain_fast, strain_half, strain_quarter, strain_eighth, basis_taps, recon_coeffs):
    streams = (strain_fast, strain_half, strain_quarter, strain_eighth)
    samples = strain_fast.shape[0] - basis_taps.shape[2]
    offset = (lax.axis_index("tmpl") * basis_taps.shape[1]).astype(jnp.int32).reshape(1)
    blocks = gather_blocks(correlate(streams, basis_taps))
    coeffs = arrange(recon_coeffs, offset)
    snr_series, local_peak = reconstruct(coeffs, blocks, samples)
    peak_snr = maximum_over_group(local_peak.reshape(samples))
    return (snr_series, peak_snr)


def solution(mesh):
    in_specs = (P(), P(), P(), P(), P("bank", "tmpl", None), P("bank", "tmpl", None))
    out_specs = (P(("bank", "tmpl"), None), P("bank"))
    return jax.shard_map(
        per_device, mesh=mesh, in_specs=in_specs, out_specs=out_specs, check_vma=False
    )
```

```python
import functools

import jax
import jax.numpy as jnp
from jax import lax
from jax.experimental import pallas as pl
from jax.experimental.pallas import tpu as pltpu
from jax.sharding import PartitionSpec as P

LANE = 128
CHUNK = 8
SUB = 16


def correlate_kernel(*refs):
    strain_refs, taps_ref, out_ref = refs[:4], refs[4], refs[5]
    held_strains = refs[6:10]
    held_taps, line_ref, row_ref, wide_ref, strain_sems, taps_sems = refs[10:]
    sections = len(strain_refs)
    rows, taps = taps_ref.shape[1], taps_ref.shape[2]
    lines = [ref.shape[0] for ref in held_strains]
    blocks = [count - taps // LANE for count in lines]
    slot = line_ref.shape[0] // sections
    every = sections * slot
    pad = (max(blocks) - 1) * LANE
    strain_copies, taps_copies = [], []
    for section, source in enumerate(strain_refs):
        strain_copies.append(
            pltpu.make_async_copy(source, held_strains[section], strain_sems.at[section])
        )
        taps_copies.append(
            pltpu.make_async_copy(
                taps_ref.at[section],
                held_taps.at[section, :, pl.ds(pad, taps)],
                taps_sems.at[section],
            )
        )
    for copy in strain_copies + taps_copies:
        copy.start()
    for section in range(sections):
        held_taps[section, :, :pad] = jnp.zeros((rows, pad), held_taps.dtype)
        after = held_taps.shape[2] - pad - taps
        held_taps[section, :, pad + taps :] = jnp.zeros((rows, after), held_taps.dtype)

    for section, copy in enumerate(strain_copies):
        copy.wait()
        first = section * slot
        line_ref[first : first + lines[section], :] = held_strains[section][...].astype(jnp.float32)
        if slot > lines[section]:
            line_ref[first + lines[section] : first + slot, :] = jnp.zeros(
                (slot - lines[section], LANE), jnp.float32
            )
    pairs = jnp.concatenate(
        [
            line_ref[...].astype(jnp.bfloat16),
            jnp.concatenate([line_ref[1:, :], jnp.zeros((1, LANE), jnp.float32)], axis=0).astype(
                jnp.bfloat16
            ),
        ],
        axis=1,
    )
    source = lax.broadcasted_iota(jnp.int32, (2 * LANE, 2 * LANE), 0)
    target = lax.broadcasted_iota(jnp.int32, (2 * LANE, 2 * LANE), 1)
    target = target % LANE + target // LANE
    for r in range(0, SUB, 2):
        select = jnp.where(source == target + r, 1.0, 0.0).astype(jnp.bfloat16)
        moved = jnp.dot(pairs, select, preferred_element_type=jnp.float32)
        row_ref[r * every : (r + 1) * every, :] = moved[:, :LANE]
        row_ref[(r + 1) * every : (r + 2) * every, :] = moved[:, LANE:]

    def place_rows(number, carry):
        for line in range(SUB):
            line = number * SUB + line
            piece = row_ref[pl.ds(line, SUB, stride=every), :].astype(jnp.bfloat16)
            wide_ref[:, pl.ds(pl.multiple_of(line * LANE, LANE), LANE)] = piece
        return carry

    lax.fori_loop(0, every // SUB, place_rows, 0)
    wide_ref[:, every * LANE :] = jnp.zeros((SUB, LANE), wide_ref.dtype)
    for copy in taps_copies:
        copy.wait()

    def frames(section, tile, tiles):
        width = (tiles + 1) * LANE
        first = (section * slot + tile) * LANE
        if not isinstance(first, int):
            first = pl.multiple_of(first, LANE)
        wide = wide_ref[:, pl.ds(first, width)]
        moved = [wide]
        for q in range(1, LANE // SUB):
            moved.append(pltpu.roll(wide, width - SUB * q, axis=1))
        pieces = []
        for number in range(tiles):
            pieces += [part[:, number * LANE : (number + 1) * LANE] for part in moved]
        return jnp.concatenate(pieces, axis=0)

    def shifted(section, tile, tiles):
        pieces = []
        for u in range(blocks[section]):
            first = pad + (tile - u) * LANE
            if not isinstance(first, int):
                first = pl.multiple_of(first, LANE)
            pieces.append(held_taps[section, :, pl.ds(first, tiles * LANE)])
        return pieces

    def term(group, tile, tiles):
        left, right = [], []
        for section in group:
            left += shifted(section, tile, tiles)
            right.append(frames(section, tile, tiles))
        left = jnp.concatenate(left, axis=0) if len(left) > 1 else left[0]
        right = jnp.concatenate(right, axis=1) if len(right) > 1 else right[0]
        both = jnp.dot(left, right, preferred_element_type=jnp.float32)
        parts, row = [], 0
        for number, section in enumerate(group):
            height = blocks[section] * rows
            parts.append(both[row : row + height, number * LANE : (number + 1) * LANE])
            row += height
        return parts

    groups = [list(range(first, min(first + 2, sections))) for first in range(0, sections, 2)]

    def step(number, totals):
        parts = []
        for group in groups:
            parts += term(group, number * CHUNK, CHUNK)
        return tuple(total + part for total, part in zip(totals, parts))

    totals = lax.fori_loop(
        0,
        taps // (CHUNK * LANE),
        step,
        tuple(jnp.zeros((count * rows, LANE), jnp.float32) for count in blocks),
    )
    totals = list(totals)
    for group in groups:
        end = max(blocks[section] for section in group) - 1
        for tile in range(0, end, CHUNK):
            active = [section for section in group if blocks[section] - 1 > tile]
            for section, part in zip(
                active, term(active, taps // LANE + tile, min(CHUNK, end - tile))
            ):
                totals[section] = totals[section] + part
    place = 0
    for section, total in enumerate(totals):
        for u in range(blocks[section]):
            part = total[u * rows : (u + 1) * rows].astype(out_ref.dtype)
            out_ref[:, place : place + LANE] = part
            place += LANE


def correlate(streams, basis_taps):
    sections, rows, taps = basis_taps.shape
    padded = -(-rows // SUB) * SUB
    if padded != rows:
        basis_taps = jnp.pad(basis_taps, ((0, 0), (0, padded - rows), (0, 0)))
    samples = sum(x.shape[0] - taps for x in streams)
    longest = max(x.shape[0] for x in streams)
    slot = -(-longest // (8 * LANE)) * 8
    lines = [x.reshape(-1, LANE) for x in streams]
    out = pl.pallas_call(
        correlate_kernel,
        out_shape=jax.ShapeDtypeStruct((padded, samples), jnp.bfloat16),
        in_specs=[pl.BlockSpec(memory_space=pltpu.HBM)] * (sections + 1),
        out_specs=pl.BlockSpec(memory_space=pltpu.VMEM),
        scratch_shapes=[pltpu.VMEM(x.shape, x.dtype) for x in lines]
        + [
            pltpu.VMEM((sections, padded, 2 * longest - taps), jnp.bfloat16),
            pltpu.VMEM((sections * slot, LANE), jnp.float32),
            pltpu.VMEM((SUB * sections * slot, LANE), jnp.float32),
            pltpu.VMEM((SUB, (sections * slot + 1) * LANE), jnp.bfloat16),
            pltpu.SemaphoreType.DMA((sections,)),
            pltpu.SemaphoreType.DMA((sections,)),
        ],
        compiler_params=pltpu.CompilerParams(vmem_limit_bytes=60 * 2**20),
        cost_estimate=pl.CostEstimate(
            flops=2 * padded * taps * samples,
            bytes_accessed=2 * sections * padded * taps,
            transcendentals=0,
        ),
        name="correlate",
    )(*lines, basis_taps)
    return out[:rows]


def exchange(block, distance):
    size = lax.axis_size("tmpl")
    return lax.ppermute(block, "tmpl", [(i, i ^ distance) for i in range(size)])


def gather_blocks(block):
    size = lax.axis_size("tmpl")
    if block.shape[0] % SUB:
        stride = 1
        while stride < size:
            radix = 4 if size // stride >= 4 else 2
            others = [exchange(block, step * stride) for step in range(1, radix)]
            block = jnp.concatenate([block] + others, axis=0)
            stride *= radix
        return [block]
    held = {0: block}
    for place in range(1, size):
        if place & 1:
            continue
        high = 1 << (place.bit_length() - 1)
        held[place] = exchange(held[0 if place == high else high], place if place == high else place ^ high)
    for place in range(1, size, 2):
        held[place] = exchange(held[place ^ 1], 1)
    return [held[place] for place in range(size)]


def maximum_over_group(values):
    size = lax.axis_size("tmpl")
    radix = 4 if size > 4 and size % 4 == 0 else 2
    near = [list(range(first, first + radix)) for first in range(0, size, radix)]
    far = [list(range(first, size, radix)) for first in range(radix)]
    values = lax.pmax(values, "tmpl", axis_index_groups=near)
    return lax.pmax(values, "tmpl", axis_index_groups=far)


def arrange_kernel(offset_ref, coeffs_ref, out_ref):
    bases = coeffs_ref.shape[2]
    source = lax.broadcasted_iota(jnp.int32, (bases, bases), 0)
    target = lax.broadcasted_iota(jnp.int32, (bases, bases), 1) ^ offset_ref[0]
    select = jnp.where(source == target, 1.0, 0.0).astype(jnp.bfloat16)
    for section in range(coeffs_ref.shape[0]):
        out_ref[section] = jnp.dot(
            coeffs_ref[section], select, preferred_element_type=jnp.float32
        ).astype(out_ref.dtype)


def arrange(coeffs, offset):
    return pl.pallas_call(
        arrange_kernel,
        out_shape=jax.ShapeDtypeStruct(coeffs.shape, coeffs.dtype),
        in_specs=[
            pl.BlockSpec(memory_space=pltpu.SMEM),
            pl.BlockSpec(memory_space=pltpu.VMEM),
        ],
        out_specs=pl.BlockSpec(memory_space=pltpu.VMEM),
        compiler_params=pltpu.CompilerParams(vmem_limit_bytes=16 * 2**20),
        cost_estimate=pl.CostEstimate(
            flops=2 * coeffs.size * coeffs.shape[2],
            bytes_accessed=4 * coeffs.size,
            transcendentals=0,
        ),
        name="arrange",
    )(offset, coeffs)


def recon_kernel(coeffs_ref, *refs):
    pieces, snr_ref, peak_ref = refs[-3::-1], refs[-2], refs[-1]
    samples = snr_ref.shape[1]
    source = lax.broadcasted_iota(jnp.int32, (2 * LANE, 2 * LANE), 0) % LANE
    target = lax.broadcasted_iota(jnp.int32, (2 * LANE, 2 * LANE), 1) // 2
    repeat = jnp.where(source == target, 1.0, 0.0).astype(jnp.bfloat16)
    running = None
    for section in (3, 2, 1, 0):
        width = samples >> section
        offset = sum(samples >> s for s in range(section))
        summed = []
        for place in range(0, width, 2 * LANE):
            size = min(2 * LANE, width)
            first = offset + place
            basis = jnp.concatenate([ref[:, first : first + size] for ref in pieces], axis=0)
            part = jnp.dot(coeffs_ref[section], basis, preferred_element_type=jnp.float32)
            if running is not None:
                coarse = running[place // (2 * LANE)]
                high = coarse.astype(jnp.bfloat16)
                low = (coarse - high.astype(jnp.float32)).astype(jnp.bfloat16)
                part = part + jnp.dot(
                    jnp.concatenate([high, low], axis=1),
                    repeat,
                    preferred_element_type=jnp.float32,
                )
            summed.append(part)
        running = []
        for part in summed:
            running += [part[:, at : at + LANE] for at in range(0, part.shape[1], LANE)]
        if section == 0:
            for number, part in enumerate(summed):
                place = number * 2 * LANE
                snr_ref[:, place : place + 2 * LANE] = part.astype(snr_ref.dtype)
                peak_ref[:, place : place + 2 * LANE] = jnp.max(
                    jnp.abs(part), axis=0, keepdims=True
                )


def reconstruct(coeffs, blocks, samples):
    return pl.pallas_call(
        recon_kernel,
        out_shape=(
            jax.ShapeDtypeStruct((coeffs.shape[1], samples), jnp.bfloat16),
            jax.ShapeDtypeStruct((1, samples), jnp.float32),
        ),
        in_specs=[pl.BlockSpec(memory_space=pltpu.VMEM)] * (1 + len(blocks)),
        out_specs=(pl.BlockSpec(memory_space=pltpu.VMEM),) * 2,
        compiler_params=pltpu.CompilerParams(vmem_limit_bytes=16 * 2**20),
        name="reconstruct",
    )(coeffs, *blocks[::-1])


def per_device(strain_fast, strain_half, strain_quarter, strain_eighth, basis_taps, recon_coeffs):
    streams = (strain_fast, strain_half, strain_quarter, strain_eighth)
    samples = strain_fast.shape[0] - basis_taps.shape[2]
    offset = (lax.axis_index("tmpl") * basis_taps.shape[1]).astype(jnp.int32).reshape(1)
    blocks = gather_blocks(correlate(streams, basis_taps))
    coeffs = arrange(recon_coeffs, offset)
    snr_series, local_peak = reconstruct(coeffs, blocks, samples)
    peak_snr = maximum_over_group(local_peak.reshape(samples))
    return (snr_series, peak_snr)


def solution(mesh):
    in_specs = (P(), P(), P(), P(), P("bank", "tmpl", None), P("bank", "tmpl", None))
    out_specs = (P(("bank", "tmpl"), None), P("bank"))
    return jax.shard_map(
        per_device, mesh=mesh, in_specs=in_specs, out_specs=out_specs, check_vma=False
    )
```

```python
import functools

import jax
import jax.numpy as jnp
from jax import lax
from jax.experimental import pallas as pl
from jax.experimental.pallas import tpu as pltpu
from jax.sharding import PartitionSpec as P

LANE = 128
CHUNK = 16
ROLLS = 4
HANDED = (0, 1, 2, 3, 8, 9, 4, 5, 6, 7, 14, 15, 12, 13, 10, 11)
SUB = 16


def correlate_kernel(*refs):
    strain_refs, taps_ref, out_ref = refs[:4], refs[4], refs[5]
    held_strains = refs[6:10]
    held_taps, line_ref, row_ref, wide_ref, strain_sems, taps_sems = refs[10:]
    sections = len(strain_refs)
    rows, taps = taps_ref.shape[1], taps_ref.shape[2]
    lines = [ref.shape[0] for ref in held_strains]
    blocks = [count - taps // LANE for count in lines]
    slot = line_ref.shape[0] // sections
    every = sections * slot
    pad = (max(blocks) - 1) * LANE
    strain_copies, taps_copies = [], []
    for section, source in enumerate(strain_refs):
        strain_copies.append(
            pltpu.make_async_copy(source, held_strains[section], strain_sems.at[section])
        )
        taps_copies.append(
            pltpu.make_async_copy(
                taps_ref.at[section],
                held_taps.at[section, :, pl.ds(pad, taps)],
                taps_sems.at[section],
            )
        )
    for copy in strain_copies + taps_copies:
        copy.start()
    for section in range(sections):
        held_taps[section, :, :pad] = jnp.zeros((rows, pad), held_taps.dtype)
        after = held_taps.shape[2] - pad - taps
        held_taps[section, :, pad + taps :] = jnp.zeros((rows, after), held_taps.dtype)

    for section, copy in enumerate(strain_copies):
        copy.wait()
        first = section * slot
        line_ref[first : first + lines[section], :] = held_strains[section][...].astype(jnp.float32)
        if slot > lines[section]:
            line_ref[first + lines[section] : first + slot, :] = jnp.zeros(
                (slot - lines[section], LANE), jnp.float32
            )
    pairs = jnp.concatenate(
        [
            line_ref[...].astype(jnp.bfloat16),
            jnp.concatenate([line_ref[1:, :], jnp.zeros((1, LANE), jnp.float32)], axis=0).astype(
                jnp.bfloat16
            ),
        ],
        axis=1,
    )
    source = lax.broadcasted_iota(jnp.int32, (2 * LANE, 2 * LANE), 0)
    target = lax.broadcasted_iota(jnp.int32, (2 * LANE, 2 * LANE), 1)
    target = target % LANE + target // LANE
    for r in range(0, SUB, 2):
        select = jnp.where(source == target + r, 1.0, 0.0).astype(jnp.bfloat16)
        moved = jnp.dot(pairs, select, preferred_element_type=jnp.float32)
        row_ref[r * every : (r + 1) * every, :] = moved[:, :LANE]
        row_ref[(r + 1) * every : (r + 2) * every, :] = moved[:, LANE:]

    def place_rows(number, carry):
        for line in range(SUB):
            line = number * SUB + line
            piece = row_ref[pl.ds(line, SUB, stride=every), :].astype(jnp.bfloat16)
            wide_ref[:, pl.ds(pl.multiple_of(line * LANE, LANE), LANE)] = piece
        return carry

    lax.fori_loop(0, every // SUB, place_rows, 0)
    wide_ref[:, every * LANE :] = jnp.zeros((SUB, LANE), wide_ref.dtype)
    for copy in taps_copies:
        copy.wait()

    extra = LANE // SUB - ROLLS
    source = lax.broadcasted_iota(jnp.int32, (2 * LANE, extra * LANE), 0)
    target = lax.broadcasted_iota(jnp.int32, (2 * LANE, extra * LANE), 1)
    target = target % LANE + (target // LANE + ROLLS) * SUB
    shifts = jnp.where(source == target, 1.0, 0.0).astype(jnp.bfloat16)

    def frames(section, tile, tiles):
        width = (tiles + 1) * LANE
        first = (section * slot + tile) * LANE
        if not isinstance(first, int):
            first = pl.multiple_of(first, LANE)
        wide = wide_ref[:, pl.ds(first, width)]
        moved = [wide]
        for q in range(1, ROLLS):
            moved.append(pltpu.roll(wide, width - SUB * q, axis=1))
        stacked = jnp.concatenate(
            [wide[:, number * LANE : (number + 2) * LANE] for number in range(tiles)], axis=0
        )
        rest = jnp.dot(stacked, shifts, preferred_element_type=jnp.float32).astype(wide.dtype)
        pieces = []
        for number in range(tiles):
            pieces += [part[:, number * LANE : (number + 1) * LANE] for part in moved]
            pieces += [
                rest[number * SUB : (number + 1) * SUB, q * LANE : (q + 1) * LANE]
                for q in range(LANE // SUB - ROLLS)
            ]
        return jnp.concatenate(pieces, axis=0)

    def shifted(section, tile, tiles):
        pieces = []
        for u in range(blocks[section]):
            first = pad + (tile - u) * LANE
            if not isinstance(first, int):
                first = pl.multiple_of(first, LANE)
            pieces.append(held_taps[section, :, pl.ds(first, tiles * LANE)])
        return pieces

    def term(group, tile, tiles):
        left, right = [], []
        for section in group:
            left += shifted(section, tile, tiles)
            right.append(frames(section, tile, tiles))
        left = jnp.concatenate(left, axis=0) if len(left) > 1 else left[0]
        right = jnp.concatenate(right, axis=1) if len(right) > 1 else right[0]
        both = jnp.dot(left, right, preferred_element_type=jnp.float32)
        parts, row = [], 0
        for number, section in enumerate(group):
            height = blocks[section] * rows
            parts.append(both[row : row + height, number * LANE : (number + 1) * LANE])
            row += height
        return parts

    groups = [list(range(first, min(first + 2, sections))) for first in range(0, sections, 2)]

    def step(number, totals):
        parts = []
        for group in groups:
            parts += term(group, number * CHUNK, CHUNK)
        return tuple(total + part for total, part in zip(totals, parts))

    totals = lax.fori_loop(
        0,
        taps // (CHUNK * LANE),
        step,
        tuple(jnp.zeros((count * rows, LANE), jnp.float32) for count in blocks),
    )
    totals = list(totals)
    for group in groups:
        end = max(blocks[section] for section in group) - 1
        for tile in range(0, end, CHUNK):
            active = [section for section in group if blocks[section] - 1 > tile]
            for section, part in zip(
                active, term(active, taps // LANE + tile, min(CHUNK, end - tile))
            ):
                totals[section] = totals[section] + part
    place = 0
    for section, total in enumerate(totals):
        for u in range(blocks[section]):
            part = total[u * rows : (u + 1) * rows].astype(out_ref.dtype)
            out_ref[:, place : place + LANE] = part
            place += LANE


def correlate(streams, basis_taps):
    sections, rows, taps = basis_taps.shape
    padded = -(-rows // SUB) * SUB
    if padded != rows:
        basis_taps = jnp.pad(basis_taps, ((0, 0), (0, padded - rows), (0, 0)))
    samples = sum(x.shape[0] - taps for x in streams)
    longest = max(x.shape[0] for x in streams)
    slot = -(-longest // (8 * LANE)) * 8
    lines = [x.reshape(-1, LANE) for x in streams]
    out = pl.pallas_call(
        correlate_kernel,
        out_shape=jax.ShapeDtypeStruct((padded, samples), jnp.bfloat16),
        in_specs=[pl.BlockSpec(memory_space=pltpu.HBM)] * (sections + 1),
        out_specs=pl.BlockSpec(memory_space=pltpu.VMEM),
        scratch_shapes=[pltpu.VMEM(x.shape, x.dtype) for x in lines]
        + [
            pltpu.VMEM((sections, padded, 2 * longest - taps), jnp.bfloat16),
            pltpu.VMEM((sections * slot, LANE), jnp.float32),
            pltpu.VMEM((SUB * sections * slot, LANE), jnp.float32),
            pltpu.VMEM((SUB, (sections * slot + 1) * LANE), jnp.bfloat16),
            pltpu.SemaphoreType.DMA((sections,)),
            pltpu.SemaphoreType.DMA((sections,)),
        ],
        compiler_params=pltpu.CompilerParams(vmem_limit_bytes=60 * 2**20),
        cost_estimate=pl.CostEstimate(
            flops=2 * padded * taps * samples,
            bytes_accessed=2 * sections * padded * taps,
            transcendentals=0,
        ),
        name="correlate",
    )(*lines, basis_taps)
    return out[:rows]


def exchange(block, distance):
    size = lax.axis_size("tmpl")
    return lax.ppermute(block, "tmpl", [(i, i ^ distance) for i in range(size)])


def gather_blocks(block):
    size = lax.axis_size("tmpl")
    if block.shape[0] % SUB:
        stride = 1
        while stride < size:
            radix = 4 if size // stride >= 4 else 2
            others = [exchange(block, step * stride) for step in range(1, radix)]
            block = jnp.concatenate([block] + others, axis=0)
            stride *= radix
        return [block]
    held = {0: block}
    for place in range(1, size):
        if place & 1:
            continue
        high = 1 << (place.bit_length() - 1)
        held[place] = exchange(held[0 if place == high else high], place if place == high else place ^ high)
    for place in range(1, size, 2):
        held[place] = exchange(held[place ^ 1], 1)
    return [held[place] for place in range(size)]


def maximum_over_group(values):
    size = lax.axis_size("tmpl")
    tiles = values.reshape(1, -1, LANE)
    copies = jnp.broadcast_to(tiles, (size,) + tiles.shape[1:])
    others = lax.all_to_all(copies, "tmpl", split_axis=0, concat_axis=0, tiled=True)
    return jnp.max(others, axis=0).reshape(values.shape)


def arrange_kernel(offset_ref, coeffs_ref, out_ref):
    bases = coeffs_ref.shape[2]
    source = lax.broadcasted_iota(jnp.int32, (bases, bases), 0)
    target = lax.broadcasted_iota(jnp.int32, (bases, bases), 1) ^ offset_ref[0]
    select = jnp.where(source == target, 1.0, 0.0).astype(jnp.bfloat16)
    for section in range(coeffs_ref.shape[0]):
        out_ref[section] = jnp.dot(
            coeffs_ref[section], select, preferred_element_type=jnp.float32
        ).astype(out_ref.dtype)


def arrange(coeffs, offset):
    return pl.pallas_call(
        arrange_kernel,
        out_shape=jax.ShapeDtypeStruct(coeffs.shape, coeffs.dtype),
        in_specs=[
            pl.BlockSpec(memory_space=pltpu.SMEM),
            pl.BlockSpec(memory_space=pltpu.VMEM),
        ],
        out_specs=pl.BlockSpec(memory_space=pltpu.VMEM),
        compiler_params=pltpu.CompilerParams(vmem_limit_bytes=16 * 2**20),
        cost_estimate=pl.CostEstimate(
            flops=2 * coeffs.size * coeffs.shape[2],
            bytes_accessed=4 * coeffs.size,
            transcendentals=0,
        ),
        name="arrange",
    )(offset, coeffs)


def recon_kernel(order, coeffs_ref, *refs):
    pieces = [refs[order.index(place)] for place in range(len(order))]
    snr_ref, peak_ref = refs[-2], refs[-1]
    samples = snr_ref.shape[1]
    source = lax.broadcasted_iota(jnp.int32, (2 * LANE, 2 * LANE), 0) % LANE
    target = lax.broadcasted_iota(jnp.int32, (2 * LANE, 2 * LANE), 1) // 2
    repeat = jnp.where(source == target, 1.0, 0.0).astype(jnp.bfloat16)
    running = None
    for section in (3, 2, 1, 0):
        width = samples >> section
        offset = sum(samples >> s for s in range(section))
        summed = []
        for place in range(0, width, 2 * LANE):
            size = min(2 * LANE, width)
            first = offset + place
            basis = jnp.concatenate([ref[:, first : first + size] for ref in pieces], axis=0)
            part = jnp.dot(coeffs_ref[section], basis, preferred_element_type=jnp.float32)
            if running is not None:
                coarse = running[place // (2 * LANE)]
                high = coarse.astype(jnp.bfloat16)
                low = (coarse - high.astype(jnp.float32)).astype(jnp.bfloat16)
                part = part + jnp.dot(
                    jnp.concatenate([high, low], axis=1),
                    repeat,
                    preferred_element_type=jnp.float32,
                )
            summed.append(part)
        running = []
        for part in summed:
            running += [part[:, at : at + LANE] for at in range(0, part.shape[1], LANE)]
        if section == 0:
            for number, part in enumerate(summed):
                place = number * 2 * LANE
                snr_ref[:, place : place + 2 * LANE] = part.astype(snr_ref.dtype)
                peak_ref[:, place : place + 2 * LANE] = jnp.max(
                    jnp.abs(part), axis=0, keepdims=True
                )


def reconstruct(coeffs, blocks, samples):
    order = HANDED if len(HANDED) == len(blocks) else tuple(range(len(blocks)))
    return pl.pallas_call(
        functools.partial(recon_kernel, order),
        out_shape=(
            jax.ShapeDtypeStruct((coeffs.shape[1], samples), jnp.bfloat16),
            jax.ShapeDtypeStruct((1, samples), jnp.float32),
        ),
        in_specs=[pl.BlockSpec(memory_space=pltpu.VMEM)] * (1 + len(blocks)),
        out_specs=(pl.BlockSpec(memory_space=pltpu.VMEM),) * 2,
        compiler_params=pltpu.CompilerParams(vmem_limit_bytes=16 * 2**20),
        name="reconstruct",
    )(coeffs, *[blocks[place] for place in order])


def per_device(strain_fast, strain_half, strain_quarter, strain_eighth, basis_taps, recon_coeffs):
    streams = (strain_fast, strain_half, strain_quarter, strain_eighth)
    samples = strain_fast.shape[0] - basis_taps.shape[2]
    offset = (lax.axis_index("tmpl") * basis_taps.shape[1]).astype(jnp.int32).reshape(1)
    blocks = gather_blocks(correlate(streams, basis_taps))
    coeffs = arrange(recon_coeffs, offset)
    snr_series, local_peak = reconstruct(coeffs, blocks, samples)
    peak_snr = maximum_over_group(local_peak.reshape(samples))
    return (snr_series, peak_snr)


def solution(mesh):
    in_specs = (P(), P(), P(), P(), P("bank", "tmpl", None), P("bank", "tmpl", None))
    out_specs = (P(("bank", "tmpl"), None), P("bank"))
    return jax.shard_map(
        per_device, mesh=mesh, in_specs=in_specs, out_specs=out_specs, check_vma=False
    )
```

```python
import functools

import jax
import jax.numpy as jnp
from jax import lax
from jax.experimental import pallas as pl
from jax.experimental.pallas import tpu as pltpu
from jax.sharding import PartitionSpec as P

LANE = 128
CHUNK = 8
SUB = 16
ROWS = 8
ROLLS = 4
TIED = 1
HANDED = (0, 1, 2, 3, 8, 9, 4, 5, 6, 7, 12, 13, 14, 15, 10, 11)
SUB = 16


def correlate_kernel(*refs):
    strain_refs, taps_ref, out_ref = refs[:4], refs[4], refs[5]
    held_strains, held_taps, line_ref, total_ref = refs[6:10], refs[10], refs[11], refs[12]
    even_refs, odd_refs, strain_sems, taps_sems = refs[13:15], refs[15:17], refs[17], refs[18]
    sections = len(strain_refs)
    rows, taps = taps_ref.shape[1], taps_ref.shape[2]
    lines = [ref.shape[0] for ref in held_strains]
    blocks = [count - taps // LANE for count in lines]
    slot = line_ref.shape[0] // sections
    pad = (max(blocks) - 1) * LANE
    groups = ((0, 1), (2, 3))
    strain_copies, taps_copies = [], []
    for section, source in enumerate(strain_refs):
        strain_copies.append(
            pltpu.make_async_copy(source, held_strains[section], strain_sems.at[section])
        )
        taps_copies.append(
            pltpu.make_async_copy(
                taps_ref.at[section],
                held_taps.at[section, :, pl.ds(pad, taps)],
                taps_sems.at[section],
            )
        )
    for copy in strain_copies + taps_copies:
        copy.start()
    after = held_taps.shape[2] - pad - taps
    for section in range(sections):
        held_taps[section, :, :pad] = jnp.zeros((rows, pad), held_taps.dtype)
        held_taps[section, :, pad + taps :] = jnp.zeros((rows, after), held_taps.dtype)
    total_ref[...] = jnp.zeros(total_ref.shape, total_ref.dtype)

    extra = LANE // SUB - ROLLS
    source = lax.broadcasted_iota(jnp.int32, (2 * LANE, extra * LANE), 0)
    target = lax.broadcasted_iota(jnp.int32, (2 * LANE, extra * LANE), 1)
    target = target % LANE + (target // LANE + ROLLS) * SUB
    shifts = jnp.where(source == target, 1.0, 0.0).astype(jnp.bfloat16)

    for section, copy in enumerate(strain_copies):
        copy.wait()
        first = section * slot
        line_ref[first : first + lines[section], :] = held_strains[section][...].astype(jnp.float32)
        line_ref[first + lines[section] : first + slot, :] = jnp.zeros(
            (slot - lines[section], LANE), jnp.float32
        )

    width = (CHUNK + 1) * LANE
    row = lax.broadcasted_iota(jnp.int32, (ROWS, width), 0)

    def build(frames, section, chunk):
        first = section * slot + chunk * CHUNK
        wide = jnp.concatenate(
            [
                jnp.broadcast_to(line_ref[pl.ds(first + number, 1), :], (ROWS, LANE))
                for number in range(CHUNK + 1)
            ],
            axis=1,
        )
        for step in (1, 2, 4):
            moved = pltpu.roll(wide, width - step, axis=1)
            wide = jnp.where((row & step) != 0, moved, wide)
        wide = jnp.concatenate([wide, pltpu.roll(wide, width - ROWS, axis=1)], axis=0)
        wide = wide.astype(jnp.bfloat16)
        moved = [wide]
        for q in range(1, ROLLS):
            moved.append(pltpu.roll(wide, width - SUB * q, axis=1))
        stacked = jnp.concatenate(
            [wide[:, number * LANE : (number + 2) * LANE] for number in range(CHUNK)], axis=0
        )
        rest = jnp.dot(stacked, shifts, preferred_element_type=jnp.float32).astype(wide.dtype)
        for number in range(CHUNK):
            pieces = [part[:, number * LANE : (number + 1) * LANE] for part in moved]
            pieces += [
                rest[number * SUB : (number + 1) * SUB, q * LANE : (q + 1) * LANE]
                for q in range(extra)
            ]
            half = section % 2
            frames[number * LANE : (number + 1) * LANE, half * LANE : (half + 1) * LANE] = (
                jnp.concatenate(pieces, axis=0)
            )

    def shifted(section, chunk, tiles):
        pieces = []
        for u in range(blocks[section]):
            first = pad + (chunk * CHUNK - u) * LANE
            if not isinstance(first, int):
                first = pl.multiple_of(first, LANE)
            pieces.append(held_taps[section, :, pl.ds(first, tiles * LANE)])
        return pieces

    def accumulate(frames, group, chunk, tiles=CHUNK):
        left = []
        for section in group:
            left += shifted(section, chunk, tiles)
        left = jnp.concatenate(left, axis=0) if len(left) > 1 else left[0]
        both = jnp.dot(
            left, frames[: tiles * LANE, :], preferred_element_type=jnp.float32
        )
        height = 0
        for section in group:
            size = blocks[section] * rows
            half = section % 2
            at = sum(blocks[:section]) * rows
            total_ref[at : at + size, :] += both[
                height : height + size, half * LANE : (half + 1) * LANE
            ]
            height += size

    def build_all(frames, chunk):
        for section in range(sections):
            build(frames[section // 2], section, chunk)

    build_all(even_refs, 0)
    for copy in taps_copies:
        copy.wait()

    def step(number, carry):
        for group, frames in zip(groups, even_refs):
            accumulate(frames, group, 2 * number)
        build_all(odd_refs, 2 * number + 1)
        for group, frames in zip(groups, odd_refs):
            accumulate(frames, group, 2 * number + 1)
        build_all(even_refs, 2 * number + 2)
        return carry

    chunks = taps // (CHUNK * LANE)
    lax.fori_loop(0, chunks // 2, step, 0)
    for group, frames in zip(groups, even_refs):
        active = [section for section in group if blocks[section] > 1]
        if active:
            accumulate(frames, active, chunks, max(blocks[section] for section in active) - 1)
    place = 0
    for section in range(sections):
        for u in range(blocks[section]):
            at = (sum(blocks[:section]) + u) * rows
            out_ref[:, place : place + LANE] = total_ref[at : at + rows, :].astype(out_ref.dtype)
            place += LANE


def correlate(streams, basis_taps):
    sections, rows, taps = basis_taps.shape
    padded = -(-rows // SUB) * SUB
    if padded != rows:
        basis_taps = jnp.pad(basis_taps, ((0, 0), (0, padded - rows), (0, 0)))
    samples = sum(x.shape[0] - taps for x in streams)
    longest = max(x.shape[0] for x in streams)
    slot = -(-(longest + LANE) // (8 * LANE)) * 8
    lines = [x.reshape(-1, LANE) for x in streams]
    out = pl.pallas_call(
        correlate_kernel,
        out_shape=jax.ShapeDtypeStruct((padded, samples), jnp.bfloat16),
        in_specs=[pl.BlockSpec(memory_space=pltpu.HBM)] * (sections + 1),
        out_specs=pl.BlockSpec(memory_space=pltpu.VMEM),
        scratch_shapes=[pltpu.VMEM(x.shape, x.dtype) for x in lines]
        + [
            pltpu.VMEM((sections, padded, 2 * longest - taps), jnp.bfloat16),
            pltpu.VMEM((sections * slot, LANE), jnp.float32),
            pltpu.VMEM((samples // LANE * padded, LANE), jnp.float32),
        ]
        + [pltpu.VMEM((CHUNK * LANE, 2 * LANE), jnp.bfloat16)] * 4
        + [
            pltpu.SemaphoreType.DMA((sections,)),
            pltpu.SemaphoreType.DMA((sections,)),
        ],
        compiler_params=pltpu.CompilerParams(vmem_limit_bytes=60 * 2**20),
        cost_estimate=pl.CostEstimate(
            flops=2 * padded * taps * samples,
            bytes_accessed=2 * sections * padded * taps,
            transcendentals=0,
        ),
        name="correlate",
    )(*lines, basis_taps)
    return out[:rows]


def exchange(block, distance):
    size = lax.axis_size("tmpl")
    return lax.ppermute(block, "tmpl", [(i, i ^ distance) for i in range(size)])


def gather_blocks(block, ready):
    size = lax.axis_size("tmpl")
    if block.shape[0] % SUB:
        stride = 1
        while stride < size:
            radix = 4 if size // stride >= 4 else 2
            others = [exchange(block, step * stride) for step in range(1, radix)]
            block = jnp.concatenate([block] + others, axis=0)
            stride *= radix
        return [block], ready
    held = {0: block}
    for place in range(2, size, 2):
        high = 1 << (place.bit_length() - 1)
        held[place] = exchange(held[place ^ high and high], place ^ high or place)
    for place in range(1, size, 2):
        source = held[place ^ 1]
        if place == TIED:
            source, ready = lax.optimization_barrier((source, ready))
        held[place] = exchange(source, 1)
    return [held[place] for place in range(size)], ready


def maximum_over_group(values):
    size = lax.axis_size("tmpl")
    tiles = values.reshape(1, -1, LANE)
    copies = jnp.broadcast_to(tiles, (size,) + tiles.shape[1:])
    others = lax.all_to_all(copies, "tmpl", split_axis=0, concat_axis=0, tiled=True)
    return jnp.max(others, axis=0).reshape(values.shape)


def arrange_kernel(offset_ref, coeffs_ref, out_ref):
    bases = coeffs_ref.shape[2]
    source = lax.broadcasted_iota(jnp.int32, (bases, bases), 0)
    target = lax.broadcasted_iota(jnp.int32, (bases, bases), 1) ^ offset_ref[0]
    select = jnp.where(source == target, 1.0, 0.0).astype(jnp.bfloat16)
    for section in range(coeffs_ref.shape[0]):
        out_ref[section] = jnp.dot(
            coeffs_ref[section], select, preferred_element_type=jnp.float32
        ).astype(out_ref.dtype)


def arrange(coeffs, offset):
    return pl.pallas_call(
        arrange_kernel,
        out_shape=jax.ShapeDtypeStruct(coeffs.shape, coeffs.dtype),
        in_specs=[
            pl.BlockSpec(memory_space=pltpu.SMEM),
            pl.BlockSpec(memory_space=pltpu.VMEM),
        ],
        out_specs=pl.BlockSpec(memory_space=pltpu.VMEM),
        compiler_params=pltpu.CompilerParams(vmem_limit_bytes=16 * 2**20),
        cost_estimate=pl.CostEstimate(
            flops=2 * coeffs.size * coeffs.shape[2],
            bytes_accessed=4 * coeffs.size,
            transcendentals=0,
        ),
        name="arrange",
    )(offset, coeffs)


def recon_kernel(order, coeffs_ref, *refs):
    pieces = [refs[order.index(place)] for place in range(len(order))]
    snr_ref, peak_ref = refs[-2], refs[-1]
    samples = snr_ref.shape[1]
    source = lax.broadcasted_iota(jnp.int32, (2 * LANE, 2 * LANE), 0) % LANE
    target = lax.broadcasted_iota(jnp.int32, (2 * LANE, 2 * LANE), 1) // 2
    repeat = jnp.where(source == target, 1.0, 0.0).astype(jnp.bfloat16)
    running = None
    for section in (3, 2, 1, 0):
        width = samples >> section
        offset = sum(samples >> s for s in range(section))
        summed = []
        for place in range(0, width, 2 * LANE):
            size = min(2 * LANE, width)
            first = offset + place
            basis = jnp.concatenate([ref[:, first : first + size] for ref in pieces], axis=0)
            part = jnp.dot(coeffs_ref[section], basis, preferred_element_type=jnp.float32)
            if running is not None:
                coarse = running[place // (2 * LANE)]
                high = coarse.astype(jnp.bfloat16)
                low = (coarse - high.astype(jnp.float32)).astype(jnp.bfloat16)
                part = part + jnp.dot(
                    jnp.concatenate([high, low], axis=1),
                    repeat,
                    preferred_element_type=jnp.float32,
                )
            summed.append(part)
        running = []
        for part in summed:
            running += [part[:, at : at + LANE] for at in range(0, part.shape[1], LANE)]
        if section == 0:
            for number, part in enumerate(summed):
                place = number * 2 * LANE
                snr_ref[:, place : place + 2 * LANE] = part.astype(snr_ref.dtype)
                peak_ref[:, place : place + 2 * LANE] = jnp.max(
                    jnp.abs(part), axis=0, keepdims=True
                )


def reconstruct(coeffs, blocks, samples):
    order = HANDED if len(HANDED) == len(blocks) else tuple(range(len(blocks)))
    return pl.pallas_call(
        functools.partial(recon_kernel, order),
        out_shape=(
            jax.ShapeDtypeStruct((coeffs.shape[1], samples), jnp.bfloat16),
            jax.ShapeDtypeStruct((1, samples), jnp.float32),
        ),
        in_specs=[pl.BlockSpec(memory_space=pltpu.VMEM)] * (1 + len(blocks)),
        out_specs=(pl.BlockSpec(memory_space=pltpu.VMEM),) * 2,
        compiler_params=pltpu.CompilerParams(vmem_limit_bytes=16 * 2**20),
        name="reconstruct",
    )(coeffs, *[blocks[place] for place in order])


def per_device(strain_fast, strain_half, strain_quarter, strain_eighth, basis_taps, recon_coeffs):
    streams = (strain_fast, strain_half, strain_quarter, strain_eighth)
    samples = strain_fast.shape[0] - basis_taps.shape[2]
    offset = (lax.axis_index("tmpl") * basis_taps.shape[1]).astype(jnp.int32).reshape(1)
    coeffs = arrange(recon_coeffs, offset)
    blocks, coeffs = gather_blocks(correlate(streams, basis_taps), coeffs)
    snr_series, local_peak = reconstruct(coeffs, blocks, samples)
    peak_snr = maximum_over_group(local_peak.reshape(samples))
    return (snr_series, peak_snr)


def solution(mesh):
    in_specs = (P(), P(), P(), P(), P("bank", "tmpl", None), P("bank", "tmpl", None))
    out_specs = (P(("bank", "tmpl"), None), P("bank"))
    return jax.shard_map(
        per_device, mesh=mesh, in_specs=in_specs, out_specs=out_specs, check_vma=False
    )
```

```python
import functools

import jax
import jax.numpy as jnp
from jax import lax
from jax.experimental import pallas as pl
from jax.experimental.pallas import tpu as pltpu
from jax.sharding import PartitionSpec as P

LANE = 128
CHUNK = 8
SUB = 16
ROWS = 8
ROLLS = 4
TIED = 1
HANDED = (0, 1, 2, 3, 8, 9, 4, 5, 6, 7, 12, 13, 14, 15, 10, 11)
SUB = 16


def correlate_kernel(*refs):
    strain_refs, taps_ref, out_ref = refs[:4], refs[4], refs[5]
    held_strains, held_taps, line_ref, total_ref = refs[6:10], refs[10], refs[11], refs[12]
    even_refs, odd_refs, strain_sems, taps_sems = refs[13:15], refs[15:17], refs[17], refs[18]
    sections = len(strain_refs)
    rows, taps = taps_ref.shape[1], taps_ref.shape[2]
    lines = [ref.shape[0] for ref in held_strains]
    blocks = [count - taps // LANE for count in lines]
    slot = line_ref.shape[0] // sections
    pad = (max(blocks) - 1) * LANE
    groups = ((0, 1), (2, 3))
    strain_copies = []
    for section, source in enumerate(strain_refs):
        strain_copies.append(
            pltpu.make_async_copy(source, held_strains[section], strain_sems.at[section])
        )
    for copy in strain_copies:
        copy.start()
    span = CHUNK * LANE
    chunks = taps // span

    def taps_copy(section, chunk):
        first = chunk * span
        if not isinstance(first, int):
            first = pl.multiple_of(first, span)
        return pltpu.make_async_copy(
            taps_ref.at[section, :, pl.ds(first, span)],
            held_taps.at[section, :, pl.ds(pad + first, span)],
            taps_sems.at[section, chunk],
        )

    for chunk in range(chunks):
        for section in range(sections):
            taps_copy(section, chunk).start()
    after = held_taps.shape[2] - pad - taps
    for section in range(sections):
        held_taps[section, :, :pad] = jnp.zeros((rows, pad), held_taps.dtype)
        held_taps[section, :, pad + taps :] = jnp.zeros((rows, after), held_taps.dtype)
    total_ref[...] = jnp.zeros(total_ref.shape, total_ref.dtype)

    extra = LANE // SUB - ROLLS
    source = lax.broadcasted_iota(jnp.int32, (2 * LANE, extra * LANE), 0)
    target = lax.broadcasted_iota(jnp.int32, (2 * LANE, extra * LANE), 1)
    target = target % LANE + (target // LANE + ROLLS) * SUB
    shifts = jnp.where(source == target, 1.0, 0.0).astype(jnp.bfloat16)

    for section, copy in enumerate(strain_copies):
        copy.wait()
        first = section * slot
        line_ref[first : first + lines[section], :] = held_strains[section][...].astype(jnp.float32)
        line_ref[first + lines[section] : first + slot, :] = jnp.zeros(
            (slot - lines[section], LANE), jnp.float32
        )

    width = (CHUNK + 1) * LANE
    row = lax.broadcasted_iota(jnp.int32, (ROWS, width), 0)

    def build(frames, section, chunk):
        first = section * slot + chunk * CHUNK
        wide = jnp.concatenate(
            [
                jnp.broadcast_to(line_ref[pl.ds(first + number, 1), :], (ROWS, LANE))
                for number in range(CHUNK + 1)
            ],
            axis=1,
        )
        for step in (1, 2, 4):
            moved = pltpu.roll(wide, width - step, axis=1)
            wide = jnp.where((row & step) != 0, moved, wide)
        wide = jnp.concatenate([wide, pltpu.roll(wide, width - ROWS, axis=1)], axis=0)
        wide = wide.astype(jnp.bfloat16)
        moved = [wide]
        for q in range(1, ROLLS):
            moved.append(pltpu.roll(wide, width - SUB * q, axis=1))
        stacked = jnp.concatenate(
            [wide[:, number * LANE : (number + 2) * LANE] for number in range(CHUNK)], axis=0
        )
        rest = jnp.dot(stacked, shifts, preferred_element_type=jnp.float32).astype(wide.dtype)
        for number in range(CHUNK):
            pieces = [part[:, number * LANE : (number + 1) * LANE] for part in moved]
            pieces += [
                rest[number * SUB : (number + 1) * SUB, q * LANE : (q + 1) * LANE]
                for q in range(extra)
            ]
            half = section % 2
            frames[number * LANE : (number + 1) * LANE, half * LANE : (half + 1) * LANE] = (
                jnp.concatenate(pieces, axis=0)
            )

    def shifted(section, chunk, tiles):
        pieces = []
        for u in range(blocks[section]):
            first = pad + (chunk * CHUNK - u) * LANE
            if not isinstance(first, int):
                first = pl.multiple_of(first, LANE)
            pieces.append(held_taps[section, :, pl.ds(first, tiles * LANE)])
        return pieces

    def accumulate(frames, group, chunk, tiles=CHUNK):
        left = []
        for section in group:
            left += shifted(section, chunk, tiles)
        left = jnp.concatenate(left, axis=0) if len(left) > 1 else left[0]
        both = jnp.dot(
            left, frames[: tiles * LANE, :], preferred_element_type=jnp.float32
        )
        height = 0
        for section in group:
            size = blocks[section] * rows
            half = section % 2
            at = sum(blocks[:section]) * rows
            total_ref[at : at + size, :] += both[
                height : height + size, half * LANE : (half + 1) * LANE
            ]
            height += size

    def build_all(frames, chunk):
        for section in range(sections):
            build(frames[section // 2], section, chunk)

    def arrive(chunk):
        for section in range(sections):
            taps_copy(section, chunk).wait()

    build_all(even_refs, 0)

    def step(number, carry):
        arrive(2 * number)
        for group, frames in zip(groups, even_refs):
            accumulate(frames, group, 2 * number)
        build_all(odd_refs, 2 * number + 1)
        arrive(2 * number + 1)
        for group, frames in zip(groups, odd_refs):
            accumulate(frames, group, 2 * number + 1)
        build_all(even_refs, 2 * number + 2)
        return carry

    lax.fori_loop(0, chunks // 2, step, 0)
    for group, frames in zip(groups, even_refs):
        active = [section for section in group if blocks[section] > 1]
        if active:
            accumulate(frames, active, chunks, max(blocks[section] for section in active) - 1)
    place = 0
    for section in range(sections):
        for u in range(blocks[section]):
            at = (sum(blocks[:section]) + u) * rows
            out_ref[:, place : place + LANE] = total_ref[at : at + rows, :].astype(out_ref.dtype)
            place += LANE


def correlate(streams, basis_taps):
    sections, rows, taps = basis_taps.shape
    padded = -(-rows // SUB) * SUB
    if padded != rows:
        basis_taps = jnp.pad(basis_taps, ((0, 0), (0, padded - rows), (0, 0)))
    samples = sum(x.shape[0] - taps for x in streams)
    longest = max(x.shape[0] for x in streams)
    slot = -(-(longest + LANE) // (8 * LANE)) * 8
    lines = [x.reshape(-1, LANE) for x in streams]
    out = pl.pallas_call(
        correlate_kernel,
        out_shape=pltpu.VMEM((padded, samples), jnp.bfloat16),
        in_specs=[pl.BlockSpec(memory_space=pltpu.HBM)] * (sections + 1),
        out_specs=pl.BlockSpec(memory_space=pltpu.VMEM),
        scratch_shapes=[pltpu.VMEM(x.shape, x.dtype) for x in lines]
        + [
            pltpu.VMEM((sections, padded, 2 * longest - taps), jnp.bfloat16),
            pltpu.VMEM((sections * slot, LANE), jnp.float32),
            pltpu.VMEM((samples // LANE * padded, LANE), jnp.float32),
        ]
        + [pltpu.VMEM((CHUNK * LANE, 2 * LANE), jnp.bfloat16)] * 4
        + [
            pltpu.SemaphoreType.DMA((sections,)),
            pltpu.SemaphoreType.DMA((sections, taps // (CHUNK * LANE))),
        ],
        compiler_params=pltpu.CompilerParams(vmem_limit_bytes=60 * 2**20),
        cost_estimate=pl.CostEstimate(
            flops=2 * padded * taps * samples,
            bytes_accessed=2 * sections * padded * taps,
            transcendentals=0,
        ),
        name="correlate",
    )(*lines, basis_taps)
    return out[:rows]


def exchange(block, distance):
    size = lax.axis_size("tmpl")
    return lax.ppermute(block, "tmpl", [(i, i ^ distance) for i in range(size)])


def gather_blocks(block, ready):
    size = lax.axis_size("tmpl")
    if block.shape[0] % SUB:
        stride = 1
        while stride < size:
            radix = 4 if size // stride >= 4 else 2
            others = [exchange(block, step * stride) for step in range(1, radix)]
            block = jnp.concatenate([block] + others, axis=0)
            stride *= radix
        return [block], ready
    held = {0: block}
    for place in range(2, size, 2):
        high = 1 << (place.bit_length() - 1)
        held[place] = exchange(held[place ^ high and high], place ^ high or place)
    for place in range(1, size, 2):
        source = held[place ^ 1]
        if place == TIED:
            source, ready = lax.optimization_barrier((source, ready))
        held[place] = exchange(source, 1)
    return [held[place] for place in range(size)], ready


def maximum_over_group(values):
    size = lax.axis_size("tmpl")
    tiles = values.reshape(1, -1, LANE)
    copies = jnp.broadcast_to(tiles, (size,) + tiles.shape[1:])
    others = lax.all_to_all(copies, "tmpl", split_axis=0, concat_axis=0, tiled=True)
    return jnp.max(others, axis=0).reshape(values.shape)


def arrange_kernel(offset_ref, coeffs_ref, out_ref):
    bases = coeffs_ref.shape[2]
    source = lax.broadcasted_iota(jnp.int32, (bases, bases), 0)
    target = lax.broadcasted_iota(jnp.int32, (bases, bases), 1) ^ offset_ref[0]
    select = jnp.where(source == target, 1.0, 0.0).astype(jnp.bfloat16)
    for section in range(coeffs_ref.shape[0]):
        out_ref[section] = jnp.dot(
            coeffs_ref[section], select, preferred_element_type=jnp.float32
        ).astype(out_ref.dtype)


def arrange(coeffs, offset):
    return pl.pallas_call(
        arrange_kernel,
        out_shape=jax.ShapeDtypeStruct(coeffs.shape, coeffs.dtype),
        in_specs=[
            pl.BlockSpec(memory_space=pltpu.SMEM),
            pl.BlockSpec(memory_space=pltpu.VMEM),
        ],
        out_specs=pl.BlockSpec(memory_space=pltpu.VMEM),
        compiler_params=pltpu.CompilerParams(vmem_limit_bytes=16 * 2**20),
        cost_estimate=pl.CostEstimate(
            flops=2 * coeffs.size * coeffs.shape[2],
            bytes_accessed=4 * coeffs.size,
            transcendentals=0,
        ),
        name="arrange",
    )(offset, coeffs)


def recon_kernel(order, coeffs_ref, *refs):
    pieces = [refs[order.index(place)] for place in range(len(order))]
    snr_ref, peak_ref = refs[-2], refs[-1]
    samples = snr_ref.shape[1]
    source = lax.broadcasted_iota(jnp.int32, (2 * LANE, 2 * LANE), 0) % LANE
    target = lax.broadcasted_iota(jnp.int32, (2 * LANE, 2 * LANE), 1) // 2
    repeat = jnp.where(source == target, 1.0, 0.0).astype(jnp.bfloat16)
    running = None
    for section in (3, 2, 1, 0):
        width = samples >> section
        offset = sum(samples >> s for s in range(section))
        summed = []
        for place in range(0, width, 2 * LANE):
            size = min(2 * LANE, width)
            first = offset + place
            basis = jnp.concatenate([ref[:, first : first + size] for ref in pieces], axis=0)
            part = jnp.dot(coeffs_ref[section], basis, preferred_element_type=jnp.float32)
            if running is not None:
                coarse = running[place // (2 * LANE)]
                high = coarse.astype(jnp.bfloat16)
                low = (coarse - high.astype(jnp.float32)).astype(jnp.bfloat16)
                part = part + jnp.dot(
                    jnp.concatenate([high, low], axis=1),
                    repeat,
                    preferred_element_type=jnp.float32,
                )
            summed.append(part)
        running = []
        for part in summed:
            running += [part[:, at : at + LANE] for at in range(0, part.shape[1], LANE)]
        if section == 0:
            for number, part in enumerate(summed):
                place = number * 2 * LANE
                snr_ref[:, place : place + 2 * LANE] = part.astype(snr_ref.dtype)
                peak_ref[:, place : place + 2 * LANE] = jnp.max(
                    jnp.abs(part), axis=0, keepdims=True
                )


def reconstruct(coeffs, blocks, samples):
    order = HANDED if len(HANDED) == len(blocks) else tuple(range(len(blocks)))
    return pl.pallas_call(
        functools.partial(recon_kernel, order),
        out_shape=(
            jax.ShapeDtypeStruct((coeffs.shape[1], samples), jnp.bfloat16),
            jax.ShapeDtypeStruct((1, samples), jnp.float32),
        ),
        in_specs=[pl.BlockSpec(memory_space=pltpu.VMEM)] * (1 + len(blocks)),
        out_specs=(pl.BlockSpec(memory_space=pltpu.VMEM),) * 2,
        compiler_params=pltpu.CompilerParams(vmem_limit_bytes=16 * 2**20),
        name="reconstruct",
    )(coeffs, *[blocks[place] for place in order])


def per_device(strain_fast, strain_half, strain_quarter, strain_eighth, basis_taps, recon_coeffs):
    streams = (strain_fast, strain_half, strain_quarter, strain_eighth)
    samples = strain_fast.shape[0] - basis_taps.shape[2]
    offset = (lax.axis_index("tmpl") * basis_taps.shape[1]).astype(jnp.int32).reshape(1)
    coeffs = arrange(recon_coeffs, offset)
    blocks, coeffs = gather_blocks(correlate(streams, basis_taps), coeffs)
    snr_series, local_peak = reconstruct(coeffs, blocks, samples)
    peak_snr = maximum_over_group(local_peak.reshape(samples))
    return (snr_series, peak_snr)


def solution(mesh):
    in_specs = (P(), P(), P(), P(), P("bank", "tmpl", None), P("bank", "tmpl", None))
    out_specs = (P(("bank", "tmpl"), None), P("bank"))
    return jax.shard_map(
        per_device, mesh=mesh, in_specs=in_specs, out_specs=out_specs, check_vma=False
    )
```

```python
import functools

import jax
import jax.numpy as jnp
from jax import lax
from jax.experimental import pallas as pl
from jax.experimental.pallas import tpu as pltpu
from jax.sharding import PartitionSpec as P

LANE = 128
CHUNK = 8
SUB = 16
ROWS = 8
ROLLS = 4
TIED = 1
HANDED = (0, 1, 2, 3, 8, 9, 4, 5, 6, 7, 12, 13, 14, 15, 10, 11)
SUB = 16


def correlate_kernel(*refs):
    strains, taps_ref, out_ref = refs[:4], refs[4], refs[5]
    line_ref, total_ref, even_refs, odd_refs = refs[6], refs[7], refs[8:10], refs[10:12]
    sections = len(strains)
    rows, taps = taps_ref.shape[1], taps_ref.shape[2]
    lines = [ref.shape[0] for ref in strains]
    blocks = [count - taps // LANE for count in lines]
    slot = line_ref.shape[0] // sections
    span = CHUNK * LANE
    chunks = taps // span
    groups = ((0, 1), (2, 3))
    total_ref[...] = jnp.zeros(total_ref.shape, total_ref.dtype)

    extra = LANE // SUB - ROLLS
    source = lax.broadcasted_iota(jnp.int32, (2 * LANE, extra * LANE), 0)
    target = lax.broadcasted_iota(jnp.int32, (2 * LANE, extra * LANE), 1)
    target = target % LANE + (target // LANE + ROLLS) * SUB
    shifts = jnp.where(source == target, 1.0, 0.0).astype(jnp.bfloat16)

    for section, strain in enumerate(strains):
        first = section * slot
        line_ref[first : first + lines[section], :] = strain[...].astype(jnp.float32)
        line_ref[first + lines[section] : first + slot, :] = jnp.zeros(
            (slot - lines[section], LANE), jnp.float32
        )

    width = (CHUNK + 1) * LANE
    row = lax.broadcasted_iota(jnp.int32, (ROWS, width), 0)

    def build(frames, section, chunk):
        first = section * slot + chunk * CHUNK
        wide = jnp.concatenate(
            [
                jnp.broadcast_to(line_ref[pl.ds(first + number, 1), :], (ROWS, LANE))
                for number in range(CHUNK + 1)
            ],
            axis=1,
        )
        for step in (1, 2, 4):
            moved = pltpu.roll(wide, width - step, axis=1)
            wide = jnp.where((row & step) != 0, moved, wide)
        wide = jnp.concatenate([wide, pltpu.roll(wide, width - ROWS, axis=1)], axis=0)
        wide = wide.astype(jnp.bfloat16)
        moved = [wide]
        for q in range(1, ROLLS):
            moved.append(pltpu.roll(wide, width - SUB * q, axis=1))
        stacked = jnp.concatenate(
            [wide[:, number * LANE : (number + 2) * LANE] for number in range(CHUNK)], axis=0
        )
        rest = jnp.dot(stacked, shifts, preferred_element_type=jnp.float32).astype(wide.dtype)
        for number in range(CHUNK):
            pieces = [part[:, number * LANE : (number + 1) * LANE] for part in moved]
            pieces += [
                rest[number * SUB : (number + 1) * SUB, q * LANE : (q + 1) * LANE]
                for q in range(extra)
            ]
            half = section % 2
            frames[number * LANE : (number + 1) * LANE, half * LANE : (half + 1) * LANE] = (
                jnp.concatenate(pieces, axis=0)
            )

    def shifted(section, chunk, tiles):
        pieces = []
        for u in range(blocks[section]):
            first, size = (chunk * CHUNK - u) * LANE, tiles * LANE
            if not isinstance(first, int):
                pieces.append(taps_ref[section, :, pl.ds(pl.multiple_of(first, LANE), size)])
                continue
            parts = []
            if first < 0:
                parts.append(jnp.zeros((rows, -first), taps_ref.dtype))
            if first < taps:
                parts.append(taps_ref[section, :, max(first, 0) : min(first + size, taps)])
            if first + size > taps:
                parts.append(jnp.zeros((rows, first + size - max(first, taps)), taps_ref.dtype))
            pieces.append(jnp.concatenate(parts, axis=1) if len(parts) > 1 else parts[0])
        return pieces

    def accumulate(frames, group, chunk, tiles=CHUNK):
        left = []
        for section in group:
            left += shifted(section, chunk, tiles)
        left = jnp.concatenate(left, axis=0) if len(left) > 1 else left[0]
        both = jnp.dot(
            left, frames[: tiles * LANE, :], preferred_element_type=jnp.float32
        )
        height = 0
        for section in group:
            size = blocks[section] * rows
            half = section % 2
            at = sum(blocks[:section]) * rows
            total_ref[at : at + size, :] += both[
                height : height + size, half * LANE : (half + 1) * LANE
            ]
            height += size

    def build_all(frames, chunk):
        for section in range(sections):
            build(frames[section // 2], section, chunk)

    def accumulate_all(frames, chunk):
        for group, part in zip(groups, frames):
            accumulate(part, group, chunk)

    build_all(even_refs, 0)
    accumulate_all(even_refs, 0)
    build_all(odd_refs, 1)

    def step(number, carry):
        accumulate_all(odd_refs, 2 * number - 1)
        build_all(even_refs, 2 * number)
        accumulate_all(even_refs, 2 * number)
        build_all(odd_refs, 2 * number + 1)
        return carry

    lax.fori_loop(1, chunks // 2, step, 0)
    accumulate_all(odd_refs, chunks - 1)
    for group, frames in zip(groups, even_refs):
        active = [section for section in group if blocks[section] > 1]
        for section in active:
            build(frames, section, chunks)
    for group, frames in zip(groups, even_refs):
        active = [section for section in group if blocks[section] > 1]
        if active:
            accumulate(frames, active, chunks, max(blocks[section] for section in active) - 1)
    place = 0
    for section in range(sections):
        for u in range(blocks[section]):
            at = (sum(blocks[:section]) + u) * rows
            out_ref[:, place : place + LANE] = total_ref[at : at + rows, :].astype(out_ref.dtype)
            place += LANE


def correlate(streams, basis_taps):
    sections, rows, taps = basis_taps.shape
    padded = -(-rows // SUB) * SUB
    if padded != rows:
        basis_taps = jnp.pad(basis_taps, ((0, 0), (0, padded - rows), (0, 0)))
    samples = sum(x.shape[0] - taps for x in streams)
    longest = max(x.shape[0] for x in streams)
    slot = -(-(longest + LANE) // (8 * LANE)) * 8
    lines = [x.reshape(-1, LANE) for x in streams]
    out = pl.pallas_call(
        correlate_kernel,
        out_shape=pltpu.VMEM((padded, samples), jnp.bfloat16),
        in_specs=[pl.BlockSpec(memory_space=pltpu.VMEM)] * (sections + 1),
        out_specs=pl.BlockSpec(memory_space=pltpu.VMEM),
        scratch_shapes=[
            pltpu.VMEM((sections * slot, LANE), jnp.float32),
            pltpu.VMEM((samples // LANE * padded, LANE), jnp.float32),
        ]
        + [pltpu.VMEM((CHUNK * LANE, 2 * LANE), jnp.bfloat16)] * 4,
        compiler_params=pltpu.CompilerParams(vmem_limit_bytes=60 * 2**20),
        cost_estimate=pl.CostEstimate(
            flops=2 * padded * taps * samples,
            bytes_accessed=2 * sections * padded * taps,
            transcendentals=0,
        ),
        name="correlate",
    )(*lines, basis_taps)
    return out[:rows]


def exchange(block, distance):
    size = lax.axis_size("tmpl")
    return lax.ppermute(block, "tmpl", [(i, i ^ distance) for i in range(size)])


def gather_blocks(block, ready):
    size = lax.axis_size("tmpl")
    if block.shape[0] % SUB:
        stride = 1
        while stride < size:
            radix = 4 if size // stride >= 4 else 2
            others = [exchange(block, step * stride) for step in range(1, radix)]
            block = jnp.concatenate([block] + others, axis=0)
            stride *= radix
        return [block], ready
    held = {0: block}
    for place in range(2, size, 2):
        high = 1 << (place.bit_length() - 1)
        held[place] = exchange(held[place ^ high and high], place ^ high or place)
    for place in range(1, size, 2):
        source = held[place ^ 1]
        if place == TIED:
            source, ready = lax.optimization_barrier((source, ready))
        held[place] = exchange(source, 1)
    return [held[place] for place in range(size)], ready


def maximum_over_group(values):
    size = lax.axis_size("tmpl")
    tiles = values.reshape(1, -1, LANE)
    copies = jnp.broadcast_to(tiles, (size,) + tiles.shape[1:])
    others = lax.all_to_all(copies, "tmpl", split_axis=0, concat_axis=0, tiled=True)
    return jnp.max(others, axis=0).reshape(values.shape)


def arrange_kernel(offset_ref, coeffs_ref, out_ref):
    bases = coeffs_ref.shape[2]
    source = lax.broadcasted_iota(jnp.int32, (bases, bases), 0)
    target = lax.broadcasted_iota(jnp.int32, (bases, bases), 1) ^ offset_ref[0]
    select = jnp.where(source == target, 1.0, 0.0).astype(jnp.bfloat16)
    for section in range(coeffs_ref.shape[0]):
        out_ref[section] = jnp.dot(
            coeffs_ref[section], select, preferred_element_type=jnp.float32
        ).astype(out_ref.dtype)


def arrange(coeffs, offset):
    return pl.pallas_call(
        arrange_kernel,
        out_shape=jax.ShapeDtypeStruct(coeffs.shape, coeffs.dtype),
        in_specs=[
            pl.BlockSpec(memory_space=pltpu.SMEM),
            pl.BlockSpec(memory_space=pltpu.VMEM),
        ],
        out_specs=pl.BlockSpec(memory_space=pltpu.VMEM),
        compiler_params=pltpu.CompilerParams(vmem_limit_bytes=16 * 2**20),
        cost_estimate=pl.CostEstimate(
            flops=2 * coeffs.size * coeffs.shape[2],
            bytes_accessed=4 * coeffs.size,
            transcendentals=0,
        ),
        name="arrange",
    )(offset, coeffs)


def recon_kernel(order, coeffs_ref, *refs):
    pieces = [refs[order.index(place)] for place in range(len(order))]
    snr_ref, peak_ref = refs[-2], refs[-1]
    samples = snr_ref.shape[1]
    source = lax.broadcasted_iota(jnp.int32, (2 * LANE, 2 * LANE), 0) % LANE
    target = lax.broadcasted_iota(jnp.int32, (2 * LANE, 2 * LANE), 1) // 2
    repeat = jnp.where(source == target, 1.0, 0.0).astype(jnp.bfloat16)
    running = None
    for section in (3, 2, 1, 0):
        width = samples >> section
        offset = sum(samples >> s for s in range(section))
        summed = []
        for place in range(0, width, 2 * LANE):
            size = min(2 * LANE, width)
            first = offset + place
            basis = jnp.concatenate([ref[:, first : first + size] for ref in pieces], axis=0)
            part = jnp.dot(coeffs_ref[section], basis, preferred_element_type=jnp.float32)
            if running is not None:
                coarse = running[place // (2 * LANE)]
                high = coarse.astype(jnp.bfloat16)
                low = (coarse - high.astype(jnp.float32)).astype(jnp.bfloat16)
                part = part + jnp.dot(
                    jnp.concatenate([high, low], axis=1),
                    repeat,
                    preferred_element_type=jnp.float32,
                )
            summed.append(part)
        running = []
        for part in summed:
            running += [part[:, at : at + LANE] for at in range(0, part.shape[1], LANE)]
        if section == 0:
            for number, part in enumerate(summed):
                place = number * 2 * LANE
                snr_ref[:, place : place + 2 * LANE] = part.astype(snr_ref.dtype)
                peak_ref[:, place : place + 2 * LANE] = jnp.max(
                    jnp.abs(part), axis=0, keepdims=True
                )


def reconstruct(coeffs, blocks, samples):
    order = HANDED if len(HANDED) == len(blocks) else tuple(range(len(blocks)))
    return pl.pallas_call(
        functools.partial(recon_kernel, order),
        out_shape=(
            jax.ShapeDtypeStruct((coeffs.shape[1], samples), jnp.bfloat16),
            jax.ShapeDtypeStruct((1, samples), jnp.float32),
        ),
        in_specs=[pl.BlockSpec(memory_space=pltpu.VMEM)] * (1 + len(blocks)),
        out_specs=(pl.BlockSpec(memory_space=pltpu.VMEM),) * 2,
        compiler_params=pltpu.CompilerParams(vmem_limit_bytes=16 * 2**20),
        name="reconstruct",
    )(coeffs, *[blocks[place] for place in order])


def per_device(strain_fast, strain_half, strain_quarter, strain_eighth, basis_taps, recon_coeffs):
    streams = (strain_fast, strain_half, strain_quarter, strain_eighth)
    samples = strain_fast.shape[0] - basis_taps.shape[2]
    offset = (lax.axis_index("tmpl") * basis_taps.shape[1]).astype(jnp.int32).reshape(1)
    coeffs = arrange(recon_coeffs, offset)
    blocks, coeffs = gather_blocks(correlate(streams, basis_taps), coeffs)
    snr_series, local_peak = reconstruct(coeffs, blocks, samples)
    peak_snr = maximum_over_group(local_peak.reshape(samples))
    return (snr_series, peak_snr)


def solution(mesh):
    in_specs = (P(), P(), P(), P(), P("bank", "tmpl", None), P("bank", "tmpl", None))
    out_specs = (P(("bank", "tmpl"), None), P("bank"))
    return jax.shard_map(
        per_device, mesh=mesh, in_specs=in_specs, out_specs=out_specs, check_vma=False
    )
```

```python
import functools

import jax
import jax.numpy as jnp
from jax import lax
from jax.experimental import pallas as pl
from jax.experimental.pallas import tpu as pltpu
from jax.sharding import PartitionSpec as P

LANE = 128
CHUNK = 16
SUB = 16
ROWS = 8
ROLLS = 4
TIED = 1
HANDED = (0, 1, 2, 3, 8, 9, 4, 5, 6, 7, 12, 13, 14, 15, 10, 11)
SUB = 16


def correlate_kernel(*refs):
    strains, source_ref, out_ref, taps_ref, sems = refs[:4], refs[4], refs[5], refs[6], refs[7]
    line_ref, total_ref, even_refs, odd_refs = refs[8], refs[9], refs[10:12], refs[12:14]
    sections = len(strains)
    copies = [
        pltpu.make_async_copy(source_ref.at[section], taps_ref.at[section], sems.at[section])
        for section in range(sections)
    ]
    for copy in copies:
        copy.start()
    rows, taps = taps_ref.shape[1], taps_ref.shape[2]
    lines = [ref.shape[0] for ref in strains]
    blocks = [count - taps // LANE for count in lines]
    slot = line_ref.shape[0] // sections
    span = CHUNK * LANE
    chunks = taps // span
    groups = ((0, 1), (2, 3))
    total_ref[...] = jnp.zeros(total_ref.shape, total_ref.dtype)

    extra = LANE // SUB - ROLLS
    source = lax.broadcasted_iota(jnp.int32, (2 * LANE, extra * LANE), 0)
    target = lax.broadcasted_iota(jnp.int32, (2 * LANE, extra * LANE), 1)
    target = target % LANE + (target // LANE + ROLLS) * SUB
    shifts = jnp.where(source == target, 1.0, 0.0).astype(jnp.bfloat16)

    for section, strain in enumerate(strains):
        first = section * slot
        line_ref[first : first + lines[section], :] = strain[...].astype(jnp.float32)
        line_ref[first + lines[section] : first + slot, :] = jnp.zeros(
            (slot - lines[section], LANE), jnp.float32
        )

    def build(frames, section, chunk, tiles=CHUNK):
        width = (tiles + 1) * LANE
        row = lax.broadcasted_iota(jnp.int32, (ROWS, width), 0)
        first = section * slot + chunk * CHUNK
        wide = jnp.concatenate(
            [
                jnp.broadcast_to(line_ref[pl.ds(first + number, 1), :], (ROWS, LANE))
                for number in range(tiles + 1)
            ],
            axis=1,
        )
        for step in (1, 2, 4):
            moved = pltpu.roll(wide, width - step, axis=1)
            wide = jnp.where((row & step) != 0, moved, wide)
        wide = jnp.concatenate([wide, pltpu.roll(wide, width - ROWS, axis=1)], axis=0)
        wide = wide.astype(jnp.bfloat16)
        moved = [wide]
        for q in range(1, ROLLS):
            moved.append(pltpu.roll(wide, width - SUB * q, axis=1))
        stacked = jnp.concatenate(
            [wide[:, number * LANE : (number + 2) * LANE] for number in range(tiles)], axis=0
        )
        rest = jnp.dot(stacked, shifts, preferred_element_type=jnp.float32).astype(wide.dtype)
        for number in range(tiles):
            pieces = [part[:, number * LANE : (number + 1) * LANE] for part in moved]
            pieces += [
                rest[number * SUB : (number + 1) * SUB, q * LANE : (q + 1) * LANE]
                for q in range(extra)
            ]
            half = section % 2
            frames[number * LANE : (number + 1) * LANE, half * LANE : (half + 1) * LANE] = (
                jnp.concatenate(pieces, axis=0)
            )

    def shifted(section, chunk, tiles):
        pieces = []
        for u in range(blocks[section]):
            first, size = (chunk * CHUNK - u) * LANE, tiles * LANE
            if not isinstance(first, int):
                pieces.append(taps_ref[section, :, pl.ds(pl.multiple_of(first, LANE), size)])
                continue
            parts = []
            if first < 0:
                parts.append(jnp.zeros((rows, -first), taps_ref.dtype))
            if first < taps:
                parts.append(taps_ref[section, :, max(first, 0) : min(first + size, taps)])
            if first + size > taps:
                parts.append(jnp.zeros((rows, first + size - max(first, taps)), taps_ref.dtype))
            pieces.append(jnp.concatenate(parts, axis=1) if len(parts) > 1 else parts[0])
        return pieces

    def accumulate(frames, group, chunk, tiles=CHUNK):
        left = []
        for section in group:
            left += shifted(section, chunk, tiles)
        left = jnp.concatenate(left, axis=0) if len(left) > 1 else left[0]
        both = jnp.dot(
            left, frames[: tiles * LANE, :], preferred_element_type=jnp.float32
        )
        height = 0
        for section in group:
            size = blocks[section] * rows
            half = section % 2
            at = sum(blocks[:section]) * rows
            total_ref[at : at + size, :] += both[
                height : height + size, half * LANE : (half + 1) * LANE
            ]
            height += size

    def build_all(frames, chunk):
        for section in range(sections):
            build(frames[section // 2], section, chunk)

    def accumulate_all(frames, chunk):
        for group, part in zip(groups, frames):
            accumulate(part, group, chunk)

    build_all(even_refs, 0)
    for copy in copies:
        copy.wait()
    accumulate_all(even_refs, 0)
    build_all(odd_refs, 1)

    def step(number, carry):
        accumulate_all(odd_refs, 2 * number - 1)
        build_all(even_refs, 2 * number)
        accumulate_all(even_refs, 2 * number)
        build_all(odd_refs, 2 * number + 1)
        return carry

    lax.fori_loop(1, chunks // 2, step, 0)
    accumulate_all(odd_refs, chunks - 1)
    for group, frames in zip(groups, even_refs):
        active = [section for section in group if blocks[section] > 1]
        if active:
            tiles = max(blocks[section] for section in active) - 1
            for section in active:
                build(frames, section, chunks, tiles)
            accumulate(frames, active, chunks, tiles)
    place = 0
    for section in range(sections):
        for u in range(blocks[section]):
            at = (sum(blocks[:section]) + u) * rows
            out_ref[:, place : place + LANE] = total_ref[at : at + rows, :].astype(out_ref.dtype)
            place += LANE


def correlate(streams, basis_taps):
    sections, rows, taps = basis_taps.shape
    padded = -(-rows // SUB) * SUB
    if padded != rows:
        basis_taps = jnp.pad(basis_taps, ((0, 0), (0, padded - rows), (0, 0)))
    samples = sum(x.shape[0] - taps for x in streams)
    longest = max(x.shape[0] for x in streams)
    slot = -(-(longest + LANE) // (8 * LANE)) * 8
    lines = [x.reshape(-1, LANE) for x in streams]
    out = pl.pallas_call(
        correlate_kernel,
        out_shape=pltpu.VMEM((padded, samples), jnp.bfloat16),
        in_specs=[pl.BlockSpec(memory_space=pltpu.VMEM)] * sections
        + [pl.BlockSpec(memory_space=pltpu.HBM)],
        out_specs=pl.BlockSpec(memory_space=pltpu.VMEM),
        scratch_shapes=[
            pltpu.VMEM((sections, padded, taps), jnp.bfloat16),
            pltpu.SemaphoreType.DMA((sections,)),
            pltpu.VMEM((sections * slot, LANE), jnp.float32),
            pltpu.VMEM((samples // LANE * padded, LANE), jnp.float32),
        ]
        + [pltpu.VMEM((CHUNK * LANE, 2 * LANE), jnp.bfloat16)] * 4,
        compiler_params=pltpu.CompilerParams(vmem_limit_bytes=60 * 2**20),
        cost_estimate=pl.CostEstimate(
            flops=2 * padded * taps * samples,
            bytes_accessed=2 * sections * padded * taps,
            transcendentals=0,
        ),
        name="correlate",
    )(*lines, basis_taps)
    return out[:rows]


def exchange(block, distance):
    size = lax.axis_size("tmpl")
    return lax.ppermute(block, "tmpl", [(i, i ^ distance) for i in range(size)])


def gather_blocks(block, ready):
    size = lax.axis_size("tmpl")
    if block.shape[0] % SUB:
        stride = 1
        while stride < size:
            radix = 4 if size // stride >= 4 else 2
            others = [exchange(block, step * stride) for step in range(1, radix)]
            block = jnp.concatenate([block] + others, axis=0)
            stride *= radix
        return [block], ready
    held = {0: block}
    for place in range(2, size, 2):
        high = 1 << (place.bit_length() - 1)
        held[place] = exchange(held[place ^ high and high], place ^ high or place)
    for place in range(1, size, 2):
        source = held[place ^ 1]
        if place == TIED:
            source, ready = lax.optimization_barrier((source, ready))
        held[place] = exchange(source, 1)
    return [held[place] for place in range(size)], ready


def maximum_over_group(values):
    size = lax.axis_size("tmpl")
    tiles = values.reshape(1, -1, LANE)
    copies = jnp.broadcast_to(tiles, (size,) + tiles.shape[1:])
    others = lax.all_to_all(copies, "tmpl", split_axis=0, concat_axis=0, tiled=True)
    return jnp.max(others, axis=0).reshape(values.shape)


def arrange_kernel(offset_ref, coeffs_ref, out_ref):
    bases = coeffs_ref.shape[2]
    source = lax.broadcasted_iota(jnp.int32, (bases, bases), 0)
    target = lax.broadcasted_iota(jnp.int32, (bases, bases), 1) ^ offset_ref[0]
    select = jnp.where(source == target, 1.0, 0.0).astype(jnp.bfloat16)
    for section in range(coeffs_ref.shape[0]):
        out_ref[section] = jnp.dot(
            coeffs_ref[section], select, preferred_element_type=jnp.float32
        ).astype(out_ref.dtype)


def arrange(coeffs, offset):
    return pl.pallas_call(
        arrange_kernel,
        out_shape=jax.ShapeDtypeStruct(coeffs.shape, coeffs.dtype),
        in_specs=[
            pl.BlockSpec(memory_space=pltpu.SMEM),
            pl.BlockSpec(memory_space=pltpu.VMEM),
        ],
        out_specs=pl.BlockSpec(memory_space=pltpu.VMEM),
        compiler_params=pltpu.CompilerParams(vmem_limit_bytes=16 * 2**20),
        cost_estimate=pl.CostEstimate(
            flops=2 * coeffs.size * coeffs.shape[2],
            bytes_accessed=4 * coeffs.size,
            transcendentals=0,
        ),
        name="arrange",
    )(offset, coeffs)


def recon_kernel(order, coeffs_ref, *refs):
    pieces = [refs[order.index(place)] for place in range(len(order))]
    snr_ref, peak_ref = refs[-2], refs[-1]
    samples = snr_ref.shape[1]
    source = lax.broadcasted_iota(jnp.int32, (2 * LANE, 2 * LANE), 0) % LANE
    target = lax.broadcasted_iota(jnp.int32, (2 * LANE, 2 * LANE), 1) // 2
    repeat = jnp.where(source == target, 1.0, 0.0).astype(jnp.bfloat16)
    running = None
    for section in (3, 2, 1, 0):
        width = samples >> section
        offset = sum(samples >> s for s in range(section))
        summed = []
        for place in range(0, width, 2 * LANE):
            size = min(2 * LANE, width)
            first = offset + place
            basis = jnp.concatenate([ref[:, first : first + size] for ref in pieces], axis=0)
            part = jnp.dot(coeffs_ref[section], basis, preferred_element_type=jnp.float32)
            if running is not None:
                coarse = running[place // (2 * LANE)]
                high = coarse.astype(jnp.bfloat16)
                low = (coarse - high.astype(jnp.float32)).astype(jnp.bfloat16)
                part = part + jnp.dot(
                    jnp.concatenate([high, low], axis=1),
                    repeat,
                    preferred_element_type=jnp.float32,
                )
            summed.append(part)
        running = []
        for part in summed:
            running += [part[:, at : at + LANE] for at in range(0, part.shape[1], LANE)]
        if section == 0:
            for number, part in enumerate(summed):
                place = number * 2 * LANE
                snr_ref[:, place : place + 2 * LANE] = part.astype(snr_ref.dtype)
                peak_ref[:, place : place + 2 * LANE] = jnp.max(
                    jnp.abs(part), axis=0, keepdims=True
                )


def reconstruct(coeffs, blocks, samples):
    order = HANDED if len(HANDED) == len(blocks) else tuple(range(len(blocks)))
    return pl.pallas_call(
        functools.partial(recon_kernel, order),
        out_shape=(
            jax.ShapeDtypeStruct((coeffs.shape[1], samples), jnp.bfloat16),
            jax.ShapeDtypeStruct((1, samples), jnp.float32),
        ),
        in_specs=[pl.BlockSpec(memory_space=pltpu.VMEM)] * (1 + len(blocks)),
        out_specs=(pl.BlockSpec(memory_space=pltpu.VMEM),) * 2,
        compiler_params=pltpu.CompilerParams(vmem_limit_bytes=16 * 2**20),
        name="reconstruct",
    )(coeffs, *[blocks[place] for place in order])


def per_device(strain_fast, strain_half, strain_quarter, strain_eighth, basis_taps, recon_coeffs):
    streams = (strain_fast, strain_half, strain_quarter, strain_eighth)
    samples = strain_fast.shape[0] - basis_taps.shape[2]
    offset = (lax.axis_index("tmpl") * basis_taps.shape[1]).astype(jnp.int32).reshape(1)
    coeffs = arrange(recon_coeffs, offset)
    blocks, coeffs = gather_blocks(correlate(streams, basis_taps), coeffs)
    snr_series, local_peak = reconstruct(coeffs, blocks, samples)
    peak_snr = maximum_over_group(local_peak.reshape(samples))
    return (snr_series, peak_snr)


def solution(mesh):
    in_specs = (P(), P(), P(), P(), P("bank", "tmpl", None), P("bank", "tmpl", None))
    out_specs = (P(("bank", "tmpl"), None), P("bank"))
    return jax.shard_map(
        per_device, mesh=mesh, in_specs=in_specs, out_specs=out_specs, check_vma=False
    )
```

```python
import functools

import jax
import jax.numpy as jnp
from jax import lax
from jax.experimental import pallas as pl
from jax.experimental.pallas import tpu as pltpu
from jax.sharding import PartitionSpec as P

LANE = 128
CHUNK = 32
SUB = 16
ROWS = 8
ROLLS = 4
TIED = 1
HANDED = (0, 1, 2, 3, 8, 9, 4, 5, 6, 7, 12, 13, 14, 15, 10, 11)
SUB = 16


def correlate_kernel(*refs):
    strains, source_ref, out_ref, taps_ref, sems = refs[:4], refs[4], refs[5], refs[6], refs[7]
    line_ref, total_ref, even_refs, odd_refs = refs[8], refs[9], refs[10:12], refs[12:14]
    sections = len(strains)
    copies = [
        pltpu.make_async_copy(source_ref.at[section], taps_ref.at[section], sems.at[section])
        for section in range(sections)
    ]
    for copy in copies:
        copy.start()
    rows, taps = taps_ref.shape[1], taps_ref.shape[2]
    lines = [ref.shape[0] for ref in strains]
    blocks = [count - taps // LANE for count in lines]
    slot = line_ref.shape[0] // sections
    span = CHUNK * LANE
    chunks = taps // span
    groups = ((0, 1), (2, 3))
    total_ref[...] = jnp.zeros(total_ref.shape, total_ref.dtype)

    extra = LANE // SUB - ROLLS
    source = lax.broadcasted_iota(jnp.int32, (2 * LANE, extra * LANE), 0)
    target = lax.broadcasted_iota(jnp.int32, (2 * LANE, extra * LANE), 1)
    target = target % LANE + (target // LANE + ROLLS) * SUB
    shifts = jnp.where(source == target, 1.0, 0.0).astype(jnp.bfloat16)

    for section, strain in enumerate(strains):
        first = section * slot
        line_ref[first : first + lines[section], :] = strain[...].astype(jnp.float32)
        line_ref[first + lines[section] : first + slot, :] = jnp.zeros(
            (slot - lines[section], LANE), jnp.float32
        )

    def build(frames, section, chunk, tiles=CHUNK):
        width = (tiles + 1) * LANE
        row = lax.broadcasted_iota(jnp.int32, (ROWS, width), 0)
        first = section * slot + chunk * CHUNK
        wide = jnp.concatenate(
            [
                jnp.broadcast_to(line_ref[pl.ds(first + number, 1), :], (ROWS, LANE))
                for number in range(tiles + 1)
            ],
            axis=1,
        )
        for step in (1, 2, 4):
            moved = pltpu.roll(wide, width - step, axis=1)
            wide = jnp.where((row & step) != 0, moved, wide)
        wide = jnp.concatenate([wide, pltpu.roll(wide, width - ROWS, axis=1)], axis=0)
        wide = wide.astype(jnp.bfloat16)
        moved = [wide]
        for q in range(1, ROLLS):
            moved.append(pltpu.roll(wide, width - SUB * q, axis=1))
        stacked = jnp.concatenate(
            [wide[:, number * LANE : (number + 2) * LANE] for number in range(tiles)], axis=0
        )
        rest = jnp.dot(stacked, shifts, preferred_element_type=jnp.float32).astype(wide.dtype)
        for number in range(tiles):
            pieces = [part[:, number * LANE : (number + 1) * LANE] for part in moved]
            pieces += [
                rest[number * SUB : (number + 1) * SUB, q * LANE : (q + 1) * LANE]
                for q in range(extra)
            ]
            half = section % 2
            frames[number * LANE : (number + 1) * LANE, half * LANE : (half + 1) * LANE] = (
                jnp.concatenate(pieces, axis=0)
            )

    def shifted(section, chunk, tiles):
        pieces = []
        for u in range(blocks[section]):
            first, size = (chunk * CHUNK - u) * LANE, tiles * LANE
            if not isinstance(first, int):
                pieces.append(taps_ref[section, :, pl.ds(pl.multiple_of(first, LANE), size)])
                continue
            parts = []
            if first < 0:
                parts.append(jnp.zeros((rows, -first), taps_ref.dtype))
            if first < taps:
                parts.append(taps_ref[section, :, max(first, 0) : min(first + size, taps)])
            if first + size > taps:
                parts.append(jnp.zeros((rows, first + size - max(first, taps)), taps_ref.dtype))
            pieces.append(jnp.concatenate(parts, axis=1) if len(parts) > 1 else parts[0])
        return pieces

    def accumulate(frames, group, chunk, tiles=CHUNK):
        left = []
        for section in group:
            left += shifted(section, chunk, tiles)
        left = jnp.concatenate(left, axis=0) if len(left) > 1 else left[0]
        both = jnp.dot(
            left, frames[: tiles * LANE, :], preferred_element_type=jnp.float32
        )
        height = 0
        for section in group:
            size = blocks[section] * rows
            half = section % 2
            at = sum(blocks[:section]) * rows
            total_ref[at : at + size, :] += both[
                height : height + size, half * LANE : (half + 1) * LANE
            ]
            height += size

    def build_all(frames, chunk):
        for section in range(sections):
            build(frames[section // 2], section, chunk)

    def accumulate_all(frames, chunk):
        for group, part in zip(groups, frames):
            accumulate(part, group, chunk)

    build_all(even_refs, 0)
    for copy in copies:
        copy.wait()
    accumulate_all(even_refs, 0)
    build_all(odd_refs, 1)

    def step(number, carry):
        accumulate_all(odd_refs, 2 * number - 1)
        build_all(even_refs, 2 * number)
        accumulate_all(even_refs, 2 * number)
        build_all(odd_refs, 2 * number + 1)
        return carry

    lax.fori_loop(1, chunks // 2, step, 0)
    accumulate_all(odd_refs, chunks - 1)
    for group, frames in zip(groups, even_refs):
        active = [section for section in group if blocks[section] > 1]
        if active:
            tiles = max(blocks[section] for section in active) - 1
            for section in active:
                build(frames, section, chunks, tiles)
            accumulate(frames, active, chunks, tiles)
    place = 0
    for section in range(sections):
        for u in range(blocks[section]):
            at = (sum(blocks[:section]) + u) * rows
            out_ref[:, place : place + LANE] = total_ref[at : at + rows, :].astype(out_ref.dtype)
            place += LANE


def correlate(streams, basis_taps):
    sections, rows, taps = basis_taps.shape
    padded = -(-rows // SUB) * SUB
    if padded != rows:
        basis_taps = jnp.pad(basis_taps, ((0, 0), (0, padded - rows), (0, 0)))
    samples = sum(x.shape[0] - taps for x in streams)
    longest = max(x.shape[0] for x in streams)
    slot = -(-(longest + LANE) // (8 * LANE)) * 8
    lines = [x.reshape(-1, LANE) for x in streams]
    out = pl.pallas_call(
        correlate_kernel,
        out_shape=pltpu.VMEM((padded, samples), jnp.bfloat16),
        in_specs=[pl.BlockSpec(memory_space=pltpu.VMEM)] * sections
        + [pl.BlockSpec(memory_space=pltpu.HBM)],
        out_specs=pl.BlockSpec(memory_space=pltpu.VMEM),
        scratch_shapes=[
            pltpu.VMEM((sections, padded, taps), jnp.bfloat16),
            pltpu.SemaphoreType.DMA((sections,)),
            pltpu.VMEM((sections * slot, LANE), jnp.float32),
            pltpu.VMEM((samples // LANE * padded, LANE), jnp.float32),
        ]
        + [pltpu.VMEM((CHUNK * LANE, 2 * LANE), jnp.bfloat16)] * 4,
        compiler_params=pltpu.CompilerParams(vmem_limit_bytes=60 * 2**20),
        cost_estimate=pl.CostEstimate(
            flops=2 * padded * taps * samples,
            bytes_accessed=2 * sections * padded * taps,
            transcendentals=0,
        ),
        name="correlate",
    )(*lines, basis_taps)
    return out[:rows]


def exchange(block, distance):
    size = lax.axis_size("tmpl")
    return lax.ppermute(block, "tmpl", [(i, i ^ distance) for i in range(size)])


def gather_blocks(block, ready):
    size = lax.axis_size("tmpl")
    if block.shape[0] % SUB:
        stride = 1
        while stride < size:
            radix = 4 if size // stride >= 4 else 2
            others = [exchange(block, step * stride) for step in range(1, radix)]
            block = jnp.concatenate([block] + others, axis=0)
            stride *= radix
        return [block], ready
    held = {0: block}
    for place in range(2, size, 2):
        high = 1 << (place.bit_length() - 1)
        held[place] = exchange(held[place ^ high and high], place ^ high or place)
    for place in range(1, size, 2):
        source = held[place ^ 1]
        if place == TIED:
            source, ready = lax.optimization_barrier((source, ready))
        held[place] = exchange(source, 1)
    return [held[place] for place in range(size)], ready


def maximum_over_group(values):
    size = lax.axis_size("tmpl")
    tiles = values.reshape(1, -1, LANE)
    copies = jnp.broadcast_to(tiles, (size,) + tiles.shape[1:])
    others = lax.all_to_all(copies, "tmpl", split_axis=0, concat_axis=0, tiled=True)
    return jnp.max(others, axis=0).reshape(values.shape)


def arrange_kernel(offset_ref, coeffs_ref, out_ref):
    bases = coeffs_ref.shape[2]
    source = lax.broadcasted_iota(jnp.int32, (bases, bases), 0)
    target = lax.broadcasted_iota(jnp.int32, (bases, bases), 1) ^ offset_ref[0]
    select = jnp.where(source == target, 1.0, 0.0).astype(jnp.bfloat16)
    for section in range(coeffs_ref.shape[0]):
        out_ref[section] = jnp.dot(
            coeffs_ref[section], select, preferred_element_type=jnp.float32
        ).astype(out_ref.dtype)


def arrange(coeffs, offset):
    return pl.pallas_call(
        arrange_kernel,
        out_shape=jax.ShapeDtypeStruct(coeffs.shape, coeffs.dtype),
        in_specs=[
            pl.BlockSpec(memory_space=pltpu.SMEM),
            pl.BlockSpec(memory_space=pltpu.VMEM),
        ],
        out_specs=pl.BlockSpec(memory_space=pltpu.VMEM),
        compiler_params=pltpu.CompilerParams(vmem_limit_bytes=16 * 2**20),
        cost_estimate=pl.CostEstimate(
            flops=2 * coeffs.size * coeffs.shape[2],
            bytes_accessed=4 * coeffs.size,
            transcendentals=0,
        ),
        name="arrange",
    )(offset, coeffs)


def recon_kernel(order, coeffs_ref, *refs):
    pieces = [refs[order.index(place)] for place in range(len(order))]
    out_ref, peak_ref, snr_ref, sems = refs[-4:]
    samples = snr_ref.shape[1]
    wide = 2 * LANE
    source = lax.broadcasted_iota(jnp.int32, (wide, wide), 0) % LANE
    target = lax.broadcasted_iota(jnp.int32, (wide, wide), 1) // 2
    repeat = jnp.where(source == target, 1.0, 0.0).astype(jnp.bfloat16)
    copies = []

    def total(section, place, size):
        first = sum(samples >> s for s in range(section)) + place
        basis = jnp.concatenate([ref[:, first : first + size] for ref in pieces], axis=0)
        part = jnp.dot(coeffs_ref[section], basis, preferred_element_type=jnp.float32)
        if section == 3:
            return part
        coarse = held[section + 1][place // wide]
        high = coarse.astype(jnp.bfloat16)
        low = (coarse - high.astype(jnp.float32)).astype(jnp.bfloat16)
        return part + jnp.dot(
            jnp.concatenate([high, low], axis=1), repeat, preferred_element_type=jnp.float32
        )

    held = {section: [] for section in range(4)}

    def extend(section):
        place = len(held[section]) * LANE
        size = min(wide, samples >> section)
        if section < 3 and len(held[section + 1]) <= place // wide:
            extend(section + 1)
        part = total(section, place, size)
        held[section] += [part[:, at : at + LANE] for at in range(0, size, LANE)]
        if section == 0:
            snr_ref[:, place : place + size] = part.astype(snr_ref.dtype)
            copy = pltpu.make_async_copy(
                snr_ref.at[:, pl.ds(place, size)],
                out_ref.at[:, pl.ds(place, size)],
                sems.at[place // wide],
            )
            copy.start()
            copies.append(copy)
            peak_ref[:, place : place + size] = jnp.max(jnp.abs(part), axis=0, keepdims=True)

    while len(held[0]) * LANE < samples:
        extend(0)
    for copy in copies:
        copy.wait()


def reconstruct(coeffs, blocks, samples):
    order = HANDED if len(HANDED) == len(blocks) else tuple(range(len(blocks)))
    return pl.pallas_call(
        functools.partial(recon_kernel, order),
        out_shape=(
            jax.ShapeDtypeStruct((coeffs.shape[1], samples), jnp.bfloat16),
            jax.ShapeDtypeStruct((1, samples), jnp.float32),
        ),
        in_specs=[pl.BlockSpec(memory_space=pltpu.VMEM)] * (1 + len(blocks)),
        out_specs=(
            pl.BlockSpec(memory_space=pltpu.HBM),
            pl.BlockSpec(memory_space=pltpu.VMEM),
        ),
        scratch_shapes=[
            pltpu.VMEM((coeffs.shape[1], samples), jnp.bfloat16),
            pltpu.SemaphoreType.DMA((samples // (2 * LANE),)),
        ],
        compiler_params=pltpu.CompilerParams(vmem_limit_bytes=16 * 2**20),
        name="reconstruct",
    )(coeffs, *[blocks[place] for place in order])


def per_device(strain_fast, strain_half, strain_quarter, strain_eighth, basis_taps, recon_coeffs):
    streams = (strain_fast, strain_half, strain_quarter, strain_eighth)
    samples = strain_fast.shape[0] - basis_taps.shape[2]
    offset = (lax.axis_index("tmpl") * basis_taps.shape[1]).astype(jnp.int32).reshape(1)
    coeffs = arrange(recon_coeffs, offset)
    blocks, coeffs = gather_blocks(correlate(streams, basis_taps), coeffs)
    snr_series, local_peak = reconstruct(coeffs, blocks, samples)
    peak_snr = maximum_over_group(local_peak.reshape(samples))
    return (snr_series, peak_snr)


def solution(mesh):
    in_specs = (P(), P(), P(), P(), P("bank", "tmpl", None), P("bank", "tmpl", None))
    out_specs = (P(("bank", "tmpl"), None), P("bank"))
    return jax.shard_map(
        per_device, mesh=mesh, in_specs=in_specs, out_specs=out_specs, check_vma=False
    )
```

```python
import functools

import jax
import jax.numpy as jnp
from jax import lax
from jax.experimental import pallas as pl
from jax.experimental.pallas import tpu as pltpu
from jax.sharding import PartitionSpec as P

LANE = 128
CHUNK = 32
SUB = 16
ROWS = 8
TIED = 1
HANDED = (0, 1, 2, 3, 8, 9, 4, 5, 6, 7, 12, 13, 14, 15, 10, 11)
SUB = 16


def correlate_kernel(*refs):
    strains, source_ref, out_ref, taps_ref, sems = refs[:4], refs[4], refs[5], refs[6], refs[7]
    line_ref, total_ref, even_refs, odd_refs = refs[8], refs[9], refs[10:12], refs[12:14]
    sections = len(strains)
    copies = [
        pltpu.make_async_copy(source_ref.at[section], taps_ref.at[section], sems.at[section])
        for section in range(sections)
    ]
    for copy in copies:
        copy.start()
    rows, taps = taps_ref.shape[1], taps_ref.shape[2]
    lines = [ref.shape[0] for ref in strains]
    blocks = [count - taps // LANE for count in lines]
    slot = line_ref.shape[0] // sections
    span = CHUNK * LANE
    chunks = taps // span
    groups = ((0, 1), (2, 3))
    total_ref[...] = jnp.zeros(total_ref.shape, total_ref.dtype)

    for section, strain in enumerate(strains):
        first = section * slot
        line_ref[first : first + lines[section], :] = strain[...].astype(jnp.float32)
        line_ref[first + lines[section] : first + slot, :] = jnp.zeros(
            (slot - lines[section], LANE), jnp.float32
        )

    def build(frames, section, chunk, tiles=CHUNK):
        width = (tiles + 1) * LANE
        row = lax.broadcasted_iota(jnp.int32, (ROWS, width), 0)
        first = section * slot + chunk * CHUNK
        wide = jnp.concatenate(
            [
                jnp.broadcast_to(line_ref[pl.ds(first + number, 1), :], (ROWS, LANE))
                for number in range(tiles + 1)
            ],
            axis=1,
        )
        for step in (1, 2, 4):
            moved = pltpu.roll(wide, width - step, axis=1)
            wide = jnp.where((row & step) != 0, moved, wide)
        wide = jnp.concatenate([wide, pltpu.roll(wide, width - ROWS, axis=1)], axis=0)
        wide = wide.astype(jnp.bfloat16)
        moved = [wide]
        for q in range(1, LANE // SUB):
            moved.append(pltpu.roll(wide, width - SUB * q, axis=1))
        for number in range(tiles):
            pieces = [part[:, number * LANE : (number + 1) * LANE] for part in moved]
            half = section % 2
            frames[number * LANE : (number + 1) * LANE, half * LANE : (half + 1) * LANE] = (
                jnp.concatenate(pieces, axis=0)
            )

    def shifted(section, chunk, tiles):
        pieces = []
        for u in range(blocks[section]):
            first, size = (chunk * CHUNK - u) * LANE, tiles * LANE
            if not isinstance(first, int):
                pieces.append(taps_ref[section, :, pl.ds(pl.multiple_of(first, LANE), size)])
                continue
            parts = []
            if first < 0:
                parts.append(jnp.zeros((rows, -first), taps_ref.dtype))
            if first < taps:
                parts.append(taps_ref[section, :, max(first, 0) : min(first + size, taps)])
            if first + size > taps:
                parts.append(jnp.zeros((rows, first + size - max(first, taps)), taps_ref.dtype))
            pieces.append(jnp.concatenate(parts, axis=1) if len(parts) > 1 else parts[0])
        return pieces

    def accumulate(frames, group, chunk, tiles=CHUNK):
        left = []
        for section in group:
            left += shifted(section, chunk, tiles)
        left = jnp.concatenate(left, axis=0) if len(left) > 1 else left[0]
        both = jnp.dot(
            left, frames[: tiles * LANE, :], preferred_element_type=jnp.float32
        )
        height = 0
        for section in group:
            size = blocks[section] * rows
            half = section % 2
            at = sum(blocks[:section]) * rows
            total_ref[at : at + size, :] += both[
                height : height + size, half * LANE : (half + 1) * LANE
            ]
            height += size

    def build_all(frames, chunk):
        for section in range(sections):
            build(frames[section // 2], section, chunk)

    def accumulate_all(frames, chunk):
        for group, part in zip(groups, frames):
            accumulate(part, group, chunk)

    build_all(even_refs, 0)
    for copy in copies:
        copy.wait()
    accumulate_all(even_refs, 0)
    build_all(odd_refs, 1)

    def step(number, carry):
        accumulate_all(odd_refs, 2 * number - 1)
        build_all(even_refs, 2 * number)
        accumulate_all(even_refs, 2 * number)
        build_all(odd_refs, 2 * number + 1)
        return carry

    lax.fori_loop(1, chunks // 2, step, 0)
    accumulate_all(odd_refs, chunks - 1)
    for group, frames in zip(groups, even_refs):
        active = [section for section in group if blocks[section] > 1]
        if active:
            tiles = max(blocks[section] for section in active) - 1
            for section in active:
                build(frames, section, chunks, tiles)
            accumulate(frames, active, chunks, tiles)
    place = 0
    for section in range(sections):
        for u in range(blocks[section]):
            at = (sum(blocks[:section]) + u) * rows
            out_ref[:, place : place + LANE] = total_ref[at : at + rows, :].astype(out_ref.dtype)
            place += LANE


def correlate(streams, basis_taps):
    sections, rows, taps = basis_taps.shape
    padded = -(-rows // SUB) * SUB
    if padded != rows:
        basis_taps = jnp.pad(basis_taps, ((0, 0), (0, padded - rows), (0, 0)))
    samples = sum(x.shape[0] - taps for x in streams)
    longest = max(x.shape[0] for x in streams)
    slot = -(-(longest + LANE) // (8 * LANE)) * 8
    lines = [x.reshape(-1, LANE) for x in streams]
    out = pl.pallas_call(
        correlate_kernel,
        out_shape=pltpu.VMEM((padded, samples), jnp.bfloat16),
        in_specs=[pl.BlockSpec(memory_space=pltpu.VMEM)] * sections
        + [pl.BlockSpec(memory_space=pltpu.HBM)],
        out_specs=pl.BlockSpec(memory_space=pltpu.VMEM),
        scratch_shapes=[
            pltpu.VMEM((sections, padded, taps), jnp.bfloat16),
            pltpu.SemaphoreType.DMA((sections,)),
            pltpu.VMEM((sections * slot, LANE), jnp.float32),
            pltpu.VMEM((samples // LANE * padded, LANE), jnp.float32),
        ]
        + [pltpu.VMEM((CHUNK * LANE, 2 * LANE), jnp.bfloat16)] * 4,
        compiler_params=pltpu.CompilerParams(vmem_limit_bytes=60 * 2**20),
        cost_estimate=pl.CostEstimate(
            flops=2 * padded * taps * samples,
            bytes_accessed=2 * sections * padded * taps,
            transcendentals=0,
        ),
        name="correlate",
    )(*lines, basis_taps)
    return out[:rows]


def exchange(block, distance):
    size = lax.axis_size("tmpl")
    return lax.ppermute(block, "tmpl", [(i, i ^ distance) for i in range(size)])


def gather_blocks(block, ready):
    size = lax.axis_size("tmpl")
    if block.shape[0] % SUB:
        stride = 1
        while stride < size:
            radix = 4 if size // stride >= 4 else 2
            others = [exchange(block, step * stride) for step in range(1, radix)]
            block = jnp.concatenate([block] + others, axis=0)
            stride *= radix
        return [block], ready
    held = {0: block}
    for place in range(2, size, 2):
        high = 1 << (place.bit_length() - 1)
        held[place] = exchange(held[place ^ high and high], place ^ high or place)
    for place in range(1, size, 2):
        source = held[place ^ 1]
        if place == TIED:
            source, ready = lax.optimization_barrier((source, ready))
        held[place] = exchange(source, 1)
    return [held[place] for place in range(size)], ready


def maximum_over_group(values):
    size = lax.axis_size("tmpl")
    tiles = values.reshape(1, -1, LANE)
    copies = jnp.broadcast_to(tiles, (size,) + tiles.shape[1:])
    others = lax.all_to_all(copies, "tmpl", split_axis=0, concat_axis=0, tiled=True)
    return jnp.max(others, axis=0).reshape(values.shape)


def arrange_kernel(offset_ref, coeffs_ref, out_ref):
    bases = coeffs_ref.shape[2]
    source = lax.broadcasted_iota(jnp.int32, (bases, bases), 0)
    target = lax.broadcasted_iota(jnp.int32, (bases, bases), 1) ^ offset_ref[0]
    select = jnp.where(source == target, 1.0, 0.0).astype(jnp.bfloat16)
    for section in range(coeffs_ref.shape[0]):
        out_ref[section] = jnp.dot(
            coeffs_ref[section], select, preferred_element_type=jnp.float32
        ).astype(out_ref.dtype)


def arrange(coeffs, offset):
    return pl.pallas_call(
        arrange_kernel,
        out_shape=jax.ShapeDtypeStruct(coeffs.shape, coeffs.dtype),
        in_specs=[
            pl.BlockSpec(memory_space=pltpu.SMEM),
            pl.BlockSpec(memory_space=pltpu.VMEM),
        ],
        out_specs=pl.BlockSpec(memory_space=pltpu.VMEM),
        compiler_params=pltpu.CompilerParams(vmem_limit_bytes=16 * 2**20),
        cost_estimate=pl.CostEstimate(
            flops=2 * coeffs.size * coeffs.shape[2],
            bytes_accessed=4 * coeffs.size,
            transcendentals=0,
        ),
        name="arrange",
    )(offset, coeffs)


def recon_kernel(order, coeffs_ref, *refs):
    pieces = [refs[order.index(place)] for place in range(len(order))]
    snr_ref, peak_ref = refs[-2], refs[-1]
    samples = snr_ref.shape[1]
    source = lax.broadcasted_iota(jnp.int32, (2 * LANE, 2 * LANE), 0) % LANE
    target = lax.broadcasted_iota(jnp.int32, (2 * LANE, 2 * LANE), 1) // 2
    repeat = jnp.where(source == target, 1.0, 0.0).astype(jnp.bfloat16)
    running = None
    for section in (3, 2, 1, 0):
        width = samples >> section
        offset = sum(samples >> s for s in range(section))
        summed = []
        for place in range(0, width, 2 * LANE):
            size = min(2 * LANE, width)
            first = offset + place
            basis = jnp.concatenate([ref[:, first : first + size] for ref in pieces], axis=0)
            part = jnp.dot(coeffs_ref[section], basis, preferred_element_type=jnp.float32)
            if running is not None:
                coarse = running[place // (2 * LANE)]
                high = coarse.astype(jnp.bfloat16)
                low = (coarse - high.astype(jnp.float32)).astype(jnp.bfloat16)
                part = part + jnp.dot(
                    jnp.concatenate([high, low], axis=1),
                    repeat,
                    preferred_element_type=jnp.float32,
                )
            summed.append(part)
        running = []
        for part in summed:
            running += [part[:, at : at + LANE] for at in range(0, part.shape[1], LANE)]
        if section == 0:
            for number, part in enumerate(summed):
                place = number * 2 * LANE
                snr_ref[:, place : place + 2 * LANE] = part.astype(snr_ref.dtype)
                peak_ref[:, place : place + 2 * LANE] = jnp.max(
                    jnp.abs(part), axis=0, keepdims=True
                )


def reconstruct(coeffs, blocks, samples):
    order = HANDED if len(HANDED) == len(blocks) else tuple(range(len(blocks)))
    return pl.pallas_call(
        functools.partial(recon_kernel, order),
        out_shape=(
            jax.ShapeDtypeStruct((coeffs.shape[1], samples), jnp.bfloat16),
            jax.ShapeDtypeStruct((1, samples), jnp.float32),
        ),
        in_specs=[pl.BlockSpec(memory_space=pltpu.VMEM)] * (1 + len(blocks)),
        out_specs=(pl.BlockSpec(memory_space=pltpu.VMEM),) * 2,
        compiler_params=pltpu.CompilerParams(vmem_limit_bytes=16 * 2**20),
        name="reconstruct",
    )(coeffs, *[blocks[place] for place in order])


def per_device(strain_fast, strain_half, strain_quarter, strain_eighth, basis_taps, recon_coeffs):
    streams = (strain_fast, strain_half, strain_quarter, strain_eighth)
    samples = strain_fast.shape[0] - basis_taps.shape[2]
    offset = (lax.axis_index("tmpl") * basis_taps.shape[1]).astype(jnp.int32).reshape(1)
    coeffs = arrange(recon_coeffs, offset)
    blocks, coeffs = gather_blocks(correlate(streams, basis_taps), coeffs)
    snr_series, local_peak = reconstruct(coeffs, blocks, samples)
    peak_snr = maximum_over_group(local_peak.reshape(samples))
    return (snr_series, peak_snr)


def solution(mesh):
    in_specs = (P(), P(), P(), P(), P("bank", "tmpl", None), P("bank", "tmpl", None))
    out_specs = (P(("bank", "tmpl"), None), P("bank"))
    return jax.shard_map(
        per_device, mesh=mesh, in_specs=in_specs, out_specs=out_specs, check_vma=False
    )
```

```python
import functools

import jax
import jax.numpy as jnp
from jax import lax
from jax.experimental import pallas as pl
from jax.experimental.pallas import tpu as pltpu
from jax.sharding import PartitionSpec as P

LANE = 128
CHUNK = 32
SUB = 16
ROWS = 8
ROLLS = 2
TIED = 1
HANDED = (0, 1, 2, 3, 8, 9, 4, 5, 6, 7, 12, 13, 14, 15, 10, 11)
SUB = 16


def correlate_kernel(*refs):
    strains, source_ref, out_ref, taps_ref, sems = refs[:4], refs[4], refs[5], refs[6], refs[7]
    line_ref, total_ref, even_refs, odd_refs = refs[8], refs[9], refs[10:12], refs[12:14]
    sections = len(strains)
    copies = [
        pltpu.make_async_copy(source_ref.at[section], taps_ref.at[section], sems.at[section])
        for section in range(sections)
    ]
    for copy in copies:
        copy.start()
    rows, taps = taps_ref.shape[1], taps_ref.shape[2]
    lines = [ref.shape[0] for ref in strains]
    blocks = [count - taps // LANE for count in lines]
    slot = line_ref.shape[0] // sections
    span = CHUNK * LANE
    chunks = taps // span
    groups = ((0, 1), (2, 3))
    total_ref[...] = jnp.zeros(total_ref.shape, total_ref.dtype)

    extra = LANE // SUB - ROLLS
    source = lax.broadcasted_iota(jnp.int32, (2 * LANE, extra * LANE), 0)
    target = lax.broadcasted_iota(jnp.int32, (2 * LANE, extra * LANE), 1)
    target = target % LANE + (target // LANE + ROLLS) * SUB
    shifts = jnp.where(source == target, 1.0, 0.0).astype(jnp.bfloat16)

    for section, strain in enumerate(strains):
        first = section * slot
        line_ref[first : first + lines[section], :] = strain[...].astype(jnp.float32)
        line_ref[first + lines[section] : first + slot, :] = jnp.zeros(
            (slot - lines[section], LANE), jnp.float32
        )

    def build(frames, section, chunk, tiles=CHUNK):
        width = (tiles + 1) * LANE
        row = lax.broadcasted_iota(jnp.int32, (ROWS, width), 0)
        first = section * slot + chunk * CHUNK
        wide = jnp.concatenate(
            [
                jnp.broadcast_to(line_ref[pl.ds(first + number, 1), :], (ROWS, LANE))
                for number in range(tiles + 1)
            ],
            axis=1,
        )
        for step in (1, 2, 4):
            moved = pltpu.roll(wide, width - step, axis=1)
            wide = jnp.where((row & step) != 0, moved, wide)
        wide = jnp.concatenate([wide, pltpu.roll(wide, width - ROWS, axis=1)], axis=0)
        wide = wide.astype(jnp.bfloat16)
        moved = [wide]
        for q in range(1, ROLLS):
            moved.append(pltpu.roll(wide, width - SUB * q, axis=1))
        stacked = jnp.concatenate(
            [wide[:, number * LANE : (number + 2) * LANE] for number in range(tiles)], axis=0
        )
        rest = jnp.dot(stacked, shifts, preferred_element_type=jnp.float32).astype(wide.dtype)
        for number in range(tiles):
            pieces = [part[:, number * LANE : (number + 1) * LANE] for part in moved]
            pieces += [
                rest[number * SUB : (number + 1) * SUB, q * LANE : (q + 1) * LANE]
                for q in range(extra)
            ]
            half = section % 2
            frames[number * LANE : (number + 1) * LANE, half * LANE : (half + 1) * LANE] = (
                jnp.concatenate(pieces, axis=0)
            )

    def shifted(section, chunk, tiles):
        pieces = []
        for u in range(blocks[section]):
            first, size = (chunk * CHUNK - u) * LANE, tiles * LANE
            if not isinstance(first, int):
                pieces.append(taps_ref[section, :, pl.ds(pl.multiple_of(first, LANE), size)])
                continue
            parts = []
            if first < 0:
                parts.append(jnp.zeros((rows, -first), taps_ref.dtype))
            if first < taps:
                parts.append(taps_ref[section, :, max(first, 0) : min(first + size, taps)])
            if first + size > taps:
                parts.append(jnp.zeros((rows, first + size - max(first, taps)), taps_ref.dtype))
            pieces.append(jnp.concatenate(parts, axis=1) if len(parts) > 1 else parts[0])
        return pieces

    def accumulate(frames, group, chunk, tiles=CHUNK):
        left = []
        for section in group:
            left += shifted(section, chunk, tiles)
        left = jnp.concatenate(left, axis=0) if len(left) > 1 else left[0]
        both = jnp.dot(
            left, frames[: tiles * LANE, :], preferred_element_type=jnp.float32
        )
        height = 0
        for section in group:
            size = blocks[section] * rows
            half = section % 2
            at = sum(blocks[:section]) * rows
            total_ref[at : at + size, :] += both[
                height : height + size, half * LANE : (half + 1) * LANE
            ]
            height += size

    def build_all(frames, chunk):
        for section in range(sections):
            build(frames[section // 2], section, chunk)

    def accumulate_all(frames, chunk):
        for group, part in zip(groups, frames):
            accumulate(part, group, chunk)

    build_all(even_refs, 0)
    for copy in copies:
        copy.wait()
    accumulate_all(even_refs, 0)
    build_all(odd_refs, 1)

    def step(number, carry):
        accumulate_all(odd_refs, 2 * number - 1)
        build_all(even_refs, 2 * number)
        accumulate_all(even_refs, 2 * number)
        build_all(odd_refs, 2 * number + 1)
        return carry

    lax.fori_loop(1, chunks // 2, step, 0)
    accumulate_all(odd_refs, chunks - 1)
    for group, frames in zip(groups, even_refs):
        active = [section for section in group if blocks[section] > 1]
        if active:
            tiles = max(blocks[section] for section in active) - 1
            for section in active:
                build(frames, section, chunks, tiles)
            accumulate(frames, active, chunks, tiles)
    place = 0
    for section in range(sections):
        for u in range(blocks[section]):
            at = (sum(blocks[:section]) + u) * rows
            out_ref[:, place : place + LANE] = total_ref[at : at + rows, :].astype(out_ref.dtype)
            place += LANE


def correlate(streams, basis_taps):
    sections, rows, taps = basis_taps.shape
    padded = -(-rows // SUB) * SUB
    if padded != rows:
        basis_taps = jnp.pad(basis_taps, ((0, 0), (0, padded - rows), (0, 0)))
    samples = sum(x.shape[0] - taps for x in streams)
    longest = max(x.shape[0] for x in streams)
    slot = -(-(longest + LANE) // (8 * LANE)) * 8
    lines = [x.reshape(-1, LANE) for x in streams]
    out = pl.pallas_call(
        correlate_kernel,
        out_shape=pltpu.VMEM((padded, samples), jnp.bfloat16),
        in_specs=[pl.BlockSpec(memory_space=pltpu.VMEM)] * sections
        + [pl.BlockSpec(memory_space=pltpu.HBM)],
        out_specs=pl.BlockSpec(memory_space=pltpu.VMEM),
        scratch_shapes=[
            pltpu.VMEM((sections, padded, taps), jnp.bfloat16),
            pltpu.SemaphoreType.DMA((sections,)),
            pltpu.VMEM((sections * slot, LANE), jnp.float32),
            pltpu.VMEM((samples // LANE * padded, LANE), jnp.float32),
        ]
        + [pltpu.VMEM((CHUNK * LANE, 2 * LANE), jnp.bfloat16)] * 4,
        compiler_params=pltpu.CompilerParams(vmem_limit_bytes=60 * 2**20),
        cost_estimate=pl.CostEstimate(
            flops=2 * padded * taps * samples,
            bytes_accessed=2 * sections * padded * taps,
            transcendentals=0,
        ),
        name="correlate",
    )(*lines, basis_taps)
    return out[:rows]


def exchange(block, distance):
    size = lax.axis_size("tmpl")
    return lax.ppermute(block, "tmpl", [(i, i ^ distance) for i in range(size)])


def gather_blocks(block, ready):
    size = lax.axis_size("tmpl")
    if block.shape[0] % SUB:
        stride = 1
        while stride < size:
            radix = 4 if size // stride >= 4 else 2
            others = [exchange(block, step * stride) for step in range(1, radix)]
            block = jnp.concatenate([block] + others, axis=0)
            stride *= radix
        return [block], ready
    held = {0: block}
    for place in range(2, size, 2):
        high = 1 << (place.bit_length() - 1)
        held[place] = exchange(held[place ^ high and high], place ^ high or place)
    for place in range(1, size, 2):
        source = held[place ^ 1]
        if place == TIED:
            source, ready = lax.optimization_barrier((source, ready))
        held[place] = exchange(source, 1)
    return [held[place] for place in range(size)], ready


def maximum_over_group(values):
    size = lax.axis_size("tmpl")
    tiles = values.reshape(1, -1, LANE)
    copies = jnp.broadcast_to(tiles, (size,) + tiles.shape[1:])
    others = lax.all_to_all(copies, "tmpl", split_axis=0, concat_axis=0, tiled=True)
    return jnp.max(others, axis=0).reshape(values.shape)


def arrange_kernel(offset_ref, coeffs_ref, out_ref):
    bases = coeffs_ref.shape[2]
    source = lax.broadcasted_iota(jnp.int32, (bases, bases), 0)
    target = lax.broadcasted_iota(jnp.int32, (bases, bases), 1) ^ offset_ref[0]
    select = jnp.where(source == target, 1.0, 0.0).astype(jnp.bfloat16)
    for section in range(coeffs_ref.shape[0]):
        out_ref[section] = jnp.dot(
            coeffs_ref[section], select, preferred_element_type=jnp.float32
        ).astype(out_ref.dtype)


def arrange(coeffs, offset):
    return pl.pallas_call(
        arrange_kernel,
        out_shape=jax.ShapeDtypeStruct(coeffs.shape, coeffs.dtype),
        in_specs=[
            pl.BlockSpec(memory_space=pltpu.SMEM),
            pl.BlockSpec(memory_space=pltpu.VMEM),
        ],
        out_specs=pl.BlockSpec(memory_space=pltpu.VMEM),
        compiler_params=pltpu.CompilerParams(vmem_limit_bytes=16 * 2**20),
        cost_estimate=pl.CostEstimate(
            flops=2 * coeffs.size * coeffs.shape[2],
            bytes_accessed=4 * coeffs.size,
            transcendentals=0,
        ),
        name="arrange",
    )(offset, coeffs)


def recon_kernel(order, coeffs_ref, *refs):
    pieces = [refs[order.index(place)] for place in range(len(order))]
    snr_ref, peak_ref = refs[-2], refs[-1]
    samples = snr_ref.shape[1]
    source = lax.broadcasted_iota(jnp.int32, (2 * LANE, 2 * LANE), 0) % LANE
    target = lax.broadcasted_iota(jnp.int32, (2 * LANE, 2 * LANE), 1) // 2
    repeat = jnp.where(source == target, 1.0, 0.0).astype(jnp.bfloat16)
    running = None
    for section in (3, 2, 1, 0):
        width = samples >> section
        offset = sum(samples >> s for s in range(section))
        summed = []
        for place in range(0, width, 2 * LANE):
            size = min(2 * LANE, width)
            first = offset + place
            basis = jnp.concatenate([ref[:, first : first + size] for ref in pieces], axis=0)
            part = jnp.dot(coeffs_ref[section], basis, preferred_element_type=jnp.float32)
            if running is not None:
                coarse = running[place // (2 * LANE)]
                high = coarse.astype(jnp.bfloat16)
                low = (coarse - high.astype(jnp.float32)).astype(jnp.bfloat16)
                part = part + jnp.dot(
                    jnp.concatenate([high, low], axis=1),
                    repeat,
                    preferred_element_type=jnp.float32,
                )
            summed.append(part)
        running = []
        for part in summed:
            running += [part[:, at : at + LANE] for at in range(0, part.shape[1], LANE)]
        if section == 0:
            for number, part in enumerate(summed):
                place = number * 2 * LANE
                snr_ref[:, place : place + 2 * LANE] = part.astype(snr_ref.dtype)
                peak_ref[:, place : place + 2 * LANE] = jnp.max(
                    jnp.abs(part), axis=0, keepdims=True
                )


def reconstruct(coeffs, blocks, samples):
    order = HANDED if len(HANDED) == len(blocks) else tuple(range(len(blocks)))
    return pl.pallas_call(
        functools.partial(recon_kernel, order),
        out_shape=(
            jax.ShapeDtypeStruct((coeffs.shape[1], samples), jnp.bfloat16),
            jax.ShapeDtypeStruct((1, samples), jnp.float32),
        ),
        in_specs=[pl.BlockSpec(memory_space=pltpu.VMEM)] * (1 + len(blocks)),
        out_specs=(pl.BlockSpec(memory_space=pltpu.VMEM),) * 2,
        compiler_params=pltpu.CompilerParams(vmem_limit_bytes=16 * 2**20),
        name="reconstruct",
    )(coeffs, *[blocks[place] for place in order])


def per_device(strain_fast, strain_half, strain_quarter, strain_eighth, basis_taps, recon_coeffs):
    streams = (strain_fast, strain_half, strain_quarter, strain_eighth)
    samples = strain_fast.shape[0] - basis_taps.shape[2]
    offset = (lax.axis_index("tmpl") * basis_taps.shape[1]).astype(jnp.int32).reshape(1)
    coeffs = arrange(recon_coeffs, offset)
    blocks, coeffs = gather_blocks(correlate(streams, basis_taps), coeffs)
    snr_series, local_peak = reconstruct(coeffs, blocks, samples)
    peak_snr = maximum_over_group(local_peak.reshape(samples))
    return (snr_series, peak_snr)


def solution(mesh):
    in_specs = (P(), P(), P(), P(), P("bank", "tmpl", None), P("bank", "tmpl", None))
    out_specs = (P(("bank", "tmpl"), None), P("bank"))
    return jax.shard_map(
        per_device, mesh=mesh, in_specs=in_specs, out_specs=out_specs, check_vma=False
    )
```

```python
import functools

import jax
import jax.numpy as jnp
from jax import lax
from jax.experimental import pallas as pl
from jax.experimental.pallas import tpu as pltpu
from jax.sharding import PartitionSpec as P

LANE = 128
CHUNK = 32
SUB = 16
ROWS = 8
ROLLS = 4
TIED = 1
HANDED = (0, 1, 2, 3, 8, 9, 4, 5, 6, 7, 12, 13, 14, 15, 10, 11)


def correlate_kernel(*refs):
    strains, source_ref, out_ref, taps_ref, sems = refs[:4], refs[4], refs[5], refs[6], refs[7]
    line_ref, total_ref, even_refs, odd_refs = refs[8], refs[9], refs[10:12], refs[12:14]
    sections = len(strains)
    copies = [
        pltpu.make_async_copy(source_ref.at[section], taps_ref.at[section], sems.at[section])
        for section in range(sections)
    ]
    for copy in copies:
        copy.start()
    rows, taps = taps_ref.shape[1], taps_ref.shape[2]
    lines = [ref.shape[0] for ref in strains]
    blocks = [count - taps // LANE for count in lines]
    slot = line_ref.shape[0] // sections
    span = CHUNK * LANE
    chunks = taps // span
    groups = ((0, 1), (2, 3))
    total_ref[...] = jnp.zeros(total_ref.shape, total_ref.dtype)

    extra = LANE // SUB - ROLLS
    source = lax.broadcasted_iota(jnp.int32, (2 * LANE, extra * LANE), 0)
    target = lax.broadcasted_iota(jnp.int32, (2 * LANE, extra * LANE), 1)
    target = target % LANE + (target // LANE + ROLLS) * SUB
    shifts = jnp.where(source == target, 1.0, 0.0).astype(jnp.bfloat16)

    for section, strain in enumerate(strains):
        first = section * slot
        line_ref[first : first + lines[section], :] = strain[...].astype(jnp.float32)
        line_ref[first + lines[section] : first + slot, :] = jnp.zeros(
            (slot - lines[section], LANE), jnp.float32
        )

    def build(frames, section, chunk, tiles=CHUNK):
        width = (tiles + 1) * LANE
        row = lax.broadcasted_iota(jnp.int32, (ROWS, width), 0)
        first = section * slot + chunk * CHUNK
        wide = jnp.concatenate(
            [
                jnp.broadcast_to(line_ref[pl.ds(first + number, 1), :], (ROWS, LANE))
                for number in range(tiles + 1)
            ],
            axis=1,
        )
        for step in (1, 2, 4):
            moved = pltpu.roll(wide, width - step, axis=1)
            wide = jnp.where((row & step) != 0, moved, wide)
        wide = jnp.concatenate([wide, pltpu.roll(wide, width - ROWS, axis=1)], axis=0)
        wide = wide.astype(jnp.bfloat16)
        moved = [wide]
        for q in range(1, ROLLS):
            moved.append(pltpu.roll(wide, width - SUB * q, axis=1))
        stacked = jnp.concatenate(
            [wide[:, number * LANE : (number + 2) * LANE] for number in range(tiles)], axis=0
        )
        rest = jnp.dot(stacked, shifts, preferred_element_type=jnp.float32).astype(wide.dtype)
        for number in range(tiles):
            pieces = [part[:, number * LANE : (number + 1) * LANE] for part in moved]
            pieces += [
                rest[number * SUB : (number + 1) * SUB, q * LANE : (q + 1) * LANE]
                for q in range(extra)
            ]
            half = section % 2
            frames[number * LANE : (number + 1) * LANE, half * LANE : (half + 1) * LANE] = (
                jnp.concatenate(pieces, axis=0)
            )

    def shifted(section, chunk, tiles):
        pieces = []
        for u in range(blocks[section]):
            first, size = (chunk * CHUNK - u) * LANE, tiles * LANE
            if not isinstance(first, int):
                pieces.append(taps_ref[section, :, pl.ds(pl.multiple_of(first, LANE), size)])
                continue
            parts = []
            if first < 0:
                parts.append(jnp.zeros((rows, -first), taps_ref.dtype))
            if first < taps:
                parts.append(taps_ref[section, :, max(first, 0) : min(first + size, taps)])
            if first + size > taps:
                parts.append(jnp.zeros((rows, first + size - max(first, taps)), taps_ref.dtype))
            pieces.append(jnp.concatenate(parts, axis=1) if len(parts) > 1 else parts[0])
        return pieces

    def accumulate(frames, group, chunk, tiles=CHUNK):
        left = []
        for section in group:
            left += shifted(section, chunk, tiles)
        left = jnp.concatenate(left, axis=0) if len(left) > 1 else left[0]
        both = jnp.dot(
            left, frames[: tiles * LANE, :], preferred_element_type=jnp.float32
        )
        height = 0
        for section in group:
            size = blocks[section] * rows
            half = section % 2
            at = sum(blocks[:section]) * rows
            total_ref[at : at + size, :] += both[
                height : height + size, half * LANE : (half + 1) * LANE
            ]
            height += size

    stages = [(number, chunk, CHUNK) for chunk in range(chunks) for number in range(len(groups))]
    for number, group in enumerate(groups):
        tiles = max(blocks[section] for section in group) - 1
        if tiles:
            stages.append((number, chunks, tiles))

    def buffer(stage):
        number, chunk, _ = stages[stage]
        return (even_refs, odd_refs)[chunk % 2][number]

    def active(stage):
        number, chunk, _ = stages[stage]
        return [s for s in groups[number] if chunk < chunks or blocks[s] > 1]

    def build_stage(stage):
        for section in active(stage):
            build(buffer(stage), section, *stages[stage][1:])

    arrived = set()
    build_stage(0)
    for stage in range(len(stages)):
        for section in active(stage):
            if section not in arrived:
                copies[section].wait()
                arrived.add(section)
        accumulate(buffer(stage), active(stage), *stages[stage][1:])
        if stage + 1 < len(stages):
            build_stage(stage + 1)
    place = 0
    for section in range(sections):
        for u in range(blocks[section]):
            at = (sum(blocks[:section]) + u) * rows
            out_ref[:, place : place + LANE] = total_ref[at : at + rows, :].astype(out_ref.dtype)
            place += LANE


def correlate(streams, basis_taps):
    sections, rows, taps = basis_taps.shape
    padded = -(-rows // SUB) * SUB
    if padded != rows:
        basis_taps = jnp.pad(basis_taps, ((0, 0), (0, padded - rows), (0, 0)))
    samples = sum(x.shape[0] - taps for x in streams)
    longest = max(x.shape[0] for x in streams)
    slot = -(-(longest + LANE) // (8 * LANE)) * 8
    lines = [x.reshape(-1, LANE) for x in streams]
    out = pl.pallas_call(
        correlate_kernel,
        out_shape=pltpu.VMEM((padded, samples), jnp.bfloat16),
        in_specs=[pl.BlockSpec(memory_space=pltpu.VMEM)] * sections
        + [pl.BlockSpec(memory_space=pltpu.HBM)],
        out_specs=pl.BlockSpec(memory_space=pltpu.VMEM),
        scratch_shapes=[
            pltpu.VMEM((sections, padded, taps), jnp.bfloat16),
            pltpu.SemaphoreType.DMA((sections,)),
            pltpu.VMEM((sections * slot, LANE), jnp.float32),
            pltpu.VMEM((samples // LANE * padded, LANE), jnp.float32),
        ]
        + [pltpu.VMEM((CHUNK * LANE, 2 * LANE), jnp.bfloat16)] * 4,
        compiler_params=pltpu.CompilerParams(vmem_limit_bytes=60 * 2**20),
        cost_estimate=pl.CostEstimate(
            flops=2 * padded * taps * samples,
            bytes_accessed=2 * sections * padded * taps,
            transcendentals=0,
        ),
        name="correlate",
    )(*lines, basis_taps)
    return out[:rows]


def exchange(block, distance):
    size = lax.axis_size("tmpl")
    return lax.ppermute(block, "tmpl", [(i, i ^ distance) for i in range(size)])


def gather_blocks(block, ready):
    size = lax.axis_size("tmpl")
    if block.shape[0] % SUB:
        stride = 1
        while stride < size:
            radix = 4 if size // stride >= 4 else 2
            others = [exchange(block, step * stride) for step in range(1, radix)]
            block = jnp.concatenate([block] + others, axis=0)
            stride *= radix
        return [block], ready
    held = {0: block}
    for place in range(2, size, 2):
        high = 1 << (place.bit_length() - 1)
        held[place] = exchange(held[place ^ high and high], place ^ high or place)
    for place in range(1, size, 2):
        source = held[place ^ 1]
        if place == TIED:
            source, ready = lax.optimization_barrier((source, ready))
        held[place] = exchange(source, 1)
    return [held[place] for place in range(size)], ready


def maximum_over_group(values):
    size = lax.axis_size("tmpl")
    tiles = values.reshape(1, -1, LANE)
    copies = jnp.broadcast_to(tiles, (size,) + tiles.shape[1:])
    others = lax.all_to_all(copies, "tmpl", split_axis=0, concat_axis=0, tiled=True)
    return jnp.max(others, axis=0).reshape(values.shape)


def arrange_kernel(offset_ref, coeffs_ref, out_ref):
    bases = coeffs_ref.shape[2]
    source = lax.broadcasted_iota(jnp.int32, (bases, bases), 0)
    target = lax.broadcasted_iota(jnp.int32, (bases, bases), 1) ^ offset_ref[0]
    select = jnp.where(source == target, 1.0, 0.0).astype(jnp.bfloat16)
    for section in range(coeffs_ref.shape[0]):
        out_ref[section] = jnp.dot(
            coeffs_ref[section], select, preferred_element_type=jnp.float32
        ).astype(out_ref.dtype)


def arrange(coeffs, offset):
    return pl.pallas_call(
        arrange_kernel,
        out_shape=jax.ShapeDtypeStruct(coeffs.shape, coeffs.dtype),
        in_specs=[
            pl.BlockSpec(memory_space=pltpu.SMEM),
            pl.BlockSpec(memory_space=pltpu.VMEM),
        ],
        out_specs=pl.BlockSpec(memory_space=pltpu.VMEM),
        compiler_params=pltpu.CompilerParams(vmem_limit_bytes=16 * 2**20),
        cost_estimate=pl.CostEstimate(
            flops=2 * coeffs.size * coeffs.shape[2],
            bytes_accessed=4 * coeffs.size,
            transcendentals=0,
        ),
        name="arrange",
    )(offset, coeffs)


def recon_kernel(order, coeffs_ref, *refs):
    pieces = [refs[order.index(place)] for place in range(len(order))]
    snr_ref, peak_ref = refs[-2], refs[-1]
    samples = snr_ref.shape[1]
    source = lax.broadcasted_iota(jnp.int32, (2 * LANE, 2 * LANE), 0) % LANE
    target = lax.broadcasted_iota(jnp.int32, (2 * LANE, 2 * LANE), 1) // 2
    repeat = jnp.where(source == target, 1.0, 0.0).astype(jnp.bfloat16)
    running = None
    for section in (3, 2, 1, 0):
        width = samples >> section
        offset = sum(samples >> s for s in range(section))
        summed = []
        for place in range(0, width, 2 * LANE):
            size = min(2 * LANE, width)
            first = offset + place
            basis = jnp.concatenate([ref[:, first : first + size] for ref in pieces], axis=0)
            part = jnp.dot(coeffs_ref[section], basis, preferred_element_type=jnp.float32)
            if running is not None:
                coarse = running[place // (2 * LANE)]
                high = coarse.astype(jnp.bfloat16)
                low = (coarse - high.astype(jnp.float32)).astype(jnp.bfloat16)
                part = part + jnp.dot(
                    jnp.concatenate([high, low], axis=1),
                    repeat,
                    preferred_element_type=jnp.float32,
                )
            summed.append(part)
        running = []
        for part in summed:
            running += [part[:, at : at + LANE] for at in range(0, part.shape[1], LANE)]
        if section == 0:
            for number, part in enumerate(summed):
                place = number * 2 * LANE
                snr_ref[:, place : place + 2 * LANE] = part.astype(snr_ref.dtype)
                peak_ref[:, place : place + 2 * LANE] = jnp.max(
                    jnp.abs(part), axis=0, keepdims=True
                )


def reconstruct(coeffs, blocks, samples):
    order = HANDED if len(HANDED) == len(blocks) else tuple(range(len(blocks)))
    return pl.pallas_call(
        functools.partial(recon_kernel, order),
        out_shape=(
            jax.ShapeDtypeStruct((coeffs.shape[1], samples), jnp.bfloat16),
            jax.ShapeDtypeStruct((1, samples), jnp.float32),
        ),
        in_specs=[pl.BlockSpec(memory_space=pltpu.VMEM)] * (1 + len(blocks)),
        out_specs=(pl.BlockSpec(memory_space=pltpu.VMEM),) * 2,
        compiler_params=pltpu.CompilerParams(vmem_limit_bytes=16 * 2**20),
        name="reconstruct",
    )(coeffs, *[blocks[place] for place in order])


def per_device(strain_fast, strain_half, strain_quarter, strain_eighth, basis_taps, recon_coeffs):
    streams = (strain_fast, strain_half, strain_quarter, strain_eighth)
    samples = strain_fast.shape[0] - basis_taps.shape[2]
    offset = (lax.axis_index("tmpl") * basis_taps.shape[1]).astype(jnp.int32).reshape(1)
    coeffs = arrange(recon_coeffs, offset)
    blocks, coeffs = gather_blocks(correlate(streams, basis_taps), coeffs)
    snr_series, local_peak = reconstruct(coeffs, blocks, samples)
    peak_snr = maximum_over_group(local_peak.reshape(samples))
    return (snr_series, peak_snr)


def solution(mesh):
    in_specs = (P(), P(), P(), P(), P("bank", "tmpl", None), P("bank", "tmpl", None))
    out_specs = (P(("bank", "tmpl"), None), P("bank"))
    return jax.shard_map(
        per_device, mesh=mesh, in_specs=in_specs, out_specs=out_specs, check_vma=False
    )
```

```python
import functools

import jax
import jax.numpy as jnp
from jax import lax
from jax.experimental import pallas as pl
from jax.experimental.pallas import tpu as pltpu
from jax.sharding import PartitionSpec as P

LANE = 128
CHUNK = 32
SUB = 16
ROWS = 8
ROLLS = 4
TIED = 9
HANDED = (12, 13, 4, 5, 0, 1, 6, 7, 14, 15, 10, 11, 2, 3, 8, 9)


def correlate_kernel(*refs):
    strains, source_ref, out_ref, taps_ref, sems = refs[:4], refs[4], refs[5], refs[6], refs[7]
    line_ref, total_ref, even_refs, odd_refs = refs[8], refs[9], refs[10:12], refs[12:14]
    sections = len(strains)
    copies = [
        pltpu.make_async_copy(source_ref.at[section], taps_ref.at[section], sems.at[section])
        for section in range(sections)
    ]
    for copy in copies:
        copy.start()
    rows, taps = taps_ref.shape[1], taps_ref.shape[2]
    lines = [ref.shape[0] for ref in strains]
    blocks = [count - taps // LANE for count in lines]
    slot = line_ref.shape[0] // sections
    span = CHUNK * LANE
    chunks = taps // span
    groups = ((0, 1), (2, 3))
    total_ref[...] = jnp.zeros(total_ref.shape, total_ref.dtype)

    extra = LANE // SUB - ROLLS
    source = lax.broadcasted_iota(jnp.int32, (2 * LANE, extra * LANE), 0)
    target = lax.broadcasted_iota(jnp.int32, (2 * LANE, extra * LANE), 1)
    target = target % LANE + (target // LANE + ROLLS) * SUB
    shifts = jnp.where(source == target, 1.0, 0.0).astype(jnp.bfloat16)

    for section, strain in enumerate(strains):
        first = section * slot
        line_ref[first : first + lines[section], :] = strain[...].astype(jnp.float32)
        line_ref[first + lines[section] : first + slot, :] = jnp.zeros(
            (slot - lines[section], LANE), jnp.float32
        )

    def build(frames, section, chunk, tiles=CHUNK):
        width = (tiles + 1) * LANE
        row = lax.broadcasted_iota(jnp.int32, (ROWS, width), 0)
        first = section * slot + chunk * CHUNK
        wide = jnp.concatenate(
            [
                jnp.broadcast_to(line_ref[pl.ds(first + number, 1), :], (ROWS, LANE))
                for number in range(tiles + 1)
            ],
            axis=1,
        )
        for step in (1, 2, 4):
            moved = pltpu.roll(wide, width - step, axis=1)
            wide = jnp.where((row & step) != 0, moved, wide)
        wide = jnp.concatenate([wide, pltpu.roll(wide, width - ROWS, axis=1)], axis=0)
        wide = wide.astype(jnp.bfloat16)
        moved = [wide]
        for q in range(1, ROLLS):
            moved.append(pltpu.roll(wide, width - SUB * q, axis=1))
        stacked = jnp.concatenate(
            [wide[:, number * LANE : (number + 2) * LANE] for number in range(tiles)], axis=0
        )
        rest = jnp.dot(stacked, shifts, preferred_element_type=jnp.float32).astype(wide.dtype)
        for number in range(tiles):
            pieces = [part[:, number * LANE : (number + 1) * LANE] for part in moved]
            pieces += [
                rest[number * SUB : (number + 1) * SUB, q * LANE : (q + 1) * LANE]
                for q in range(extra)
            ]
            half = section % 2
            frames[number * LANE : (number + 1) * LANE, half * LANE : (half + 1) * LANE] = (
                jnp.concatenate(pieces, axis=0)
            )

    def shifted(section, chunk, tiles):
        pieces = []
        for u in range(blocks[section]):
            first, size = (chunk * CHUNK - u) * LANE, tiles * LANE
            if not isinstance(first, int):
                pieces.append(taps_ref[section, :, pl.ds(pl.multiple_of(first, LANE), size)])
                continue
            parts = []
            if first < 0:
                parts.append(jnp.zeros((rows, -first), taps_ref.dtype))
            if first < taps:
                parts.append(taps_ref[section, :, max(first, 0) : min(first + size, taps)])
            if first + size > taps:
                parts.append(jnp.zeros((rows, first + size - max(first, taps)), taps_ref.dtype))
            pieces.append(jnp.concatenate(parts, axis=1) if len(parts) > 1 else parts[0])
        return pieces

    def accumulate(frames, group, chunk, tiles=CHUNK):
        left = []
        for section in group:
            left += shifted(section, chunk, tiles)
        left = jnp.concatenate(left, axis=0) if len(left) > 1 else left[0]
        both = jnp.dot(
            left, frames[: tiles * LANE, :], preferred_element_type=jnp.float32
        )
        height = 0
        for section in group:
            size = blocks[section] * rows
            half = section % 2
            at = sum(blocks[:section]) * rows
            total_ref[at : at + size, :] += both[
                height : height + size, half * LANE : (half + 1) * LANE
            ]
            height += size

    stages = [(number, chunk, CHUNK) for chunk in range(chunks) for number in range(len(groups))]
    for number, group in enumerate(groups):
        tiles = max(blocks[section] for section in group) - 1
        if tiles:
            stages.append((number, chunks, tiles))

    def buffer(stage):
        number, chunk, _ = stages[stage]
        return (even_refs, odd_refs)[chunk % 2][number]

    def active(stage):
        number, chunk, _ = stages[stage]
        return [s for s in groups[number] if chunk < chunks or blocks[s] > 1]

    def build_stage(stage):
        for section in active(stage):
            build(buffer(stage), section, *stages[stage][1:])

    arrived = set()
    build_stage(0)
    for stage in range(len(stages)):
        for section in active(stage):
            if section not in arrived:
                copies[section].wait()
                arrived.add(section)
        accumulate(buffer(stage), active(stage), *stages[stage][1:])
        if stage + 1 < len(stages):
            build_stage(stage + 1)
    place = 0
    for section in range(sections):
        for u in range(blocks[section]):
            at = (sum(blocks[:section]) + u) * rows
            out_ref[:, place : place + LANE] = total_ref[at : at + rows, :].astype(out_ref.dtype)
            place += LANE


def correlate(streams, basis_taps):
    sections, rows, taps = basis_taps.shape
    padded = -(-rows // SUB) * SUB
    if padded != rows:
        basis_taps = jnp.pad(basis_taps, ((0, 0), (0, padded - rows), (0, 0)))
    samples = sum(x.shape[0] - taps for x in streams)
    longest = max(x.shape[0] for x in streams)
    slot = -(-(longest + LANE) // (8 * LANE)) * 8
    lines = [x.reshape(-1, LANE) for x in streams]
    out = pl.pallas_call(
        correlate_kernel,
        out_shape=pltpu.VMEM((padded, samples), jnp.bfloat16),
        in_specs=[pl.BlockSpec(memory_space=pltpu.VMEM)] * sections
        + [pl.BlockSpec(memory_space=pltpu.HBM)],
        out_specs=pl.BlockSpec(memory_space=pltpu.VMEM),
        scratch_shapes=[
            pltpu.VMEM((sections, padded, taps), jnp.bfloat16),
            pltpu.SemaphoreType.DMA((sections,)),
            pltpu.VMEM((sections * slot, LANE), jnp.float32),
            pltpu.VMEM((samples // LANE * padded, LANE), jnp.float32),
        ]
        + [pltpu.VMEM((CHUNK * LANE, 2 * LANE), jnp.bfloat16)] * 4,
        compiler_params=pltpu.CompilerParams(vmem_limit_bytes=60 * 2**20),
        cost_estimate=pl.CostEstimate(
            flops=2 * padded * taps * samples,
            bytes_accessed=2 * sections * padded * taps,
            transcendentals=0,
        ),
        name="correlate",
    )(*lines, basis_taps)
    return out[:rows]


def exchange(block, distance):
    size = lax.axis_size("tmpl")
    return lax.ppermute(block, "tmpl", [(i, i ^ distance) for i in range(size)])


def gather_blocks(block, ready):
    size = lax.axis_size("tmpl")
    if block.shape[0] % SUB:
        stride = 1
        while stride < size:
            radix = 4 if size // stride >= 4 else 2
            others = [exchange(block, step * stride) for step in range(1, radix)]
            block = jnp.concatenate([block] + others, axis=0)
            stride *= radix
        return [block], ready
    held = {0: block}
    for place in range(2, size, 2):
        high = 1 << (place.bit_length() - 1)
        held[place] = exchange(held[place ^ high and high], place ^ high or place)
    for place in range(1, size, 2):
        source = held[place ^ 1]
        if place == TIED:
            source, ready = lax.optimization_barrier((source, ready))
        held[place] = exchange(source, 1)
    return [held[place] for place in range(size)], ready


def maximum_over_group(values):
    size = lax.axis_size("tmpl")
    values = jnp.maximum(values, exchange(values, 1))
    tiles = values.reshape(1, -1, LANE)
    copies = jnp.broadcast_to(tiles, (size // 2,) + tiles.shape[1:])
    groups = [list(range(core, size, 2)) for core in range(2)]
    others = lax.all_to_all(
        copies, "tmpl", split_axis=0, concat_axis=0, axis_index_groups=groups, tiled=True
    )
    return jnp.max(others, axis=0).reshape(values.shape)


def arrange_kernel(offset_ref, coeffs_ref, out_ref):
    bases = coeffs_ref.shape[2]
    source = lax.broadcasted_iota(jnp.int32, (bases, bases), 0)
    target = lax.broadcasted_iota(jnp.int32, (bases, bases), 1) ^ offset_ref[0]
    select = jnp.where(source == target, 1.0, 0.0).astype(jnp.bfloat16)
    for section in range(coeffs_ref.shape[0]):
        out_ref[section] = jnp.dot(
            coeffs_ref[section], select, preferred_element_type=jnp.float32
        ).astype(out_ref.dtype)


def arrange(coeffs, offset):
    return pl.pallas_call(
        arrange_kernel,
        out_shape=jax.ShapeDtypeStruct(coeffs.shape, coeffs.dtype),
        in_specs=[
            pl.BlockSpec(memory_space=pltpu.SMEM),
            pl.BlockSpec(memory_space=pltpu.VMEM),
        ],
        out_specs=pl.BlockSpec(memory_space=pltpu.VMEM),
        compiler_params=pltpu.CompilerParams(vmem_limit_bytes=16 * 2**20),
        cost_estimate=pl.CostEstimate(
            flops=2 * coeffs.size * coeffs.shape[2],
            bytes_accessed=4 * coeffs.size,
            transcendentals=0,
        ),
        name="arrange",
    )(offset, coeffs)


def recon_kernel(order, coeffs_ref, *refs):
    pieces = [refs[order.index(place)] for place in range(len(order))]
    snr_ref, peak_ref = refs[-2], refs[-1]
    samples = snr_ref.shape[1]
    source = lax.broadcasted_iota(jnp.int32, (2 * LANE, 2 * LANE), 0) % LANE
    target = lax.broadcasted_iota(jnp.int32, (2 * LANE, 2 * LANE), 1) // 2
    repeat = jnp.where(source == target, 1.0, 0.0).astype(jnp.bfloat16)
    running = None
    for section in (3, 2, 1, 0):
        width = samples >> section
        offset = sum(samples >> s for s in range(section))
        summed = []
        for place in range(0, width, 2 * LANE):
            size = min(2 * LANE, width)
            first = offset + place
            basis = jnp.concatenate([ref[:, first : first + size] for ref in pieces], axis=0)
            part = jnp.dot(coeffs_ref[section], basis, preferred_element_type=jnp.float32)
            if running is not None:
                coarse = running[place // (2 * LANE)]
                high = coarse.astype(jnp.bfloat16)
                low = (coarse - high.astype(jnp.float32)).astype(jnp.bfloat16)
                part = part + jnp.dot(
                    jnp.concatenate([high, low], axis=1),
                    repeat,
                    preferred_element_type=jnp.float32,
                )
            summed.append(part)
        running = []
        for part in summed:
            running += [part[:, at : at + LANE] for at in range(0, part.shape[1], LANE)]
        if section == 0:
            for number, part in enumerate(summed):
                place = number * 2 * LANE
                snr_ref[:, place : place + 2 * LANE] = part.astype(snr_ref.dtype)
                peak_ref[:, place : place + 2 * LANE] = jnp.max(
                    jnp.abs(part), axis=0, keepdims=True
                )


def reconstruct(coeffs, blocks, samples):
    order = HANDED if len(HANDED) == len(blocks) else tuple(range(len(blocks)))
    return pl.pallas_call(
        functools.partial(recon_kernel, order),
        out_shape=(
            jax.ShapeDtypeStruct((coeffs.shape[1], samples), jnp.bfloat16),
            jax.ShapeDtypeStruct((1, samples), jnp.float32),
        ),
        in_specs=[pl.BlockSpec(memory_space=pltpu.VMEM)] * (1 + len(blocks)),
        out_specs=(pl.BlockSpec(memory_space=pltpu.VMEM),) * 2,
        compiler_params=pltpu.CompilerParams(vmem_limit_bytes=16 * 2**20),
        name="reconstruct",
    )(coeffs, *[blocks[place] for place in order])


def per_device(strain_fast, strain_half, strain_quarter, strain_eighth, basis_taps, recon_coeffs):
    streams = (strain_fast, strain_half, strain_quarter, strain_eighth)
    samples = strain_fast.shape[0] - basis_taps.shape[2]
    offset = (lax.axis_index("tmpl") * basis_taps.shape[1]).astype(jnp.int32).reshape(1)
    coeffs = arrange(recon_coeffs, offset)
    blocks, coeffs = gather_blocks(correlate(streams, basis_taps), coeffs)
    snr_series, local_peak = reconstruct(coeffs, blocks, samples)
    peak_snr = maximum_over_group(local_peak.reshape(samples))
    return (snr_series, peak_snr)


def solution(mesh):
    in_specs = (P(), P(), P(), P(), P("bank", "tmpl", None), P("bank", "tmpl", None))
    out_specs = (P(("bank", "tmpl"), None), P("bank"))
    return jax.shard_map(
        per_device, mesh=mesh, in_specs=in_specs, out_specs=out_specs, check_vma=False
    )
```

```python
import functools

import jax
import jax.numpy as jnp
from jax import lax
from jax.experimental import pallas as pl
from jax.experimental.pallas import tpu as pltpu
from jax.sharding import PartitionSpec as P

LANE = 128
CHUNK = 32
SUB = 16
ROWS = 8
ROLLS = 4
TIED = 1
FIRST = (0, 5, 3, 7, 6, 4, 1, 2)
SECOND = (7, 1, 4, 5, 3, 0, 2, 6)


def correlate_kernel(*refs):
    strains, source_ref, out_ref, taps_ref, sems = refs[:4], refs[4], refs[5], refs[6], refs[7]
    line_ref, total_ref, even_refs, odd_refs = refs[8], refs[9], refs[10:12], refs[12:14]
    sections = len(strains)
    copies = [
        pltpu.make_async_copy(source_ref.at[section], taps_ref.at[section], sems.at[section])
        for section in range(sections)
    ]
    for copy in copies:
        copy.start()
    rows, taps = taps_ref.shape[1], taps_ref.shape[2]
    lines = [ref.shape[0] for ref in strains]
    blocks = [count - taps // LANE for count in lines]
    slot = line_ref.shape[0] // sections
    span = CHUNK * LANE
    chunks = taps // span
    groups = ((0, 1), (2, 3))
    total_ref[...] = jnp.zeros(total_ref.shape, total_ref.dtype)

    extra = LANE // SUB - ROLLS
    source = lax.broadcasted_iota(jnp.int32, (2 * LANE, extra * LANE), 0)
    target = lax.broadcasted_iota(jnp.int32, (2 * LANE, extra * LANE), 1)
    target = target % LANE + (target // LANE + ROLLS) * SUB
    shifts = jnp.where(source == target, 1.0, 0.0).astype(jnp.bfloat16)

    for section, strain in enumerate(strains):
        first = section * slot
        line_ref[first : first + lines[section], :] = strain[...].astype(jnp.float32)
        line_ref[first + lines[section] : first + slot, :] = jnp.zeros(
            (slot - lines[section], LANE), jnp.float32
        )

    def build(frames, section, chunk, tiles=CHUNK):
        width = (tiles + 1) * LANE
        row = lax.broadcasted_iota(jnp.int32, (ROWS, width), 0)
        first = section * slot + chunk * CHUNK
        wide = jnp.concatenate(
            [
                jnp.broadcast_to(line_ref[pl.ds(first + number, 1), :], (ROWS, LANE))
                for number in range(tiles + 1)
            ],
            axis=1,
        )
        for step in (1, 2, 4):
            moved = pltpu.roll(wide, width - step, axis=1)
            wide = jnp.where((row & step) != 0, moved, wide)
        wide = jnp.concatenate([wide, pltpu.roll(wide, width - ROWS, axis=1)], axis=0)
        wide = wide.astype(jnp.bfloat16)
        moved = [wide]
        for q in range(1, ROLLS):
            moved.append(pltpu.roll(wide, width - SUB * q, axis=1))
        stacked = jnp.concatenate(
            [wide[:, number * LANE : (number + 2) * LANE] for number in range(tiles)], axis=0
        )
        rest = jnp.dot(stacked, shifts, preferred_element_type=jnp.float32).astype(wide.dtype)
        for number in range(tiles):
            pieces = [part[:, number * LANE : (number + 1) * LANE] for part in moved]
            pieces += [
                rest[number * SUB : (number + 1) * SUB, q * LANE : (q + 1) * LANE]
                for q in range(extra)
            ]
            half = section % 2
            frames[number * LANE : (number + 1) * LANE, half * LANE : (half + 1) * LANE] = (
                jnp.concatenate(pieces, axis=0)
            )

    def shifted(section, chunk, tiles):
        pieces = []
        for u in range(blocks[section]):
            first, size = (chunk * CHUNK - u) * LANE, tiles * LANE
            if not isinstance(first, int):
                pieces.append(taps_ref[section, :, pl.ds(pl.multiple_of(first, LANE), size)])
                continue
            parts = []
            if first < 0:
                parts.append(jnp.zeros((rows, -first), taps_ref.dtype))
            if first < taps:
                parts.append(taps_ref[section, :, max(first, 0) : min(first + size, taps)])
            if first + size > taps:
                parts.append(jnp.zeros((rows, first + size - max(first, taps)), taps_ref.dtype))
            pieces.append(jnp.concatenate(parts, axis=1) if len(parts) > 1 else parts[0])
        return pieces

    def accumulate(frames, group, chunk, tiles=CHUNK):
        left = []
        for section in group:
            left += shifted(section, chunk, tiles)
        left = jnp.concatenate(left, axis=0) if len(left) > 1 else left[0]
        both = jnp.dot(
            left, frames[: tiles * LANE, :], preferred_element_type=jnp.float32
        )
        height = 0
        for section in group:
            size = blocks[section] * rows
            half = section % 2
            at = sum(blocks[:section]) * rows
            total_ref[at : at + size, :] += both[
                height : height + size, half * LANE : (half + 1) * LANE
            ]
            height += size

    stages = [(number, chunk, CHUNK) for chunk in range(chunks) for number in range(len(groups))]
    for number, group in enumerate(groups):
        tiles = max(blocks[section] for section in group) - 1
        if tiles:
            stages.append((number, chunks, tiles))

    def buffer(stage):
        number, chunk, _ = stages[stage]
        return (even_refs, odd_refs)[chunk % 2][number]

    def active(stage):
        number, chunk, _ = stages[stage]
        return [s for s in groups[number] if chunk < chunks or blocks[s] > 1]

    def build_stage(stage):
        for section in active(stage):
            build(buffer(stage), section, *stages[stage][1:])

    arrived = set()
    build_stage(0)
    for stage in range(len(stages)):
        for section in active(stage):
            if section not in arrived:
                copies[section].wait()
                arrived.add(section)
        accumulate(buffer(stage), active(stage), *stages[stage][1:])
        if stage + 1 < len(stages):
            build_stage(stage + 1)
    place = 0
    for section in range(sections):
        for u in range(blocks[section]):
            at = (sum(blocks[:section]) + u) * rows
            out_ref[:, place : place + LANE] = total_ref[at : at + rows, :].astype(out_ref.dtype)
            place += LANE


def correlate(streams, basis_taps):
    sections, rows, taps = basis_taps.shape
    padded = -(-rows // SUB) * SUB
    if padded != rows:
        basis_taps = jnp.pad(basis_taps, ((0, 0), (0, padded - rows), (0, 0)))
    samples = sum(x.shape[0] - taps for x in streams)
    longest = max(x.shape[0] for x in streams)
    slot = -(-(longest + LANE) // (8 * LANE)) * 8
    lines = [x.reshape(-1, LANE) for x in streams]
    out = pl.pallas_call(
        correlate_kernel,
        out_shape=pltpu.VMEM((padded, samples), jnp.bfloat16),
        in_specs=[pl.BlockSpec(memory_space=pltpu.VMEM)] * sections
        + [pl.BlockSpec(memory_space=pltpu.HBM)],
        out_specs=pl.BlockSpec(memory_space=pltpu.VMEM),
        scratch_shapes=[
            pltpu.VMEM((sections, padded, taps), jnp.bfloat16),
            pltpu.SemaphoreType.DMA((sections,)),
            pltpu.VMEM((sections * slot, LANE), jnp.float32),
            pltpu.VMEM((samples // LANE * padded, LANE), jnp.float32),
        ]
        + [pltpu.VMEM((CHUNK * LANE, 2 * LANE), jnp.bfloat16)] * 4,
        compiler_params=pltpu.CompilerParams(vmem_limit_bytes=60 * 2**20),
        cost_estimate=pl.CostEstimate(
            flops=2 * padded * taps * samples,
            bytes_accessed=2 * sections * padded * taps,
            transcendentals=0,
        ),
        name="correlate",
    )(*lines, basis_taps)
    return out[:rows]


def exchange(block, distance):
    size = lax.axis_size("tmpl")
    return lax.ppermute(block, "tmpl", [(i, i ^ distance) for i in range(size)])


def gather_blocks(block, ready):
    size = lax.axis_size("tmpl")
    if block.shape[0] % SUB:
        stride = 1
        while stride < size:
            radix = 4 if size // stride >= 4 else 2
            others = [exchange(block, step * stride) for step in range(1, radix)]
            block = jnp.concatenate([block] + others, axis=0)
            stride *= radix
        return [block], ready
    held = {0: block}
    for place in range(2, size, 2):
        high = 1 << (place.bit_length() - 1)
        held[place] = exchange(held[place ^ high and high], place ^ high or place)
    for place in range(1, size, 2):
        source = held[place ^ 1]
        if place == TIED:
            source, ready = lax.optimization_barrier((source, ready))
        held[place] = exchange(source, 1)
    return [held[place] for place in range(size)], ready


def maximum_over_group(values):
    size = lax.axis_size("tmpl")
    tiles = values.reshape(1, -1, LANE)
    copies = jnp.broadcast_to(tiles, (size,) + tiles.shape[1:])
    others = lax.all_to_all(copies, "tmpl", split_axis=0, concat_axis=0, tiled=True)
    return jnp.max(others, axis=0).reshape(values.shape)


def arrange_kernel(order, offset_ref, coeffs_ref, out_ref):
    bases = coeffs_ref.shape[2]
    rows = bases // len(order)
    source = lax.broadcasted_iota(jnp.int32, (bases, bases), 0)
    column = lax.broadcasted_iota(jnp.int32, (1, bases), 1)
    target = column
    for group, place in enumerate(order):
        if group != place:
            inside = (column >= group * rows) & (column < (group + 1) * rows)
            target = jnp.where(inside, column + (place - group) * rows, target)
    select = jnp.where(source == (target ^ offset_ref[0]), 1.0, 0.0).astype(jnp.bfloat16)
    for section in range(coeffs_ref.shape[0]):
        out_ref[section] = jnp.dot(
            coeffs_ref[section], select, preferred_element_type=jnp.float32
        ).astype(out_ref.dtype)


def arrange(coeffs, offset, order):
    return pl.pallas_call(
        functools.partial(arrange_kernel, order),
        out_shape=jax.ShapeDtypeStruct(coeffs.shape, coeffs.dtype),
        in_specs=[
            pl.BlockSpec(memory_space=pltpu.SMEM),
            pl.BlockSpec(memory_space=pltpu.VMEM),
        ],
        out_specs=pl.BlockSpec(memory_space=pltpu.VMEM),
        compiler_params=pltpu.CompilerParams(vmem_limit_bytes=16 * 2**20),
        cost_estimate=pl.CostEstimate(
            flops=2 * coeffs.size * coeffs.shape[2],
            bytes_accessed=4 * coeffs.size,
            transcendentals=0,
        ),
        name="arrange",
    )(offset, coeffs)


def section_product(coeffs_ref, pieces, samples, section, place, size, at):
    first = sum(samples >> s for s in range(section)) + place
    basis = jnp.concatenate([ref[:, first : first + size] for ref in pieces], axis=0)
    left = coeffs_ref[section, :, at : at + basis.shape[0]]
    return jnp.dot(left, basis, preferred_element_type=jnp.float32)


def partial_kernel(order, samples, coeffs_ref, *refs):
    pieces, out_ref = [refs[order.index(place)] for place in range(len(order))], refs[-1]
    for section in range(coeffs_ref.shape[0]):
        width = samples >> section
        offset = sum(samples >> s for s in range(section))
        for place in range(0, width, 2 * LANE):
            size = min(2 * LANE, width)
            out_ref[:, offset + place : offset + place + size] = section_product(
                coeffs_ref, pieces, samples, section, place, size, 0
            )


def partial_sums(coeffs, blocks, samples):
    order = FIRST if len(FIRST) == len(blocks) else tuple(range(len(blocks)))
    rows, width = sum(block.shape[0] for block in blocks), blocks[0].shape[1]
    return pl.pallas_call(
        functools.partial(partial_kernel, order, samples),
        out_shape=pltpu.VMEM((coeffs.shape[1], width), jnp.float32),
        in_specs=[pl.BlockSpec(memory_space=pltpu.VMEM)] * (1 + len(blocks)),
        out_specs=pl.BlockSpec(memory_space=pltpu.VMEM),
        compiler_params=pltpu.CompilerParams(vmem_limit_bytes=16 * 2**20),
        cost_estimate=pl.CostEstimate(
            flops=2 * coeffs.shape[1] * rows * width,
            bytes_accessed=4 * coeffs.shape[1] * width + 2 * rows * width,
            transcendentals=0,
        ),
        name="partial_sums",
    )(coeffs, *[blocks[place] for place in order])


def recon_kernel(order, begun, *refs):
    coeffs_ref, refs = refs[0], refs[1:]
    first_ref, refs = (refs[0], refs[1:]) if begun else (None, refs)
    pieces = [refs[order.index(place)] for place in range(len(order))]
    snr_ref, peak_ref = refs[-2], refs[-1]
    samples = snr_ref.shape[1]
    at = coeffs_ref.shape[2] - sum(piece.shape[0] for piece in pieces)
    source = lax.broadcasted_iota(jnp.int32, (2 * LANE, 2 * LANE), 0) % LANE
    target = lax.broadcasted_iota(jnp.int32, (2 * LANE, 2 * LANE), 1) // 2
    repeat = jnp.where(source == target, 1.0, 0.0).astype(jnp.bfloat16)
    running = None
    for section in (3, 2, 1, 0):
        width = samples >> section
        offset = sum(samples >> s for s in range(section))
        summed = []
        for place in range(0, width, 2 * LANE):
            size = min(2 * LANE, width)
            part = section_product(coeffs_ref, pieces, samples, section, place, size, at)
            if begun:
                part = part + first_ref[:, offset + place : offset + place + size]
            if running is not None:
                coarse = running[place // (2 * LANE)]
                high = coarse.astype(jnp.bfloat16)
                low = (coarse - high.astype(jnp.float32)).astype(jnp.bfloat16)
                part = part + jnp.dot(
                    jnp.concatenate([high, low], axis=1),
                    repeat,
                    preferred_element_type=jnp.float32,
                )
            summed.append(part)
        running = []
        for part in summed:
            running += [part[:, at_ : at_ + LANE] for at_ in range(0, part.shape[1], LANE)]
        if section == 0:
            for number, part in enumerate(summed):
                place = number * 2 * LANE
                snr_ref[:, place : place + 2 * LANE] = part.astype(snr_ref.dtype)
                peak_ref[:, place : place + 2 * LANE] = jnp.max(
                    jnp.abs(part), axis=0, keepdims=True
                )


def reconstruct(coeffs, first, blocks, samples):
    order = SECOND if len(SECOND) == len(blocks) else tuple(range(len(blocks)))
    begun = () if first is None else (first,)
    return pl.pallas_call(
        functools.partial(recon_kernel, order, bool(begun)),
        out_shape=(
            jax.ShapeDtypeStruct((coeffs.shape[1], samples), jnp.bfloat16),
            jax.ShapeDtypeStruct((1, samples), jnp.float32),
        ),
        in_specs=[pl.BlockSpec(memory_space=pltpu.VMEM)] * (1 + len(begun) + len(blocks)),
        out_specs=(pl.BlockSpec(memory_space=pltpu.VMEM),) * 2,
        compiler_params=pltpu.CompilerParams(vmem_limit_bytes=16 * 2**20),
        name="reconstruct",
    )(coeffs, *begun, *[blocks[place] for place in order])


def per_device(strain_fast, strain_half, strain_quarter, strain_eighth, basis_taps, recon_coeffs):
    streams = (strain_fast, strain_half, strain_quarter, strain_eighth)
    samples = strain_fast.shape[0] - basis_taps.shape[2]
    rows = basis_taps.shape[1]
    places = tuple(range(lax.axis_size("tmpl")))
    early = places[::2] if rows % SUB == 0 else ()
    order = early + tuple(place for place in places if place not in early)
    offset = (lax.axis_index("tmpl") * rows).astype(jnp.int32).reshape(1)
    coeffs = arrange(recon_coeffs, offset, order)
    blocks, coeffs = gather_blocks(correlate(streams, basis_taps), coeffs)
    first = None
    if early:
        first = partial_sums(coeffs, blocks[::2], samples)
        blocks = blocks[1::2]
    snr_series, local_peak = reconstruct(coeffs, first, blocks, samples)
    peak_snr = maximum_over_group(local_peak.reshape(samples))
    return (snr_series, peak_snr)


def solution(mesh):
    in_specs = (P(), P(), P(), P(), P("bank", "tmpl", None), P("bank", "tmpl", None))
    out_specs = (P(("bank", "tmpl"), None), P("bank"))
    return jax.shard_map(
        per_device, mesh=mesh, in_specs=in_specs, out_specs=out_specs, check_vma=False
    )
```

```python
import functools

import jax
import jax.numpy as jnp
from jax import lax
from jax.experimental import pallas as pl
from jax.experimental.pallas import tpu as pltpu
from jax.sharding import PartitionSpec as P

LANE = 128
CHUNK = 32
SUB = 16
ROWS = 8
ROLLS = 4
TIED = 1
HANDED = (6, 7, 2, 3, 0, 1, 12, 13, 8, 9, 10, 11, 4, 5, 14, 15)


def correlate_kernel(*refs):
    strains, source_ref, out_ref, taps_ref, sems = refs[:4], refs[4], refs[5], refs[6], refs[7]
    line_ref, total_ref, even_refs, odd_refs = refs[8], refs[9], refs[10:12], refs[12:14]
    sections = len(strains)
    copies = [
        pltpu.make_async_copy(source_ref.at[section], taps_ref.at[section], sems.at[section])
        for section in range(sections)
    ]
    for copy in copies:
        copy.start()
    rows, taps = taps_ref.shape[1], taps_ref.shape[2]
    lines = [ref.shape[0] for ref in strains]
    blocks = [count - taps // LANE for count in lines]
    slot = line_ref.shape[0] // sections
    span = CHUNK * LANE
    chunks = taps // span
    groups = ((0, 1), (2, 3))
    total_ref[...] = jnp.zeros(total_ref.shape, total_ref.dtype)

    extra = LANE // SUB - ROLLS
    source = lax.broadcasted_iota(jnp.int32, (2 * LANE, extra * LANE), 0)
    target = lax.broadcasted_iota(jnp.int32, (2 * LANE, extra * LANE), 1)
    target = target % LANE + (target // LANE + ROLLS) * SUB
    shifts = jnp.where(source == target, 1.0, 0.0).astype(jnp.bfloat16)

    for section, strain in enumerate(strains):
        first = section * slot
        line_ref[first : first + lines[section], :] = strain[...].astype(jnp.float32)
        line_ref[first + lines[section] : first + slot, :] = jnp.zeros(
            (slot - lines[section], LANE), jnp.float32
        )

    def build(frames, section, chunk, tiles=CHUNK):
        width = (tiles + 1) * LANE
        row = lax.broadcasted_iota(jnp.int32, (ROWS, width), 0)
        first = section * slot + chunk * CHUNK
        wide = jnp.concatenate(
            [
                jnp.broadcast_to(line_ref[pl.ds(first + number, 1), :], (ROWS, LANE))
                for number in range(tiles + 1)
            ],
            axis=1,
        )
        for step in (1, 2, 4):
            moved = pltpu.roll(wide, width - step, axis=1)
            wide = jnp.where((row & step) != 0, moved, wide)
        wide = jnp.concatenate([wide, pltpu.roll(wide, width - ROWS, axis=1)], axis=0)
        wide = wide.astype(jnp.bfloat16)
        moved = [wide]
        for q in range(1, ROLLS):
            moved.append(pltpu.roll(wide, width - SUB * q, axis=1))
        stacked = jnp.concatenate(
            [wide[:, number * LANE : (number + 2) * LANE] for number in range(tiles)], axis=0
        )
        rest = jnp.dot(stacked, shifts, preferred_element_type=jnp.float32).astype(wide.dtype)
        for number in range(tiles):
            pieces = [part[:, number * LANE : (number + 1) * LANE] for part in moved]
            pieces += [
                rest[number * SUB : (number + 1) * SUB, q * LANE : (q + 1) * LANE]
                for q in range(extra)
            ]
            half = section % 2
            frames[number * LANE : (number + 1) * LANE, half * LANE : (half + 1) * LANE] = (
                jnp.concatenate(pieces, axis=0)
            )

    def shifted(section, chunk, tiles):
        pieces = []
        for u in range(blocks[section]):
            first, size = (chunk * CHUNK - u) * LANE, tiles * LANE
            if not isinstance(first, int):
                pieces.append(taps_ref[section, :, pl.ds(pl.multiple_of(first, LANE), size)])
                continue
            parts = []
            if first < 0:
                parts.append(jnp.zeros((rows, -first), taps_ref.dtype))
            if first < taps:
                parts.append(taps_ref[section, :, max(first, 0) : min(first + size, taps)])
            if first + size > taps:
                parts.append(jnp.zeros((rows, first + size - max(first, taps)), taps_ref.dtype))
            pieces.append(jnp.concatenate(parts, axis=1) if len(parts) > 1 else parts[0])
        return pieces

    def accumulate(frames, group, chunk, tiles=CHUNK):
        left = []
        for section in group:
            left += shifted(section, chunk, tiles)
        left = jnp.concatenate(left, axis=0) if len(left) > 1 else left[0]
        both = jnp.dot(
            left, frames[: tiles * LANE, :], preferred_element_type=jnp.float32
        )
        height = 0
        for section in group:
            size = blocks[section] * rows
            half = section % 2
            at = sum(blocks[:section]) * rows
            total_ref[at : at + size, :] += both[
                height : height + size, half * LANE : (half + 1) * LANE
            ]
            height += size

    stages = [(number, chunk, CHUNK) for chunk in range(chunks) for number in range(len(groups))]
    for number, group in enumerate(groups):
        tiles = max(blocks[section] for section in group) - 1
        if tiles:
            stages.append((number, chunks, tiles))

    def buffer(stage):
        number, chunk, _ = stages[stage]
        return (even_refs, odd_refs)[chunk % 2][number]

    def active(stage):
        number, chunk, _ = stages[stage]
        return [s for s in groups[number] if chunk < chunks or blocks[s] > 1]

    def build_stage(stage):
        for section in active(stage):
            build(buffer(stage), section, *stages[stage][1:])

    arrived = set()
    build_stage(0)
    for stage in range(len(stages)):
        for section in active(stage):
            if section not in arrived:
                copies[section].wait()
                arrived.add(section)
        accumulate(buffer(stage), active(stage), *stages[stage][1:])
        if stage + 1 < len(stages):
            build_stage(stage + 1)
    place = 0
    for section in range(sections):
        for u in range(blocks[section]):
            at = (sum(blocks[:section]) + u) * rows
            out_ref[:, place : place + LANE] = total_ref[at : at + rows, :].astype(out_ref.dtype)
            place += LANE


def correlate(streams, basis_taps):
    sections, rows, taps = basis_taps.shape
    padded = -(-rows // SUB) * SUB
    if padded != rows:
        basis_taps = jnp.pad(basis_taps, ((0, 0), (0, padded - rows), (0, 0)))
    samples = sum(x.shape[0] - taps for x in streams)
    longest = max(x.shape[0] for x in streams)
    slot = -(-(longest + LANE) // (8 * LANE)) * 8
    lines = [x.reshape(-1, LANE) for x in streams]
    out = pl.pallas_call(
        correlate_kernel,
        out_shape=pltpu.VMEM((padded, samples), jnp.bfloat16),
        in_specs=[pl.BlockSpec(memory_space=pltpu.VMEM)] * sections
        + [pl.BlockSpec(memory_space=pltpu.HBM)],
        out_specs=pl.BlockSpec(memory_space=pltpu.VMEM),
        scratch_shapes=[
            pltpu.VMEM((sections, padded, taps), jnp.bfloat16),
            pltpu.SemaphoreType.DMA((sections,)),
            pltpu.VMEM((sections * slot, LANE), jnp.float32),
            pltpu.VMEM((samples // LANE * padded, LANE), jnp.float32),
        ]
        + [pltpu.VMEM((CHUNK * LANE, 2 * LANE), jnp.bfloat16)] * 4,
        compiler_params=pltpu.CompilerParams(vmem_limit_bytes=60 * 2**20),
        cost_estimate=pl.CostEstimate(
            flops=2 * padded * taps * samples,
            bytes_accessed=2 * sections * padded * taps,
            transcendentals=0,
        ),
        name="correlate",
    )(*lines, basis_taps)
    return out[:rows]


def exchange(block, distance):
    size = lax.axis_size("tmpl")
    return lax.ppermute(block, "tmpl", [(i, i ^ distance) for i in range(size)])


def gather_blocks(block, ready):
    size = lax.axis_size("tmpl")
    if block.shape[0] % SUB:
        stride = 1
        while stride < size:
            radix = 4 if size // stride >= 4 else 2
            others = [exchange(block, step * stride) for step in range(1, radix)]
            block = jnp.concatenate([block] + others, axis=0)
            stride *= radix
        return [block], ready
    held = {0: block}
    for place in range(2, size, 2):
        high = 1 << (place.bit_length() - 1)
        if place in (high, size - 2):
            held[place] = exchange(block, place)
        else:
            held[place] = exchange(held[high], place ^ high)
    for place in range(1, size, 2):
        source = held[place ^ 1]
        if place == size - 1:
            source, held[place - 9] = lax.optimization_barrier((source, held[place - 9]))
        if place == TIED:
            source, ready = lax.optimization_barrier((source, ready))
        held[place] = exchange(source, 1)
    return [held[place] for place in range(size)], ready


def maximum_over_group(values):
    size = lax.axis_size("tmpl")
    tiles = values.reshape(1, -1, LANE)
    copies = jnp.broadcast_to(tiles, (size,) + tiles.shape[1:])
    others = lax.all_to_all(copies, "tmpl", split_axis=0, concat_axis=0, tiled=True)
    return jnp.max(others, axis=0).reshape(values.shape)


def arrange_kernel(offset_ref, coeffs_ref, out_ref):
    bases = coeffs_ref.shape[2]
    source = lax.broadcasted_iota(jnp.int32, (bases, bases), 0)
    target = lax.broadcasted_iota(jnp.int32, (bases, bases), 1) ^ offset_ref[0]
    select = jnp.where(source == target, 1.0, 0.0).astype(jnp.bfloat16)
    for section in range(coeffs_ref.shape[0]):
        out_ref[section] = jnp.dot(
            coeffs_ref[section], select, preferred_element_type=jnp.float32
        ).astype(out_ref.dtype)


def arrange(coeffs, offset):
    return pl.pallas_call(
        arrange_kernel,
        out_shape=jax.ShapeDtypeStruct(coeffs.shape, coeffs.dtype),
        in_specs=[
            pl.BlockSpec(memory_space=pltpu.SMEM),
            pl.BlockSpec(memory_space=pltpu.VMEM),
        ],
        out_specs=pl.BlockSpec(memory_space=pltpu.VMEM),
        compiler_params=pltpu.CompilerParams(vmem_limit_bytes=16 * 2**20),
        cost_estimate=pl.CostEstimate(
            flops=2 * coeffs.size * coeffs.shape[2],
            bytes_accessed=4 * coeffs.size,
            transcendentals=0,
        ),
        name="arrange",
    )(offset, coeffs)


def recon_kernel(order, coeffs_ref, *refs):
    pieces = [refs[order.index(place)] for place in range(len(order))]
    snr_ref, peak_ref = refs[-2], refs[-1]
    samples = snr_ref.shape[1]
    source = lax.broadcasted_iota(jnp.int32, (2 * LANE, 2 * LANE), 0) % LANE
    target = lax.broadcasted_iota(jnp.int32, (2 * LANE, 2 * LANE), 1) // 2
    repeat = jnp.where(source == target, 1.0, 0.0).astype(jnp.bfloat16)
    running = None
    for section in (3, 2, 1, 0):
        width = samples >> section
        offset = sum(samples >> s for s in range(section))
        summed = []
        for place in range(0, width, 2 * LANE):
            size = min(2 * LANE, width)
            first = offset + place
            basis = jnp.concatenate([ref[:, first : first + size] for ref in pieces], axis=0)
            part = jnp.dot(coeffs_ref[section], basis, preferred_element_type=jnp.float32)
            if running is not None:
                coarse = running[place // (2 * LANE)]
                high = coarse.astype(jnp.bfloat16)
                low = (coarse - high.astype(jnp.float32)).astype(jnp.bfloat16)
                part = part + jnp.dot(
                    jnp.concatenate([high, low], axis=1),
                    repeat,
                    preferred_element_type=jnp.float32,
                )
            summed.append(part)
        running = []
        for part in summed:
            running += [part[:, at : at + LANE] for at in range(0, part.shape[1], LANE)]
        if section == 0:
            for number, part in enumerate(summed):
                place = number * 2 * LANE
                snr_ref[:, place : place + 2 * LANE] = part.astype(snr_ref.dtype)
                peak_ref[:, place : place + 2 * LANE] = jnp.max(
                    jnp.abs(part), axis=0, keepdims=True
                )


def reconstruct(coeffs, blocks, samples):
    order = HANDED if len(HANDED) == len(blocks) else tuple(range(len(blocks)))
    return pl.pallas_call(
        functools.partial(recon_kernel, order),
        out_shape=(
            jax.ShapeDtypeStruct((coeffs.shape[1], samples), jnp.bfloat16),
            jax.ShapeDtypeStruct((1, samples), jnp.float32),
        ),
        in_specs=[pl.BlockSpec(memory_space=pltpu.VMEM)] * (1 + len(blocks)),
        out_specs=(pl.BlockSpec(memory_space=pltpu.VMEM),) * 2,
        compiler_params=pltpu.CompilerParams(vmem_limit_bytes=16 * 2**20),
        name="reconstruct",
    )(coeffs, *[blocks[place] for place in order])


def per_device(strain_fast, strain_half, strain_quarter, strain_eighth, basis_taps, recon_coeffs):
    streams = (strain_fast, strain_half, strain_quarter, strain_eighth)
    samples = strain_fast.shape[0] - basis_taps.shape[2]
    offset = (lax.axis_index("tmpl") * basis_taps.shape[1]).astype(jnp.int32).reshape(1)
    coeffs = arrange(recon_coeffs, offset)
    blocks, coeffs = gather_blocks(correlate(streams, basis_taps), coeffs)
    snr_series, local_peak = reconstruct(coeffs, blocks, samples)
    peak_snr = maximum_over_group(local_peak.reshape(samples))
    return (snr_series, peak_snr)


def solution(mesh):
    in_specs = (P(), P(), P(), P(), P("bank", "tmpl", None), P("bank", "tmpl", None))
    out_specs = (P(("bank", "tmpl"), None), P("bank"))
    return jax.shard_map(
        per_device, mesh=mesh, in_specs=in_specs, out_specs=out_specs, check_vma=False
    )
```

```python
import functools

import jax
import jax.numpy as jnp
from jax import lax
from jax.experimental import pallas as pl
from jax.experimental.pallas import tpu as pltpu
from jax.sharding import PartitionSpec as P

LANE = 128
CHUNK = 32
SUB = 16
ROWS = 8
ROLLS = 4
TIED = 1
HANDED = (0, 1, 2, 3, 8, 9, 4, 5, 6, 7, 12, 13, 14, 15, 10, 11)


def correlate_kernel(*refs):
    strains, source_ref, out_ref, taps_ref, sems = refs[:4], refs[4], refs[5], refs[6], refs[7]
    line_ref, total_ref, even_refs, odd_refs = refs[8], refs[9], refs[10:12], refs[12:14]
    sections = len(strains)
    copies = [
        pltpu.make_async_copy(source_ref.at[section], taps_ref.at[section], sems.at[section])
        for section in range(sections)
    ]
    for copy in copies:
        copy.start()
    rows, taps = taps_ref.shape[1], taps_ref.shape[2]
    lines = [ref.shape[0] for ref in strains]
    blocks = [count - taps // LANE for count in lines]
    slot = line_ref.shape[0] // sections
    span = CHUNK * LANE
    chunks = taps // span
    groups = ((0, 1), (2, 3))
    total_ref[...] = jnp.zeros(total_ref.shape, total_ref.dtype)

    extra = LANE // SUB - ROLLS
    source = lax.broadcasted_iota(jnp.int32, (2 * LANE, extra * LANE), 0)
    target = lax.broadcasted_iota(jnp.int32, (2 * LANE, extra * LANE), 1)
    target = target % LANE + (target // LANE + ROLLS) * SUB
    shifts = jnp.where(source == target, 1.0, 0.0).astype(jnp.bfloat16)

    for section, strain in enumerate(strains):
        first = section * slot
        line_ref[first : first + lines[section], :] = strain[...].astype(jnp.float32)
        line_ref[first + lines[section] : first + slot, :] = jnp.zeros(
            (slot - lines[section], LANE), jnp.float32
        )

    def build(frames, section, chunk, tiles=CHUNK):
        width = (tiles + 1) * LANE
        row = lax.broadcasted_iota(jnp.int32, (ROWS, width), 0)
        first = section * slot + chunk * CHUNK
        wide = jnp.concatenate(
            [
                jnp.broadcast_to(line_ref[pl.ds(first + number, 1), :], (ROWS, LANE))
                for number in range(tiles + 1)
            ],
            axis=1,
        )
        for step in (1, 2, 4):
            moved = pltpu.roll(wide, width - step, axis=1)
            wide = jnp.where((row & step) != 0, moved, wide)
        wide = jnp.concatenate([wide, pltpu.roll(wide, width - ROWS, axis=1)], axis=0)
        wide = wide.astype(jnp.bfloat16)
        moved = [wide]
        for q in range(1, ROLLS):
            moved.append(pltpu.roll(wide, width - SUB * q, axis=1))
        stacked = jnp.concatenate(
            [wide[:, number * LANE : (number + 2) * LANE] for number in range(tiles)], axis=0
        )
        rest = jnp.dot(stacked, shifts, preferred_element_type=jnp.float32).astype(wide.dtype)
        for number in range(tiles):
            pieces = [part[:, number * LANE : (number + 1) * LANE] for part in moved]
            pieces += [
                rest[number * SUB : (number + 1) * SUB, q * LANE : (q + 1) * LANE]
                for q in range(extra)
            ]
            half = section % 2
            frames[number * LANE : (number + 1) * LANE, half * LANE : (half + 1) * LANE] = (
                jnp.concatenate(pieces, axis=0)
            )

    def shifted(section, chunk, tiles):
        pieces = []
        for u in range(blocks[section]):
            first, size = (chunk * CHUNK - u) * LANE, tiles * LANE
            if not isinstance(first, int):
                pieces.append(taps_ref[section, :, pl.ds(pl.multiple_of(first, LANE), size)])
                continue
            parts = []
            if first < 0:
                parts.append(jnp.zeros((rows, -first), taps_ref.dtype))
            if first < taps:
                parts.append(taps_ref[section, :, max(first, 0) : min(first + size, taps)])
            if first + size > taps:
                parts.append(jnp.zeros((rows, first + size - max(first, taps)), taps_ref.dtype))
            pieces.append(jnp.concatenate(parts, axis=1) if len(parts) > 1 else parts[0])
        return pieces

    def accumulate(frames, group, chunk, tiles=CHUNK):
        left = []
        for section in group:
            left += shifted(section, chunk, tiles)
        left = jnp.concatenate(left, axis=0) if len(left) > 1 else left[0]
        both = jnp.dot(
            left, frames[: tiles * LANE, :], preferred_element_type=jnp.float32
        )
        height = 0
        for section in group:
            size = blocks[section] * rows
            half = section % 2
            at = sum(blocks[:section]) * rows
            total_ref[at : at + size, :] += both[
                height : height + size, half * LANE : (half + 1) * LANE
            ]
            height += size

    def build_all(frames, chunk):
        for section in range(sections):
            build(frames[section // 2], section, chunk)

    def accumulate_all(frames, chunk):
        for group, part in zip(groups, frames):
            accumulate(part, group, chunk)

    build_all(even_refs, 0)
    for copy in copies:
        copy.wait()
    accumulate_all(even_refs, 0)
    build_all(odd_refs, 1)

    def step(number, carry):
        accumulate_all(odd_refs, 2 * number - 1)
        build_all(even_refs, 2 * number)
        accumulate_all(even_refs, 2 * number)
        build_all(odd_refs, 2 * number + 1)
        return carry

    lax.fori_loop(1, chunks // 2, step, 0)
    accumulate_all(odd_refs, chunks - 1)
    for group, frames in zip(groups, even_refs):
        active = [section for section in group if blocks[section] > 1]
        if active:
            tiles = max(blocks[section] for section in active) - 1
            for section in active:
                build(frames, section, chunks, tiles)
            accumulate(frames, active, chunks, tiles)
    place = 0
    for section in range(sections):
        for u in range(blocks[section]):
            at = (sum(blocks[:section]) + u) * rows
            out_ref[:, place : place + LANE] = total_ref[at : at + rows, :].astype(out_ref.dtype)
            place += LANE


def correlate(streams, basis_taps):
    sections, rows, taps = basis_taps.shape
    padded = -(-rows // SUB) * SUB
    if padded != rows:
        basis_taps = jnp.pad(basis_taps, ((0, 0), (0, padded - rows), (0, 0)))
    samples = sum(x.shape[0] - taps for x in streams)
    longest = max(x.shape[0] for x in streams)
    slot = -(-(longest + LANE) // (8 * LANE)) * 8
    lines = [x.reshape(-1, LANE) for x in streams]
    out = pl.pallas_call(
        correlate_kernel,
        out_shape=pltpu.VMEM((padded, samples), jnp.bfloat16),
        in_specs=[pl.BlockSpec(memory_space=pltpu.VMEM)] * sections
        + [pl.BlockSpec(memory_space=pltpu.HBM)],
        out_specs=pl.BlockSpec(memory_space=pltpu.VMEM),
        scratch_shapes=[
            pltpu.VMEM((sections, padded, taps), jnp.bfloat16),
            pltpu.SemaphoreType.DMA((sections,)),
            pltpu.VMEM((sections * slot, LANE), jnp.float32),
            pltpu.VMEM((samples // LANE * padded, LANE), jnp.float32),
        ]
        + [pltpu.VMEM((CHUNK * LANE, 2 * LANE), jnp.bfloat16)] * 4,
        compiler_params=pltpu.CompilerParams(vmem_limit_bytes=60 * 2**20),
        cost_estimate=pl.CostEstimate(
            flops=2 * padded * taps * samples,
            bytes_accessed=2 * sections * padded * taps,
            transcendentals=0,
        ),
        name="correlate",
    )(*lines, basis_taps)
    return out[:rows]


def exchange(block, distance):
    size = lax.axis_size("tmpl")
    return lax.ppermute(block, "tmpl", [(i, i ^ distance) for i in range(size)])


def gather_blocks(block, ready):
    size = lax.axis_size("tmpl")
    if block.shape[0] % SUB:
        stride = 1
        while stride < size:
            radix = 4 if size // stride >= 4 else 2
            others = [exchange(block, step * stride) for step in range(1, radix)]
            block = jnp.concatenate([block] + others, axis=0)
            stride *= radix
        return [block], ready
    held = {0: block}
    for place in range(2, size, 2):
        high = 1 << (place.bit_length() - 1)
        held[place] = exchange(held[place ^ high and high], place ^ high or place)
    for place in range(1, size, 2):
        source = held[place ^ 1]
        if place == TIED:
            source, ready = lax.optimization_barrier((source, ready))
        held[place] = exchange(source, 1)
    return [held[place] for place in range(size)], ready


def maximum_over_group(values):
    size = lax.axis_size("tmpl")
    tiles = values.reshape(1, -1, LANE)
    copies = jnp.broadcast_to(tiles, (size,) + tiles.shape[1:])
    others = lax.all_to_all(copies, "tmpl", split_axis=0, concat_axis=0, tiled=True)
    return jnp.max(others, axis=0).reshape(values.shape)


def arrange_kernel(offset_ref, coeffs_ref, out_ref):
    bases = coeffs_ref.shape[2]
    source = lax.broadcasted_iota(jnp.int32, (bases, bases), 0)
    target = lax.broadcasted_iota(jnp.int32, (bases, bases), 1) ^ offset_ref[0]
    select = jnp.where(source == target, 1.0, 0.0).astype(jnp.bfloat16)
    for section in range(coeffs_ref.shape[0]):
        out_ref[section] = jnp.dot(
            coeffs_ref[section], select, preferred_element_type=jnp.float32
        ).astype(out_ref.dtype)


def arrange(coeffs, offset):
    return pl.pallas_call(
        arrange_kernel,
        out_shape=jax.ShapeDtypeStruct(coeffs.shape, coeffs.dtype),
        in_specs=[
            pl.BlockSpec(memory_space=pltpu.SMEM),
            pl.BlockSpec(memory_space=pltpu.VMEM),
        ],
        out_specs=pl.BlockSpec(memory_space=pltpu.VMEM),
        compiler_params=pltpu.CompilerParams(vmem_limit_bytes=16 * 2**20),
        cost_estimate=pl.CostEstimate(
            flops=2 * coeffs.size * coeffs.shape[2],
            bytes_accessed=4 * coeffs.size,
            transcendentals=0,
        ),
        name="arrange",
    )(offset, coeffs)


def recon_kernel(order, coeffs_ref, *refs):
    pieces = [refs[order.index(place)] for place in range(len(order))]
    snr_ref, peak_ref = refs[-2], refs[-1]
    samples = snr_ref.shape[1]
    wide = 2 * LANE

    def product(section, place, size):
        first = sum(samples >> s for s in range(section)) + place
        basis = jnp.concatenate([ref[:, first : first + size] for ref in pieces], axis=0)
        return jnp.dot(coeffs_ref[section], basis, preferred_element_type=jnp.float32)

    slow = {}
    for section in (3, 2, 1):
        for place in range(0, samples >> section, wide):
            size = min(wide, samples >> section)
            part = product(section, place, size)
            high = part.astype(jnp.bfloat16)
            low = (part - high.astype(jnp.float32)).astype(jnp.bfloat16)
            for at in range(0, size, LANE):
                slow[section, (place + at) // LANE] = [high[:, at : at + LANE], low[:, at : at + LANE]]
    source = lax.broadcasted_iota(jnp.int32, (wide, wide), 0) % LANE
    target = lax.broadcasted_iota(jnp.int32, (wide, wide), 1)

    for place in range(0, samples, wide):
        left, right = [], []
        for section in (1, 2, 3):
            column = place >> section
            left += slow[section, column // LANE]
            match = source == (target >> section) + column % LANE
            right.append(jnp.where(match, 1.0, 0.0).astype(jnp.bfloat16))
        total = product(0, place, wide) + jnp.dot(
            jnp.concatenate(left, axis=1),
            jnp.concatenate(right, axis=0),
            preferred_element_type=jnp.float32,
        )
        snr_ref[:, place : place + wide] = total.astype(snr_ref.dtype)
        peak_ref[:, place : place + wide] = jnp.max(jnp.abs(total), axis=0, keepdims=True)


def reconstruct(coeffs, blocks, samples):
    order = HANDED if len(HANDED) == len(blocks) else tuple(range(len(blocks)))
    return pl.pallas_call(
        functools.partial(recon_kernel, order),
        out_shape=(
            jax.ShapeDtypeStruct((coeffs.shape[1], samples), jnp.bfloat16),
            jax.ShapeDtypeStruct((1, samples), jnp.float32),
        ),
        in_specs=[pl.BlockSpec(memory_space=pltpu.VMEM)] * (1 + len(blocks)),
        out_specs=(pl.BlockSpec(memory_space=pltpu.VMEM),) * 2,
        compiler_params=pltpu.CompilerParams(vmem_limit_bytes=16 * 2**20),
        name="reconstruct",
    )(coeffs, *[blocks[place] for place in order])


def per_device(strain_fast, strain_half, strain_quarter, strain_eighth, basis_taps, recon_coeffs):
    streams = (strain_fast, strain_half, strain_quarter, strain_eighth)
    samples = strain_fast.shape[0] - basis_taps.shape[2]
    offset = (lax.axis_index("tmpl") * basis_taps.shape[1]).astype(jnp.int32).reshape(1)
    coeffs = arrange(recon_coeffs, offset)
    blocks, coeffs = gather_blocks(correlate(streams, basis_taps), coeffs)
    snr_series, local_peak = reconstruct(coeffs, blocks, samples)
    peak_snr = maximum_over_group(local_peak.reshape(samples))
    return (snr_series, peak_snr)


def solution(mesh):
    in_specs = (P(), P(), P(), P(), P("bank", "tmpl", None), P("bank", "tmpl", None))
    out_specs = (P(("bank", "tmpl"), None), P("bank"))
    return jax.shard_map(
        per_device, mesh=mesh, in_specs=in_specs, out_specs=out_specs, check_vma=False
    )
```

```python
import functools

import jax
import jax.numpy as jnp
from jax import lax
from jax.experimental import pallas as pl
from jax.experimental.pallas import tpu as pltpu
from jax.sharding import PartitionSpec as P

LANE = 128
CHUNK = 32
SUB = 16
ROWS = 8
ROLLS = 4
TIED = 10
HANDED = (0, 8, 1, 4, 10, 2, 3, 9, 6, 12, 7, 13, 5, 11)


def correlate_kernel(*refs):
    strains, source_ref, out_ref, taps_ref, sems = refs[:4], refs[4], refs[5], refs[6], refs[7]
    line_ref, total_ref, even_refs, odd_refs = refs[8], refs[9], refs[10:12], refs[12:14]
    sections = len(strains)
    copies = [
        pltpu.make_async_copy(source_ref.at[section], taps_ref.at[section], sems.at[section])
        for section in range(sections)
    ]
    for copy in copies:
        copy.start()
    rows, taps = taps_ref.shape[1], taps_ref.shape[2]
    lines = [ref.shape[0] for ref in strains]
    blocks = [count - taps // LANE for count in lines]
    slot = line_ref.shape[0] // sections
    span = CHUNK * LANE
    chunks = taps // span
    groups = ((0, 1), (2, 3))
    total_ref[...] = jnp.zeros(total_ref.shape, total_ref.dtype)

    extra = LANE // SUB - ROLLS
    source = lax.broadcasted_iota(jnp.int32, (2 * LANE, extra * LANE), 0)
    target = lax.broadcasted_iota(jnp.int32, (2 * LANE, extra * LANE), 1)
    target = target % LANE + (target // LANE + ROLLS) * SUB
    shifts = jnp.where(source == target, 1.0, 0.0).astype(jnp.bfloat16)

    for section, strain in enumerate(strains):
        first = section * slot
        line_ref[first : first + lines[section], :] = strain[...].astype(jnp.float32)
        line_ref[first + lines[section] : first + slot, :] = jnp.zeros(
            (slot - lines[section], LANE), jnp.float32
        )

    def build(frames, section, chunk, tiles=CHUNK):
        width = (tiles + 1) * LANE
        row = lax.broadcasted_iota(jnp.int32, (ROWS, width), 0)
        first = section * slot + chunk * CHUNK
        wide = jnp.concatenate(
            [
                jnp.broadcast_to(line_ref[pl.ds(first + number, 1), :], (ROWS, LANE))
                for number in range(tiles + 1)
            ],
            axis=1,
        )
        for step in (1, 2, 4):
            moved = pltpu.roll(wide, width - step, axis=1)
            wide = jnp.where((row & step) != 0, moved, wide)
        wide = jnp.concatenate([wide, pltpu.roll(wide, width - ROWS, axis=1)], axis=0)
        wide = wide.astype(jnp.bfloat16)
        moved = [wide]
        for q in range(1, ROLLS):
            moved.append(pltpu.roll(wide, width - SUB * q, axis=1))
        stacked = jnp.concatenate(
            [wide[:, number * LANE : (number + 2) * LANE] for number in range(tiles)], axis=0
        )
        rest = jnp.dot(stacked, shifts, preferred_element_type=jnp.float32).astype(wide.dtype)
        for number in range(tiles):
            pieces = [part[:, number * LANE : (number + 1) * LANE] for part in moved]
            pieces += [
                rest[number * SUB : (number + 1) * SUB, q * LANE : (q + 1) * LANE]
                for q in range(extra)
            ]
            half = section % 2
            frames[number * LANE : (number + 1) * LANE, half * LANE : (half + 1) * LANE] = (
                jnp.concatenate(pieces, axis=0)
            )

    def shifted(section, chunk, tiles):
        pieces = []
        for u in range(blocks[section]):
            first, size = (chunk * CHUNK - u) * LANE, tiles * LANE
            if not isinstance(first, int):
                pieces.append(taps_ref[section, :, pl.ds(pl.multiple_of(first, LANE), size)])
                continue
            parts = []
            if first < 0:
                parts.append(jnp.zeros((rows, -first), taps_ref.dtype))
            if first < taps:
                parts.append(taps_ref[section, :, max(first, 0) : min(first + size, taps)])
            if first + size > taps:
                parts.append(jnp.zeros((rows, first + size - max(first, taps)), taps_ref.dtype))
            pieces.append(jnp.concatenate(parts, axis=1) if len(parts) > 1 else parts[0])
        return pieces

    def accumulate(frames, group, chunk, tiles=CHUNK):
        left = []
        for section in group:
            left += shifted(section, chunk, tiles)
        left = jnp.concatenate(left, axis=0) if len(left) > 1 else left[0]
        both = jnp.dot(
            left, frames[: tiles * LANE, :], preferred_element_type=jnp.float32
        )
        height = 0
        for section in group:
            size = blocks[section] * rows
            half = section % 2
            at = sum(blocks[:section]) * rows
            total_ref[at : at + size, :] += both[
                height : height + size, half * LANE : (half + 1) * LANE
            ]
            height += size

    def build_all(frames, chunk):
        for section in range(sections):
            build(frames[section // 2], section, chunk)

    def accumulate_all(frames, chunk):
        for group, part in zip(groups, frames):
            accumulate(part, group, chunk)

    build_all(even_refs, 0)
    for copy in copies:
        copy.wait()
    accumulate_all(even_refs, 0)
    build_all(odd_refs, 1)

    def step(number, carry):
        accumulate_all(odd_refs, 2 * number - 1)
        build_all(even_refs, 2 * number)
        accumulate_all(even_refs, 2 * number)
        build_all(odd_refs, 2 * number + 1)
        return carry

    lax.fori_loop(1, chunks // 2, step, 0)
    accumulate_all(odd_refs, chunks - 1)
    for group, frames in zip(groups, even_refs):
        active = [section for section in group if blocks[section] > 1]
        if active:
            tiles = max(blocks[section] for section in active) - 1
            for section in active:
                build(frames, section, chunks, tiles)
            accumulate(frames, active, chunks, tiles)
    place = 0
    for section in range(sections):
        for u in range(blocks[section]):
            at = (sum(blocks[:section]) + u) * rows
            out_ref[:, place : place + LANE] = total_ref[at : at + rows, :].astype(out_ref.dtype)
            place += LANE


def correlate(streams, basis_taps):
    sections, rows, taps = basis_taps.shape
    padded = -(-rows // SUB) * SUB
    if padded != rows:
        basis_taps = jnp.pad(basis_taps, ((0, 0), (0, padded - rows), (0, 0)))
    samples = sum(x.shape[0] - taps for x in streams)
    longest = max(x.shape[0] for x in streams)
    slot = -(-(longest + LANE) // (8 * LANE)) * 8
    lines = [x.reshape(-1, LANE) for x in streams]
    out = pl.pallas_call(
        correlate_kernel,
        out_shape=pltpu.VMEM((padded, samples), jnp.bfloat16),
        in_specs=[pl.BlockSpec(memory_space=pltpu.VMEM)] * sections
        + [pl.BlockSpec(memory_space=pltpu.HBM)],
        out_specs=pl.BlockSpec(memory_space=pltpu.VMEM),
        scratch_shapes=[
            pltpu.VMEM((sections, padded, taps), jnp.bfloat16),
            pltpu.SemaphoreType.DMA((sections,)),
            pltpu.VMEM((sections * slot, LANE), jnp.float32),
            pltpu.VMEM((samples // LANE * padded, LANE), jnp.float32),
        ]
        + [pltpu.VMEM((CHUNK * LANE, 2 * LANE), jnp.bfloat16)] * 4,
        compiler_params=pltpu.CompilerParams(vmem_limit_bytes=60 * 2**20),
        cost_estimate=pl.CostEstimate(
            flops=2 * padded * taps * samples,
            bytes_accessed=2 * sections * padded * taps,
            transcendentals=0,
        ),
        name="correlate",
    )(*lines, basis_taps)
    return out[:rows]


def exchange(block, distance):
    size = lax.axis_size("tmpl")
    return lax.ppermute(block, "tmpl", [(i, i ^ distance) for i in range(size)])


def gather_blocks(block, ready, groups):
    size = lax.axis_size("tmpl")
    if block.shape[0] % SUB:
        stride = 1
        while stride < size:
            radix = 4 if size // stride >= 4 else 2
            others = [exchange(block, step * stride) for step in range(1, radix)]
            block = jnp.concatenate([block] + others, axis=0)
            stride *= radix
        return [block], ready
    held = {0: block}
    for place in range(2, size, 2):
        high = 1 << (place.bit_length() - 1)
        held[place] = exchange(held[place ^ high and high], place ^ high or place)
    blocks = []
    for places in groups:
        if places[0] & 1 == 0:
            blocks += [held[place] for place in places]
            continue
        sources = [held[place ^ 1] for place in places]
        source = sources[0] if len(sources) == 1 else jnp.concatenate(sources, axis=0)
        if places == groups[TIED]:
            source, ready = lax.optimization_barrier((source, ready))
        blocks.append(exchange(source, 1))
    return blocks, ready


def block_groups(size):
    first = [place for place in range(1, size, 2) if (place ^ 1) & ((place ^ 1) - 1) == 0][:-1]
    rest = [place for place in range(1, size, 2) if place not in first]
    alone = [(place,) for place in list(range(0, size, 2))]
    return alone + [tuple(first)] + [(place,) for place in rest]


def maximum_over_group(values):
    size = lax.axis_size("tmpl")
    tiles = values.reshape(1, -1, LANE)
    copies = jnp.broadcast_to(tiles, (size,) + tiles.shape[1:])
    others = lax.all_to_all(copies, "tmpl", split_axis=0, concat_axis=0, tiled=True)
    return jnp.max(others, axis=0).reshape(values.shape)


def arrange_kernel(order, offset_ref, coeffs_ref, out_ref):
    bases = coeffs_ref.shape[2]
    rows = bases // len(order)
    source = lax.broadcasted_iota(jnp.int32, (bases, bases), 0)
    column = lax.broadcasted_iota(jnp.int32, (1, bases), 1)
    target = column
    for group, place in enumerate(order):
        if group != place:
            inside = (column >= group * rows) & (column < (group + 1) * rows)
            target = jnp.where(inside, column + (place - group) * rows, target)
    select = jnp.where(source == (target ^ offset_ref[0]), 1.0, 0.0).astype(jnp.bfloat16)
    for section in range(coeffs_ref.shape[0]):
        out_ref[section] = jnp.dot(
            coeffs_ref[section], select, preferred_element_type=jnp.float32
        ).astype(out_ref.dtype)


def arrange(coeffs, offset, order):
    return pl.pallas_call(
        functools.partial(arrange_kernel, order),
        out_shape=jax.ShapeDtypeStruct(coeffs.shape, coeffs.dtype),
        in_specs=[
            pl.BlockSpec(memory_space=pltpu.SMEM),
            pl.BlockSpec(memory_space=pltpu.VMEM),
        ],
        out_specs=pl.BlockSpec(memory_space=pltpu.VMEM),
        compiler_params=pltpu.CompilerParams(vmem_limit_bytes=16 * 2**20),
        cost_estimate=pl.CostEstimate(
            flops=2 * coeffs.size * coeffs.shape[2],
            bytes_accessed=4 * coeffs.size,
            transcendentals=0,
        ),
        name="arrange",
    )(offset, coeffs)


def recon_kernel(order, coeffs_ref, *refs):
    pieces = [refs[order.index(place)] for place in range(len(order))]
    out_ref, peak_ref, snr_ref, sems = refs[-4:]
    samples = snr_ref.shape[1]
    wide = 2 * LANE
    copies = []

    def product(section, place, size):
        first = sum(samples >> s for s in range(section)) + place
        basis = jnp.concatenate([ref[:, first : first + size] for ref in pieces], axis=0)
        return jnp.dot(coeffs_ref[section], basis, preferred_element_type=jnp.float32)

    slow = {}
    for section in (3, 2, 1):
        for place in range(0, samples >> section, wide):
            size = min(wide, samples >> section)
            part = product(section, place, size)
            high = part.astype(jnp.bfloat16)
            low = (part - high.astype(jnp.float32)).astype(jnp.bfloat16)
            for at in range(0, size, LANE):
                slow[section, (place + at) // LANE] = [high[:, at : at + LANE], low[:, at : at + LANE]]
    source = lax.broadcasted_iota(jnp.int32, (wide, wide), 0) % LANE
    target = lax.broadcasted_iota(jnp.int32, (wide, wide), 1)

    for place in range(0, samples, wide):
        left, right = [], []
        for section in (1, 2, 3):
            column = place >> section
            left += slow[section, column // LANE]
            match = source == (target >> section) + column % LANE
            right.append(jnp.where(match, 1.0, 0.0).astype(jnp.bfloat16))
        total = product(0, place, wide) + jnp.dot(
            jnp.concatenate(left, axis=1),
            jnp.concatenate(right, axis=0),
            preferred_element_type=jnp.float32,
        )
        snr_ref[:, place : place + wide] = total.astype(snr_ref.dtype)
        copies.append(
            pltpu.make_async_copy(
                snr_ref.at[:, pl.ds(place, wide)],
                out_ref.at[:, pl.ds(place, wide)],
                sems.at[place // wide],
            )
        )
        copies[-1].start()
        peak_ref[:, place : place + wide] = jnp.max(jnp.abs(total), axis=0, keepdims=True)
    for copy in copies:
        copy.wait()


def reconstruct(coeffs, blocks, samples):
    order = HANDED if len(HANDED) == len(blocks) else tuple(range(len(blocks)))
    return pl.pallas_call(
        functools.partial(recon_kernel, order),
        out_shape=(
            jax.ShapeDtypeStruct((coeffs.shape[1], samples), jnp.bfloat16),
            jax.ShapeDtypeStruct((1, samples), jnp.float32),
        ),
        in_specs=[pl.BlockSpec(memory_space=pltpu.VMEM)] * (1 + len(blocks)),
        out_specs=(
            pl.BlockSpec(memory_space=pltpu.HBM),
            pl.BlockSpec(memory_space=pltpu.VMEM),
        ),
        scratch_shapes=[
            pltpu.VMEM((coeffs.shape[1], samples), jnp.bfloat16),
            pltpu.SemaphoreType.DMA((samples // (2 * LANE),)),
        ],
        compiler_params=pltpu.CompilerParams(vmem_limit_bytes=16 * 2**20),
        name="reconstruct",
    )(coeffs, *[blocks[place] for place in order])


def per_device(strain_fast, strain_half, strain_quarter, strain_eighth, basis_taps, recon_coeffs):
    streams = (strain_fast, strain_half, strain_quarter, strain_eighth)
    samples = strain_fast.shape[0] - basis_taps.shape[2]
    size, rows = lax.axis_size("tmpl"), basis_taps.shape[1]
    groups = block_groups(size) if rows % SUB == 0 else [tuple(range(size))]
    order = tuple(place for places in groups for place in places)
    offset = (lax.axis_index("tmpl") * rows).astype(jnp.int32).reshape(1)
    coeffs = arrange(recon_coeffs, offset, order)
    blocks, coeffs = gather_blocks(correlate(streams, basis_taps), coeffs, groups)
    snr_series, local_peak = reconstruct(coeffs, blocks, samples)
    peak_snr = maximum_over_group(local_peak.reshape(samples))
    return (snr_series, peak_snr)


def solution(mesh):
    in_specs = (P(), P(), P(), P(), P("bank", "tmpl", None), P("bank", "tmpl", None))
    out_specs = (P(("bank", "tmpl"), None), P("bank"))
    return jax.shard_map(
        per_device, mesh=mesh, in_specs=in_specs, out_specs=out_specs, check_vma=False
    )
```

```python
import functools

import jax
import jax.numpy as jnp
from jax import lax
from jax.experimental import pallas as pl
from jax.experimental.pallas import tpu as pltpu
from jax.sharding import PartitionSpec as P

LANE = 128
CHUNK = 32
SUB = 16
ROWS = 8
ROLLS = 4
TIED = 7
HANDED = (0, 1, 2, 3, 8, 9, 4, 5, 6, 7, 12, 13, 14, 15, 10, 11)


def correlate_kernel(*refs):
    strains, source_ref, out_ref, taps_ref, sems = refs[:4], refs[4], refs[5], refs[6], refs[7]
    line_ref, total_ref, even_refs, odd_refs = refs[8], refs[9], refs[10:12], refs[12:14]
    sections = len(strains)
    copies = [
        pltpu.make_async_copy(source_ref.at[section], taps_ref.at[section], sems.at[section])
        for section in range(sections)
    ]
    for copy in copies:
        copy.start()
    rows, taps = taps_ref.shape[1], taps_ref.shape[2]
    lines = [ref.shape[0] for ref in strains]
    blocks = [count - taps // LANE for count in lines]
    slot = line_ref.shape[0] // sections
    span = CHUNK * LANE
    chunks = taps // span
    groups = ((0, 1), (2, 3))
    total_ref[...] = jnp.zeros(total_ref.shape, total_ref.dtype)

    extra = LANE // SUB - ROLLS
    source = lax.broadcasted_iota(jnp.int32, (2 * LANE, extra * LANE), 0)
    target = lax.broadcasted_iota(jnp.int32, (2 * LANE, extra * LANE), 1)
    target = target % LANE + (target // LANE + ROLLS) * SUB
    shifts = jnp.where(source == target, 1.0, 0.0).astype(jnp.bfloat16)

    for section, strain in enumerate(strains):
        first = section * slot
        line_ref[first : first + lines[section], :] = strain[...].astype(jnp.float32)
        line_ref[first + lines[section] : first + slot, :] = jnp.zeros(
            (slot - lines[section], LANE), jnp.float32
        )

    def build(frames, section, chunk, tiles=CHUNK):
        width = (tiles + 1) * LANE
        row = lax.broadcasted_iota(jnp.int32, (ROWS, width), 0)
        first = section * slot + chunk * CHUNK
        wide = jnp.concatenate(
            [
                jnp.broadcast_to(line_ref[pl.ds(first + number, 1), :], (ROWS, LANE))
                for number in range(tiles + 1)
            ],
            axis=1,
        )
        for step in (1, 2, 4):
            moved = pltpu.roll(wide, width - step, axis=1)
            wide = jnp.where((row & step) != 0, moved, wide)
        wide = jnp.concatenate([wide, pltpu.roll(wide, width - ROWS, axis=1)], axis=0)
        wide = wide.astype(jnp.bfloat16)
        moved = [wide]
        for q in range(1, ROLLS):
            moved.append(pltpu.roll(wide, width - SUB * q, axis=1))
        stacked = jnp.concatenate(
            [wide[:, number * LANE : (number + 2) * LANE] for number in range(tiles)], axis=0
        )
        rest = jnp.dot(stacked, shifts, preferred_element_type=jnp.float32).astype(wide.dtype)
        for number in range(tiles):
            pieces = [part[:, number * LANE : (number + 1) * LANE] for part in moved]
            pieces += [
                rest[number * SUB : (number + 1) * SUB, q * LANE : (q + 1) * LANE]
                for q in range(extra)
            ]
            half = section % 2
            frames[number * LANE : (number + 1) * LANE, half * LANE : (half + 1) * LANE] = (
                jnp.concatenate(pieces, axis=0)
            )

    def shifted(section, chunk, tiles):
        pieces = []
        for u in range(blocks[section]):
            first, size = (chunk * CHUNK - u) * LANE, tiles * LANE
            if not isinstance(first, int):
                pieces.append(taps_ref[section, :, pl.ds(pl.multiple_of(first, LANE), size)])
                continue
            parts = []
            if first < 0:
                parts.append(jnp.zeros((rows, -first), taps_ref.dtype))
            if first < taps:
                parts.append(taps_ref[section, :, max(first, 0) : min(first + size, taps)])
            if first + size > taps:
                parts.append(jnp.zeros((rows, first + size - max(first, taps)), taps_ref.dtype))
            pieces.append(jnp.concatenate(parts, axis=1) if len(parts) > 1 else parts[0])
        return pieces

    def accumulate(frames, group, chunk, tiles=CHUNK):
        left = []
        for section in group:
            left += shifted(section, chunk, tiles)
        left = jnp.concatenate(left, axis=0) if len(left) > 1 else left[0]
        both = jnp.dot(
            left, frames[: tiles * LANE, :], preferred_element_type=jnp.float32
        )
        height = 0
        for section in group:
            size = blocks[section] * rows
            half = section % 2
            at = sum(blocks[:section]) * rows
            total_ref[at : at + size, :] += both[
                height : height + size, half * LANE : (half + 1) * LANE
            ]
            height += size

    def build_all(frames, chunk):
        for section in range(sections):
            build(frames[section // 2], section, chunk)

    def accumulate_all(frames, chunk):
        for group, part in zip(groups, frames):
            accumulate(part, group, chunk)

    build_all(even_refs, 0)
    for copy in copies:
        copy.wait()
    accumulate_all(even_refs, 0)
    build_all(odd_refs, 1)

    def step(number, carry):
        accumulate_all(odd_refs, 2 * number - 1)
        build_all(even_refs, 2 * number)
        accumulate_all(even_refs, 2 * number)
        build_all(odd_refs, 2 * number + 1)
        return carry

    lax.fori_loop(1, chunks // 2, step, 0)
    accumulate_all(odd_refs, chunks - 1)
    for group, frames in zip(groups, even_refs):
        active = [section for section in group if blocks[section] > 1]
        if active:
            tiles = max(blocks[section] for section in active) - 1
            for section in active:
                build(frames, section, chunks, tiles)
            accumulate(frames, active, chunks, tiles)
    place = 0
    for section in range(sections):
        for u in range(blocks[section]):
            at = (sum(blocks[:section]) + u) * rows
            out_ref[:, place : place + LANE] = total_ref[at : at + rows, :].astype(out_ref.dtype)
            place += LANE


def correlate(streams, basis_taps):
    sections, rows, taps = basis_taps.shape
    padded = -(-rows // SUB) * SUB
    if padded != rows:
        basis_taps = jnp.pad(basis_taps, ((0, 0), (0, padded - rows), (0, 0)))
    samples = sum(x.shape[0] - taps for x in streams)
    longest = max(x.shape[0] for x in streams)
    slot = -(-(longest + LANE) // (8 * LANE)) * 8
    lines = [x.reshape(-1, LANE) for x in streams]
    out = pl.pallas_call(
        correlate_kernel,
        out_shape=pltpu.VMEM((padded, samples), jnp.bfloat16),
        in_specs=[pl.BlockSpec(memory_space=pltpu.VMEM)] * sections
        + [pl.BlockSpec(memory_space=pltpu.HBM)],
        out_specs=pl.BlockSpec(memory_space=pltpu.VMEM),
        scratch_shapes=[
            pltpu.VMEM((sections, padded, taps), jnp.bfloat16),
            pltpu.SemaphoreType.DMA((sections,)),
            pltpu.VMEM((sections * slot, LANE), jnp.float32),
            pltpu.VMEM((samples // LANE * padded, LANE), jnp.float32),
        ]
        + [pltpu.VMEM((CHUNK * LANE, 2 * LANE), jnp.bfloat16)] * 4,
        compiler_params=pltpu.CompilerParams(vmem_limit_bytes=60 * 2**20),
        cost_estimate=pl.CostEstimate(
            flops=2 * padded * taps * samples,
            bytes_accessed=2 * sections * padded * taps,
            transcendentals=0,
        ),
        name="correlate",
    )(*lines, basis_taps)
    return out[:rows]


def exchange(block, distance):
    size = lax.axis_size("tmpl")
    return lax.ppermute(block, "tmpl", [(i, i ^ distance) for i in range(size)])


def gather_blocks(block, ready):
    size = lax.axis_size("tmpl")
    if block.shape[0] % SUB:
        stride = 1
        while stride < size:
            radix = 4 if size // stride >= 4 else 2
            others = [exchange(block, step * stride) for step in range(1, radix)]
            block = jnp.concatenate([block] + others, axis=0)
            stride *= radix
        return [block], ready
    held = {0: block}
    for place in range(2, size, 2):
        high = 1 << (place.bit_length() - 1)
        if place <= size // 2:
            held[place] = exchange(block, place)
        else:
            held[place] = exchange(held[high], place ^ high)
    for place in range(1, size, 2):
        source = held[place ^ 1]
        if place == TIED:
            source, ready = lax.optimization_barrier((source, ready))
        held[place] = exchange(source, 1)
    return [held[place] for place in range(size)], ready


def maximum_over_group(values):
    size = lax.axis_size("tmpl")
    tiles = values.reshape(1, -1, LANE)
    copies = jnp.broadcast_to(tiles, (size,) + tiles.shape[1:])
    others = lax.all_to_all(copies, "tmpl", split_axis=0, concat_axis=0, tiled=True)
    return jnp.max(others, axis=0).reshape(values.shape)


def arrange_kernel(offset_ref, coeffs_ref, out_ref):
    bases = coeffs_ref.shape[2]
    source = lax.broadcasted_iota(jnp.int32, (bases, bases), 0)
    target = lax.broadcasted_iota(jnp.int32, (bases, bases), 1) ^ offset_ref[0]
    select = jnp.where(source == target, 1.0, 0.0).astype(jnp.bfloat16)
    for section in range(coeffs_ref.shape[0]):
        out_ref[section] = jnp.dot(
            coeffs_ref[section], select, preferred_element_type=jnp.float32
        ).astype(out_ref.dtype)


def arrange(coeffs, offset):
    return pl.pallas_call(
        arrange_kernel,
        out_shape=jax.ShapeDtypeStruct(coeffs.shape, coeffs.dtype),
        in_specs=[
            pl.BlockSpec(memory_space=pltpu.SMEM),
            pl.BlockSpec(memory_space=pltpu.VMEM),
        ],
        out_specs=pl.BlockSpec(memory_space=pltpu.VMEM),
        compiler_params=pltpu.CompilerParams(vmem_limit_bytes=16 * 2**20),
        cost_estimate=pl.CostEstimate(
            flops=2 * coeffs.size * coeffs.shape[2],
            bytes_accessed=4 * coeffs.size,
            transcendentals=0,
        ),
        name="arrange",
    )(offset, coeffs)


def recon_kernel(order, coeffs_ref, *refs):
    pieces = [refs[order.index(place)] for place in range(len(order))]
    snr_ref, peak_ref = refs[-2], refs[-1]
    samples = snr_ref.shape[1]
    wide = 2 * LANE

    def product(section, place, size):
        first = sum(samples >> s for s in range(section)) + place
        basis = jnp.concatenate([ref[:, first : first + size] for ref in pieces], axis=0)
        return jnp.dot(coeffs_ref[section], basis, preferred_element_type=jnp.float32)

    slow = {}
    for section in (3, 2, 1):
        for place in range(0, samples >> section, wide):
            size = min(wide, samples >> section)
            part = product(section, place, size)
            high = part.astype(jnp.bfloat16)
            low = (part - high.astype(jnp.float32)).astype(jnp.bfloat16)
            for at in range(0, size, LANE):
                slow[section, (place + at) // LANE] = [high[:, at : at + LANE], low[:, at : at + LANE]]
    source = lax.broadcasted_iota(jnp.int32, (wide, wide), 0) % LANE
    target = lax.broadcasted_iota(jnp.int32, (wide, wide), 1)

    for place in range(0, samples, wide):
        left, right = [], []
        for section in (1, 2, 3):
            column = place >> section
            left += slow[section, column // LANE]
            match = source == (target >> section) + column % LANE
            right.append(jnp.where(match, 1.0, 0.0).astype(jnp.bfloat16))
        total = product(0, place, wide) + jnp.dot(
            jnp.concatenate(left, axis=1),
            jnp.concatenate(right, axis=0),
            preferred_element_type=jnp.float32,
        )
        snr_ref[:, place : place + wide] = total.astype(snr_ref.dtype)
        peak_ref[:, place : place + wide] = jnp.max(jnp.abs(total), axis=0, keepdims=True)


def reconstruct(coeffs, blocks, samples):
    order = HANDED if len(HANDED) == len(blocks) else tuple(range(len(blocks)))
    return pl.pallas_call(
        functools.partial(recon_kernel, order),
        out_shape=(
            jax.ShapeDtypeStruct((coeffs.shape[1], samples), jnp.bfloat16),
            jax.ShapeDtypeStruct((1, samples), jnp.float32),
        ),
        in_specs=[pl.BlockSpec(memory_space=pltpu.VMEM)] * (1 + len(blocks)),
        out_specs=(pl.BlockSpec(memory_space=pltpu.VMEM),) * 2,
        compiler_params=pltpu.CompilerParams(vmem_limit_bytes=16 * 2**20),
        name="reconstruct",
    )(coeffs, *[blocks[place] for place in order])


def per_device(strain_fast, strain_half, strain_quarter, strain_eighth, basis_taps, recon_coeffs):
    streams = (strain_fast, strain_half, strain_quarter, strain_eighth)
    samples = strain_fast.shape[0] - basis_taps.shape[2]
    offset = (lax.axis_index("tmpl") * basis_taps.shape[1]).astype(jnp.int32).reshape(1)
    coeffs = arrange(recon_coeffs, offset)
    blocks, coeffs = gather_blocks(correlate(streams, basis_taps), coeffs)
    snr_series, local_peak = reconstruct(coeffs, blocks, samples)
    peak_snr = maximum_over_group(local_peak.reshape(samples))
    return (snr_series, peak_snr)


def solution(mesh):
    in_specs = (P(), P(), P(), P(), P("bank", "tmpl", None), P("bank", "tmpl", None))
    out_specs = (P(("bank", "tmpl"), None), P("bank"))
    return jax.shard_map(
        per_device, mesh=mesh, in_specs=in_specs, out_specs=out_specs, check_vma=False
    )
```

```python
import functools

import jax
import jax.numpy as jnp
from jax import lax
from jax.experimental import pallas as pl
from jax.experimental.pallas import tpu as pltpu
from jax.sharding import PartitionSpec as P

LANE = 128
CHUNK = 32
SUB = 16
ROWS = 8
ROLLS = 4
TIED = 8
HANDED = (0, 1, 8, 4, 2, 3, 6, 7, 5, 9)


def correlate_kernel(*refs):
    strains, source_ref, out_ref, taps_ref, sems = refs[:4], refs[4], refs[5], refs[6], refs[7]
    line_ref, total_ref, even_refs, odd_refs = refs[8], refs[9], refs[10:12], refs[12:14]
    sections = len(strains)
    copies = [
        pltpu.make_async_copy(source_ref.at[section], taps_ref.at[section], sems.at[section])
        for section in range(sections)
    ]
    for copy in copies:
        copy.start()
    rows, taps = taps_ref.shape[1], taps_ref.shape[2]
    lines = [ref.shape[0] for ref in strains]
    blocks = [count - taps // LANE for count in lines]
    slot = line_ref.shape[0] // sections
    span = CHUNK * LANE
    chunks = taps // span
    groups = ((0, 1), (2, 3))
    total_ref[...] = jnp.zeros(total_ref.shape, total_ref.dtype)

    extra = LANE // SUB - ROLLS
    source = lax.broadcasted_iota(jnp.int32, (2 * LANE, extra * LANE), 0)
    target = lax.broadcasted_iota(jnp.int32, (2 * LANE, extra * LANE), 1)
    target = target % LANE + (target // LANE + ROLLS) * SUB
    shifts = jnp.where(source == target, 1.0, 0.0).astype(jnp.bfloat16)

    for section, strain in enumerate(strains):
        first = section * slot
        line_ref[first : first + lines[section], :] = strain[...].astype(jnp.float32)
        line_ref[first + lines[section] : first + slot, :] = jnp.zeros(
            (slot - lines[section], LANE), jnp.float32
        )

    def build(frames, section, chunk, tiles=CHUNK):
        width = (tiles + 1) * LANE
        row = lax.broadcasted_iota(jnp.int32, (ROWS, width), 0)
        first = section * slot + chunk * CHUNK
        wide = jnp.concatenate(
            [
                jnp.broadcast_to(line_ref[pl.ds(first + number, 1), :], (ROWS, LANE))
                for number in range(tiles + 1)
            ],
            axis=1,
        )
        for step in (1, 2, 4):
            moved = pltpu.roll(wide, width - step, axis=1)
            wide = jnp.where((row & step) != 0, moved, wide)
        wide = jnp.concatenate([wide, pltpu.roll(wide, width - ROWS, axis=1)], axis=0)
        wide = wide.astype(jnp.bfloat16)
        moved = [wide]
        for q in range(1, ROLLS):
            moved.append(pltpu.roll(wide, width - SUB * q, axis=1))
        stacked = jnp.concatenate(
            [wide[:, number * LANE : (number + 2) * LANE] for number in range(tiles)], axis=0
        )
        rest = jnp.dot(stacked, shifts, preferred_element_type=jnp.float32).astype(wide.dtype)
        for number in range(tiles):
            pieces = [part[:, number * LANE : (number + 1) * LANE] for part in moved]
            pieces += [
                rest[number * SUB : (number + 1) * SUB, q * LANE : (q + 1) * LANE]
                for q in range(extra)
            ]
            half = section % 2
            frames[number * LANE : (number + 1) * LANE, half * LANE : (half + 1) * LANE] = (
                jnp.concatenate(pieces, axis=0)
            )

    def shifted(section, chunk, tiles):
        pieces = []
        for u in range(blocks[section]):
            first, size = (chunk * CHUNK - u) * LANE, tiles * LANE
            if not isinstance(first, int):
                pieces.append(taps_ref[section, :, pl.ds(pl.multiple_of(first, LANE), size)])
                continue
            parts = []
            if first < 0:
                parts.append(jnp.zeros((rows, -first), taps_ref.dtype))
            if first < taps:
                parts.append(taps_ref[section, :, max(first, 0) : min(first + size, taps)])
            if first + size > taps:
                parts.append(jnp.zeros((rows, first + size - max(first, taps)), taps_ref.dtype))
            pieces.append(jnp.concatenate(parts, axis=1) if len(parts) > 1 else parts[0])
        return pieces

    def accumulate(frames, group, chunk, tiles=CHUNK):
        left = []
        for section in group:
            left += shifted(section, chunk, tiles)
        left = jnp.concatenate(left, axis=0) if len(left) > 1 else left[0]
        both = jnp.dot(
            left, frames[: tiles * LANE, :], preferred_element_type=jnp.float32
        )
        height = 0
        for section in group:
            size = blocks[section] * rows
            half = section % 2
            at = sum(blocks[:section]) * rows
            total_ref[at : at + size, :] += both[
                height : height + size, half * LANE : (half + 1) * LANE
            ]
            height += size

    def build_all(frames, chunk):
        for section in range(sections):
            build(frames[section // 2], section, chunk)

    def accumulate_all(frames, chunk):
        for group, part in zip(groups, frames):
            accumulate(part, group, chunk)

    build_all(even_refs, 0)
    for copy in copies:
        copy.wait()
    accumulate_all(even_refs, 0)
    build_all(odd_refs, 1)

    def step(number, carry):
        accumulate_all(odd_refs, 2 * number - 1)
        build_all(even_refs, 2 * number)
        accumulate_all(even_refs, 2 * number)
        build_all(odd_refs, 2 * number + 1)
        return carry

    lax.fori_loop(1, chunks // 2, step, 0)
    accumulate_all(odd_refs, chunks - 1)
    for group, frames in zip(groups, even_refs):
        active = [section for section in group if blocks[section] > 1]
        if active:
            tiles = max(blocks[section] for section in active) - 1
            for section in active:
                build(frames, section, chunks, tiles)
            accumulate(frames, active, chunks, tiles)
    place = 0
    for section in range(sections):
        for u in range(blocks[section]):
            at = (sum(blocks[:section]) + u) * rows
            out_ref[:, place : place + LANE] = total_ref[at : at + rows, :].astype(out_ref.dtype)
            place += LANE


def correlate(streams, basis_taps):
    sections, rows, taps = basis_taps.shape
    padded = -(-rows // SUB) * SUB
    if padded != rows:
        basis_taps = jnp.pad(basis_taps, ((0, 0), (0, padded - rows), (0, 0)))
    samples = sum(x.shape[0] - taps for x in streams)
    longest = max(x.shape[0] for x in streams)
    slot = -(-(longest + LANE) // (8 * LANE)) * 8
    lines = [x.reshape(-1, LANE) for x in streams]
    out = pl.pallas_call(
        correlate_kernel,
        out_shape=pltpu.VMEM((padded, samples), jnp.bfloat16),
        in_specs=[pl.BlockSpec(memory_space=pltpu.VMEM)] * sections
        + [pl.BlockSpec(memory_space=pltpu.HBM)],
        out_specs=pl.BlockSpec(memory_space=pltpu.VMEM),
        scratch_shapes=[
            pltpu.VMEM((sections, padded, taps), jnp.bfloat16),
            pltpu.SemaphoreType.DMA((sections,)),
            pltpu.VMEM((sections * slot, LANE), jnp.float32),
            pltpu.VMEM((samples // LANE * padded, LANE), jnp.float32),
        ]
        + [pltpu.VMEM((CHUNK * LANE, 2 * LANE), jnp.bfloat16)] * 4,
        compiler_params=pltpu.CompilerParams(vmem_limit_bytes=60 * 2**20),
        cost_estimate=pl.CostEstimate(
            flops=2 * padded * taps * samples,
            bytes_accessed=2 * sections * padded * taps,
            transcendentals=0,
        ),
        name="correlate",
    )(*lines, basis_taps)
    return out[:rows]


def exchange(block, distance):
    size = lax.axis_size("tmpl")
    return lax.ppermute(block, "tmpl", [(i, i ^ distance) for i in range(size)])


def gather_blocks(block, ready, groups):
    size = lax.axis_size("tmpl")
    if block.shape[0] % SUB:
        stride = 1
        while stride < size:
            radix = 4 if size // stride >= 4 else 2
            others = [exchange(block, step * stride) for step in range(1, radix)]
            block = jnp.concatenate([block] + others, axis=0)
            stride *= radix
        return [block], ready
    held = {0: block}
    for place in range(2, size, 2):
        high = 1 << (place.bit_length() - 1)
        if place <= size // 2:
            held[place] = exchange(block, place)
        else:
            held[place] = exchange(held[high], place ^ high)
    blocks = []
    for places in groups:
        if places[0] & 1 == 0:
            blocks += [held[place] for place in places]
            continue
        sources = [held[place ^ 1] for place in places]
        source = sources[0] if len(sources) == 1 else jnp.concatenate(sources, axis=0)
        if places == groups[TIED]:
            source, ready = lax.optimization_barrier((source, ready))
        blocks.append(exchange(source, 1))
    return blocks, ready


def block_groups(size):
    middle = size // 2 + 1
    alone = [(place,) for place in range(0, size, 2)]
    return alone + [
        tuple(range(1, middle + 1, 2)),
        tuple(range(middle + 2, size, 2)),
    ]


def maximum_over_group(values):
    size = lax.axis_size("tmpl")
    tiles = values.reshape(1, -1, LANE)
    copies = jnp.broadcast_to(tiles, (size,) + tiles.shape[1:])
    others = lax.all_to_all(copies, "tmpl", split_axis=0, concat_axis=0, tiled=True)
    return jnp.max(others, axis=0).reshape(values.shape)


def arrange_kernel(order, offset_ref, coeffs_ref, out_ref):
    bases = coeffs_ref.shape[2]
    rows = bases // len(order)
    source = lax.broadcasted_iota(jnp.int32, (bases, bases), 0)
    column = lax.broadcasted_iota(jnp.int32, (1, bases), 1)
    target = column
    for group, place in enumerate(order):
        if group != place:
            inside = (column >= group * rows) & (column < (group + 1) * rows)
            target = jnp.where(inside, column + (place - group) * rows, target)
    select = jnp.where(source == (target ^ offset_ref[0]), 1.0, 0.0).astype(jnp.bfloat16)
    for section in range(coeffs_ref.shape[0]):
        out_ref[section] = jnp.dot(
            coeffs_ref[section], select, preferred_element_type=jnp.float32
        ).astype(out_ref.dtype)


def arrange(coeffs, offset, order):
    return pl.pallas_call(
        functools.partial(arrange_kernel, order),
        out_shape=jax.ShapeDtypeStruct(coeffs.shape, coeffs.dtype),
        in_specs=[
            pl.BlockSpec(memory_space=pltpu.SMEM),
            pl.BlockSpec(memory_space=pltpu.VMEM),
        ],
        out_specs=pl.BlockSpec(memory_space=pltpu.VMEM),
        compiler_params=pltpu.CompilerParams(vmem_limit_bytes=16 * 2**20),
        cost_estimate=pl.CostEstimate(
            flops=2 * coeffs.size * coeffs.shape[2],
            bytes_accessed=4 * coeffs.size,
            transcendentals=0,
        ),
        name="arrange",
    )(offset, coeffs)


def recon_kernel(order, coeffs_ref, *refs):
    pieces = [refs[order.index(place)] for place in range(len(order))]
    out_ref, peak_ref, snr_ref, sems = refs[-4:]
    samples = snr_ref.shape[1]
    wide = 2 * LANE
    copies = []

    def product(section, place, size):
        first = sum(samples >> s for s in range(section)) + place
        basis = jnp.concatenate([ref[:, first : first + size] for ref in pieces], axis=0)
        return jnp.dot(coeffs_ref[section], basis, preferred_element_type=jnp.float32)

    slow = {}
    for section in (3, 2, 1):
        for place in range(0, samples >> section, wide):
            size = min(wide, samples >> section)
            part = product(section, place, size)
            high = part.astype(jnp.bfloat16)
            low = (part - high.astype(jnp.float32)).astype(jnp.bfloat16)
            for at in range(0, size, LANE):
                slow[section, (place + at) // LANE] = [high[:, at : at + LANE], low[:, at : at + LANE]]
    source = lax.broadcasted_iota(jnp.int32, (wide, wide), 0) % LANE
    target = lax.broadcasted_iota(jnp.int32, (wide, wide), 1)

    for place in range(0, samples, wide):
        left, right = [], []
        for section in (1, 2, 3):
            column = place >> section
            left += slow[section, column // LANE]
            match = source == (target >> section) + column % LANE
            right.append(jnp.where(match, 1.0, 0.0).astype(jnp.bfloat16))
        total = product(0, place, wide) + jnp.dot(
            jnp.concatenate(left, axis=1),
            jnp.concatenate(right, axis=0),
            preferred_element_type=jnp.float32,
        )
        snr_ref[:, place : place + wide] = total.astype(snr_ref.dtype)
        copies.append(
            pltpu.make_async_copy(
                snr_ref.at[:, pl.ds(place, wide)],
                out_ref.at[:, pl.ds(place, wide)],
                sems.at[place // wide],
            )
        )
        copies[-1].start()
        peak_ref[:, place : place + wide] = jnp.max(jnp.abs(total), axis=0, keepdims=True)
    for copy in copies:
        copy.wait()


def reconstruct(coeffs, blocks, samples):
    order = HANDED if len(HANDED) == len(blocks) else tuple(range(len(blocks)))
    return pl.pallas_call(
        functools.partial(recon_kernel, order),
        out_shape=(
            jax.ShapeDtypeStruct((coeffs.shape[1], samples), jnp.bfloat16),
            jax.ShapeDtypeStruct((1, samples), jnp.float32),
        ),
        in_specs=[pl.BlockSpec(memory_space=pltpu.VMEM)] * (1 + len(blocks)),
        out_specs=(
            pl.BlockSpec(memory_space=pltpu.HBM),
            pl.BlockSpec(memory_space=pltpu.VMEM),
        ),
        scratch_shapes=[
            pltpu.VMEM((coeffs.shape[1], samples), jnp.bfloat16),
            pltpu.SemaphoreType.DMA((samples // (2 * LANE),)),
        ],
        compiler_params=pltpu.CompilerParams(vmem_limit_bytes=16 * 2**20),
        name="reconstruct",
    )(coeffs, *[blocks[place] for place in order])


def per_device(strain_fast, strain_half, strain_quarter, strain_eighth, basis_taps, recon_coeffs):
    streams = (strain_fast, strain_half, strain_quarter, strain_eighth)
    samples = strain_fast.shape[0] - basis_taps.shape[2]
    size, rows = lax.axis_size("tmpl"), basis_taps.shape[1]
    groups = block_groups(size) if rows % SUB == 0 else [tuple(range(size))]
    order = tuple(place for places in groups for place in places)
    offset = (lax.axis_index("tmpl") * rows).astype(jnp.int32).reshape(1)
    coeffs = arrange(recon_coeffs, offset, order)
    blocks, coeffs = gather_blocks(correlate(streams, basis_taps), coeffs, groups)
    snr_series, local_peak = reconstruct(coeffs, blocks, samples)
    peak_snr = maximum_over_group(local_peak.reshape(samples))
    return (snr_series, peak_snr)


def solution(mesh):
    in_specs = (P(), P(), P(), P(), P("bank", "tmpl", None), P("bank", "tmpl", None))
    out_specs = (P(("bank", "tmpl"), None), P("bank"))
    return jax.shard_map(
        per_device, mesh=mesh, in_specs=in_specs, out_specs=out_specs, check_vma=False
    )
```

```python
import functools

import jax
import jax.numpy as jnp
from jax import lax
from jax.experimental import pallas as pl
from jax.experimental.pallas import tpu as pltpu
from jax.sharding import PartitionSpec as P

LANE = 128
CHUNK = 32
SUB = 16
ROWS = 8
ROLLS = 4
TIED = 3
HANDED = (0, 1, 6, 7, 2, 3, 4, 5, 8, 9, 12, 13, 14, 15, 10, 11)


def correlate_kernel(*refs):
    strains, source_ref, out_ref, taps_ref, sems = refs[:4], refs[4], refs[5], refs[6], refs[7]
    line_ref, total_ref, even_refs, odd_refs = refs[8], refs[9], refs[10:12], refs[12:14]
    sections = len(strains)
    copies = [
        pltpu.make_async_copy(source_ref.at[section], taps_ref.at[section], sems.at[section])
        for section in range(sections)
    ]
    for copy in copies:
        copy.start()
    rows, taps = taps_ref.shape[1], taps_ref.shape[2]
    lines = [ref.shape[0] for ref in strains]
    blocks = [count - taps // LANE for count in lines]
    slot = line_ref.shape[0] // sections
    span = CHUNK * LANE
    chunks = taps // span
    groups = ((0, 1), (2, 3))
    total_ref[...] = jnp.zeros(total_ref.shape, total_ref.dtype)

    extra = LANE // SUB - ROLLS
    source = lax.broadcasted_iota(jnp.int32, (2 * LANE, extra * LANE), 0)
    target = lax.broadcasted_iota(jnp.int32, (2 * LANE, extra * LANE), 1)
    target = target % LANE + (target // LANE + ROLLS) * SUB
    shifts = jnp.where(source == target, 1.0, 0.0).astype(jnp.bfloat16)

    for section, strain in enumerate(strains):
        first = section * slot
        line_ref[first : first + lines[section], :] = strain[...].astype(jnp.float32)
        line_ref[first + lines[section] : first + slot, :] = jnp.zeros(
            (slot - lines[section], LANE), jnp.float32
        )

    def build(frames, section, chunk, tiles=CHUNK):
        width = (tiles + 1) * LANE
        row = lax.broadcasted_iota(jnp.int32, (ROWS, width), 0)
        first = section * slot + chunk * CHUNK
        wide = jnp.concatenate(
            [
                jnp.broadcast_to(line_ref[pl.ds(first + number, 1), :], (ROWS, LANE))
                for number in range(tiles + 1)
            ],
            axis=1,
        )
        for step in (1, 2, 4):
            moved = pltpu.roll(wide, width - step, axis=1)
            wide = jnp.where((row & step) != 0, moved, wide)
        wide = jnp.concatenate([wide, pltpu.roll(wide, width - ROWS, axis=1)], axis=0)
        wide = wide.astype(jnp.bfloat16)
        moved = [wide]
        for q in range(1, ROLLS):
            moved.append(pltpu.roll(wide, width - SUB * q, axis=1))
        stacked = jnp.concatenate(
            [wide[:, number * LANE : (number + 2) * LANE] for number in range(tiles)], axis=0
        )
        rest = jnp.dot(stacked, shifts, preferred_element_type=jnp.float32).astype(wide.dtype)
        for number in range(tiles):
            pieces = [part[:, number * LANE : (number + 1) * LANE] for part in moved]
            pieces += [
                rest[number * SUB : (number + 1) * SUB, q * LANE : (q + 1) * LANE]
                for q in range(extra)
            ]
            half = section % 2
            frames[number * LANE : (number + 1) * LANE, half * LANE : (half + 1) * LANE] = (
                jnp.concatenate(pieces, axis=0)
            )

    def shifted(section, chunk, tiles):
        pieces = []
        for u in range(blocks[section]):
            first, size = (chunk * CHUNK - u) * LANE, tiles * LANE
            if not isinstance(first, int):
                pieces.append(taps_ref[section, :, pl.ds(pl.multiple_of(first, LANE), size)])
                continue
            parts = []
            if first < 0:
                parts.append(jnp.zeros((rows, -first), taps_ref.dtype))
            if first < taps:
                parts.append(taps_ref[section, :, max(first, 0) : min(first + size, taps)])
            if first + size > taps:
                parts.append(jnp.zeros((rows, first + size - max(first, taps)), taps_ref.dtype))
            pieces.append(jnp.concatenate(parts, axis=1) if len(parts) > 1 else parts[0])
        return pieces

    def accumulate(frames, group, chunk, tiles=CHUNK):
        left = []
        for section in group:
            left += shifted(section, chunk, tiles)
        left = jnp.concatenate(left, axis=0) if len(left) > 1 else left[0]
        both = jnp.dot(
            left, frames[: tiles * LANE, :], preferred_element_type=jnp.float32
        )
        height = 0
        for section in group:
            size = blocks[section] * rows
            half = section % 2
            at = sum(blocks[:section]) * rows
            total_ref[at : at + size, :] += both[
                height : height + size, half * LANE : (half + 1) * LANE
            ]
            height += size

    def build_all(frames, chunk):
        for section in range(sections):
            build(frames[section // 2], section, chunk)

    def accumulate_all(frames, chunk):
        for group, part in zip(groups, frames):
            accumulate(part, group, chunk)

    build_all(even_refs, 0)
    for copy in copies:
        copy.wait()
    accumulate_all(even_refs, 0)
    build_all(odd_refs, 1)

    def step(number, carry):
        accumulate_all(odd_refs, 2 * number - 1)
        build_all(even_refs, 2 * number)
        accumulate_all(even_refs, 2 * number)
        build_all(odd_refs, 2 * number + 1)
        return carry

    lax.fori_loop(1, chunks // 2, step, 0)
    accumulate_all(odd_refs, chunks - 1)
    for group, frames in zip(groups, even_refs):
        active = [section for section in group if blocks[section] > 1]
        if active:
            tiles = max(blocks[section] for section in active) - 1
            for section in active:
                build(frames, section, chunks, tiles)
            accumulate(frames, active, chunks, tiles)
    place = 0
    for section in range(sections):
        for u in range(blocks[section]):
            at = (sum(blocks[:section]) + u) * rows
            out_ref[:, place : place + LANE] = total_ref[at : at + rows, :].astype(out_ref.dtype)
            place += LANE


def correlate(streams, basis_taps):
    sections, rows, taps = basis_taps.shape
    padded = -(-rows // SUB) * SUB
    if padded != rows:
        basis_taps = jnp.pad(basis_taps, ((0, 0), (0, padded - rows), (0, 0)))
    samples = sum(x.shape[0] - taps for x in streams)
    longest = max(x.shape[0] for x in streams)
    slot = -(-(longest + LANE) // (8 * LANE)) * 8
    lines = [x.reshape(-1, LANE) for x in streams]
    out = pl.pallas_call(
        correlate_kernel,
        out_shape=pltpu.VMEM((padded, samples), jnp.bfloat16),
        in_specs=[pl.BlockSpec(memory_space=pltpu.VMEM)] * sections
        + [pl.BlockSpec(memory_space=pltpu.HBM)],
        out_specs=pl.BlockSpec(memory_space=pltpu.VMEM),
        scratch_shapes=[
            pltpu.VMEM((sections, padded, taps), jnp.bfloat16),
            pltpu.SemaphoreType.DMA((sections,)),
            pltpu.VMEM((sections * slot, LANE), jnp.float32),
            pltpu.VMEM((samples // LANE * padded, LANE), jnp.float32),
        ]
        + [pltpu.VMEM((CHUNK * LANE, 2 * LANE), jnp.bfloat16)] * 4,
        compiler_params=pltpu.CompilerParams(vmem_limit_bytes=60 * 2**20),
        cost_estimate=pl.CostEstimate(
            flops=2 * padded * taps * samples,
            bytes_accessed=2 * sections * padded * taps,
            transcendentals=0,
        ),
        name="correlate",
    )(*lines, basis_taps)
    return out[:rows]


def exchange(block, distance):
    size = lax.axis_size("tmpl")
    return lax.ppermute(block, "tmpl", [(i, i ^ distance) for i in range(size)])


def gather_blocks(block, ready):
    size = lax.axis_size("tmpl")
    if block.shape[0] % SUB:
        stride = 1
        while stride < size:
            radix = 4 if size // stride >= 4 else 2
            others = [exchange(block, step * stride) for step in range(1, radix)]
            block = jnp.concatenate([block] + others, axis=0)
            stride *= radix
        return [block], ready
    held = {0: block}
    for place in range(2, size, 2):
        high = 1 << (place.bit_length() - 1)
        if place <= size // 2:
            held[place] = exchange(block, place)
        else:
            held[place] = exchange(held[high], place ^ high)
    for place in range(1, size, 2):
        source = held[place ^ 1]
        if place == TIED:
            source, ready = lax.optimization_barrier((source, ready))
        held[place] = exchange(source, 1)
    return [held[place] for place in range(size)], ready


def maximum_over_group(values):
    size = lax.axis_size("tmpl")
    tiles = values.reshape(1, -1, LANE)
    copies = jnp.broadcast_to(tiles, (size,) + tiles.shape[1:])
    others = lax.all_to_all(copies, "tmpl", split_axis=0, concat_axis=0, tiled=True)
    return jnp.max(others, axis=0).reshape(values.shape)


def arrange_kernel(offset_ref, coeffs_ref, out_ref):
    bases = coeffs_ref.shape[2]
    source = lax.broadcasted_iota(jnp.int32, (bases, bases), 0)
    target = lax.broadcasted_iota(jnp.int32, (bases, bases), 1) ^ offset_ref[0]
    select = jnp.where(source == target, 1.0, 0.0).astype(jnp.bfloat16)
    for section in range(coeffs_ref.shape[0]):
        out_ref[section] = jnp.dot(
            coeffs_ref[section], select, preferred_element_type=jnp.float32
        ).astype(out_ref.dtype)


def arrange(coeffs, offset):
    return pl.pallas_call(
        arrange_kernel,
        out_shape=jax.ShapeDtypeStruct(coeffs.shape, coeffs.dtype),
        in_specs=[
            pl.BlockSpec(memory_space=pltpu.SMEM),
            pl.BlockSpec(memory_space=pltpu.VMEM),
        ],
        out_specs=pl.BlockSpec(memory_space=pltpu.VMEM),
        compiler_params=pltpu.CompilerParams(vmem_limit_bytes=16 * 2**20),
        cost_estimate=pl.CostEstimate(
            flops=2 * coeffs.size * coeffs.shape[2],
            bytes_accessed=4 * coeffs.size,
            transcendentals=0,
        ),
        name="arrange",
    )(offset, coeffs)


def recon_kernel(order, coeffs_ref, *refs):
    pieces = [refs[order.index(place)] for place in range(len(order))]
    snr_ref, peak_ref = refs[-2], refs[-1]
    samples = snr_ref.shape[1]
    wide = 2 * LANE

    def product(section, place, size):
        first = sum(samples >> s for s in range(section)) + place
        basis = jnp.concatenate([ref[:, first : first + size] for ref in pieces], axis=0)
        return jnp.dot(coeffs_ref[section], basis, preferred_element_type=jnp.float32)

    slow = {}
    for section in (3, 2, 1):
        for place in range(0, samples >> section, wide):
            size = min(wide, samples >> section)
            part = product(section, place, size)
            high = part.astype(jnp.bfloat16)
            low = (part - high.astype(jnp.float32)).astype(jnp.bfloat16)
            for at in range(0, size, LANE):
                slow[section, (place + at) // LANE] = [high[:, at : at + LANE], low[:, at : at + LANE]]
    source = lax.broadcasted_iota(jnp.int32, (wide, wide), 0) % LANE
    target = lax.broadcasted_iota(jnp.int32, (wide, wide), 1)

    for place in range(0, samples, wide):
        left, right = [], []
        for section in (1, 2, 3):
            column = place >> section
            left += slow[section, column // LANE]
            match = source == (target >> section) + column % LANE
            right.append(jnp.where(match, 1.0, 0.0).astype(jnp.bfloat16))
        total = product(0, place, wide) + jnp.dot(
            jnp.concatenate(left, axis=1),
            jnp.concatenate(right, axis=0),
            preferred_element_type=jnp.float32,
        )
        snr_ref[:, place : place + wide] = total.astype(snr_ref.dtype)
        peak_ref[:, place : place + wide] = jnp.max(jnp.abs(total), axis=0, keepdims=True)


def reconstruct(coeffs, blocks, samples):
    order = HANDED if len(HANDED) == len(blocks) else tuple(range(len(blocks)))
    return pl.pallas_call(
        functools.partial(recon_kernel, order),
        out_shape=(
            jax.ShapeDtypeStruct((coeffs.shape[1], samples), jnp.bfloat16),
            jax.ShapeDtypeStruct((1, samples), jnp.float32),
        ),
        in_specs=[pl.BlockSpec(memory_space=pltpu.VMEM)] * (1 + len(blocks)),
        out_specs=(pl.BlockSpec(memory_space=pltpu.VMEM),) * 2,
        compiler_params=pltpu.CompilerParams(vmem_limit_bytes=16 * 2**20),
        name="reconstruct",
    )(coeffs, *[blocks[place] for place in order])


def per_device(strain_fast, strain_half, strain_quarter, strain_eighth, basis_taps, recon_coeffs):
    streams = (strain_fast, strain_half, strain_quarter, strain_eighth)
    samples = strain_fast.shape[0] - basis_taps.shape[2]
    offset = (lax.axis_index("tmpl") * basis_taps.shape[1]).astype(jnp.int32).reshape(1)
    coeffs = arrange(recon_coeffs, offset)
    blocks, coeffs = gather_blocks(correlate(streams, basis_taps), coeffs)
    snr_series, local_peak = reconstruct(coeffs, blocks, samples)
    peak_snr = maximum_over_group(local_peak.reshape(samples))
    return (snr_series, peak_snr)


def solution(mesh):
    in_specs = (P(), P(), P(), P(), P("bank", "tmpl", None), P("bank", "tmpl", None))
    out_specs = (P(("bank", "tmpl"), None), P("bank"))
    return jax.shard_map(
        per_device, mesh=mesh, in_specs=in_specs, out_specs=out_specs, check_vma=False
    )
```
